32 devices in a mesh: dp: 8 (over z, y), mp: 4 (over x, core).
Axes of the slice: x: 2, y: 2, z: 4, core: 2. Of those that a mesh axis runs over, the one named last changes fastest.
Arguments:
- tokens: bfloat16 [16384, 1152], P('dp'), may hold values from -6 to 6
- seg_ids: int32 [16384], P('dp'), may hold values from 0 to 15, as said below
- time_steps: int32 [16, 16], P('dp'), may hold values from 0 to 999
- cotangent: bfloat16 [16384, 1152], P('dp'), may hold values from -6 to 6
- weight_cols: float32 [15, 1152, 1152], P(None, 'dp', 'mp')
- weight_rows: float32 [5, 1152, 1152], P(None, 'mp', 'dp')
- bias_cols: float32 [12, 1152], P(None, 'mp'), may hold values from -3 to 3
- bias_rows: float32 [2, 1152], replicated, may hold values from -3 to 3
- first_cols: float32 [15, 1152, 1152], P(None, 'dp', 'mp'), may hold values from -80 to 80
- first_rows: float32 [5, 1152, 1152], P(None, 'mp', 'dp'), may hold values from -80 to 80
- first_bias_cols: float32 [12, 1152], P(None, 'mp'), may hold values from -80 to 80
- first_bias_rows: float32 [2, 1152], replicated, may hold values from -80 to 80
- second_cols: float32 [15, 1152, 1152], P(None, 'dp', 'mp'), may hold values from 16.384 to 65.536
- second_rows: float32 [5, 1152, 1152], P(None, 'mp', 'dp'), may hold values from 16.384 to 65.536
- second_bias_cols: float32 [12, 1152], P(None, 'mp'), may hold values from 16.384 to 65.536
- second_bias_rows: float32 [2, 1152], replicated, may hold values from 16.384 to 65.536
- ema_cols: float32 [15, 1152, 1152], P(None, 'dp', 'mp'), may hold values from -0.1875 to 0.1875
- ema_rows: float32 [5, 1152, 1152], P(None, 'mp', 'dp'), may hold values from -0.1875 to 0.1875
- ema_bias_cols: float32 [12, 1152], P(None, 'mp'), may hold values from -3 to 3
- ema_bias_rows: float32 [2, 1152], replicated, may hold values from -3 to 3
Outputs:
- out_tokens: bfloat16 [16384, 1152], P('dp')
- input_grad: float32 [16384, 1152], P('dp')
- first_cols_new: float32 [15, 1152, 1152], P(None, 'dp', 'mp')
- second_cols_new: float32 [15, 1152, 1152], P(None, 'dp', 'mp')
- weight_cols_new: float32 [15, 1152, 1152], P(None, 'dp', 'mp')
- ema_cols_new: float32 [15, 1152, 1152], P(None, 'dp', 'mp')
- first_rows_new: float32 [5, 1152, 1152], P(None, 'mp', 'dp')
- second_rows_new: float32 [5, 1152, 1152], P(None, 'mp', 'dp')
- weight_rows_new: float32 [5, 1152, 1152], P(None, 'mp', 'dp')
- ema_rows_new: float32 [5, 1152, 1152], P(None, 'mp', 'dp')
- first_bias_cols_new: float32 [12, 1152], P(None, 'mp')
- second_bias_cols_new: float32 [12, 1152], P(None, 'mp')
- bias_cols_new: float32 [12, 1152], P(None, 'mp')
- ema_bias_cols_new: float32 [12, 1152], P(None, 'mp')
- first_bias_rows_new: float32 [2, 1152], replicated
- second_bias_rows_new: float32 [2, 1152], replicated
- bias_rows_new: float32 [2, 1152], replicated
- ema_bias_rows_new: float32 [2, 1152], replicated
The draws below stay inside these ranges and needn't reach their ends.
Inputs may be any that keep to these rules, and one draw needn't show every extreme that they name: `seg_ids`: within each packed row of 1024 tokens the image number starts at 0 and rises by one from image to image; an image holds a multiple of 64 tokens, 64 to 256; in every draw one row holds 16 images of 64 tokens and every other row an image of 256 tokens. `time_steps`: entry j of a row is the timestep of that row's image j; entries past the row's last image are not read.
All inputs are finite; a program needn't handle non-finite values.
Results may differ from the reference program's by a relative error of at most 0.039.
Values may be sent and summed in bfloat16 or wider, within the bound.
No kernel may reach another device: no remote copies, remote signals or barrier semaphores. Data moves between devices by JAX's collectives and lax.ppermute only.
A program may use at most 320 MiB of HBM per device.

```python
import math
import jax
import jax.numpy as jnp
from jax import lax

D = 1152
HEADS = 16
HEAD_DIM = 72
UNIT = 64
UNITS = 16
STEP = 10
ROW_LEN = 1024
QB = 512
ROWS = 16
TOKENS = 16384
N_MP = 4


def draw_seg_ids(key, part):
    key = jax.random.fold_in(key, 11)
    rows_all = TOKENS // ROW_LEN
    key_units, key_slot, key_small = jax.random.split(key, 3)
    image_units = jax.random.randint(key_units, (rows_all, UNITS), 1, 5)
    forced_slot = jax.random.randint(key_slot, (rows_all, 1), 0, 4)
    image_units = jnp.where(jnp.arange(UNITS)[None, :] == forced_slot, 4, image_units)
    small_row = jax.random.randint(key_small, (), 0, rows_all)
    image_units = jnp.where(jnp.arange(rows_all)[:, None] == small_row, 1, image_units)
    unit_ends = jnp.cumsum(image_units, axis=1)
    unit_seg = jnp.sum((unit_ends[:, None, :] <= jnp.arange(UNITS)[None, :, None]).astype(jnp.int32), axis=2)
    return jnp.repeat(unit_seg, UNIT, axis=1).reshape(TOKENS).astype(jnp.int32)


def draw_weight_cols(key, part):
    key = jax.random.fold_in(key, 21)
    normal_values = jax.random.normal(key, (15, D, D), jnp.float32)
    slab_scale = jnp.where(jnp.arange(15) >= 9, 2.0, 1.0) * D ** (-0.5)
    return (normal_values * slab_scale[:, None, None]).astype(jnp.float32)


def draw_weight_rows(key, part):
    key = jax.random.fold_in(key, 22)
    normal_values = jax.random.normal(key, (5, D, D), jnp.float32)
    slab_scale = jnp.where(jnp.arange(5) == 0, 2.0, 0.75) * D ** (-0.5)
    return (normal_values * slab_scale[:, None, None]).astype(jnp.float32)


def place_ends(values, own_key, low, high):
    extent = values.shape
    place = [jax.random.randint(jax.random.fold_in(own_key, axis), (), 0, extent[axis]) for axis in range(len(extent))]
    values = values.at[tuple(place)].set(low)
    longest = extent.index(max(extent))
    place[longest] = (place[longest] + 1) % extent[longest]
    return values.at[tuple(place)].set(high)


def levels(key, shape, pieces, least, largest):
    loudness = 1.0
    for axis_at, parts in pieces:
        heights = jax.random.uniform(jax.random.fold_in(jax.random.fold_in(key, 6), axis_at), (parts,), jnp.float32, least / len(pieces), largest / len(pieces))
        loudness = loudness * jnp.repeat(jnp.exp(heights), shape[axis_at] // parts).reshape((-1,) + (1,) * (len(shape) - 1 - axis_at))
    return loudness


def centred(rng, shape, scale, most, cuts=(), kind=jnp.bfloat16):
    values = jax.random.normal(rng, shape, jnp.float32) * scale
    if len(cuts) > 0:
        values = levels(rng, shape, cuts, -0.22, 0.18) * values
    return jnp.clip(values, min=-most, max=most).astype(kind)


def setup_inputs(seed: int = 0) -> dict:
    key_of = jax.random.split(jax.random.key(seed), 21)
    tokens = centred(key_of[0], (TOKENS, D), 1.0, 6.0, ((0, 8),))
    seg_ids = draw_seg_ids(jax.random.fold_in(key_of[20], 71), 0)
    time_steps = place_ends(jax.random.randint(key_of[2], (ROWS, UNITS), 0, 1000), jax.random.fold_in(key_of[2], 1), 0, 999).astype(jnp.int32)
    cotangent = centred(key_of[3], (TOKENS, D), 1.0, 6.0, ((0, 8),))
    weight_cols = draw_weight_cols(jax.random.fold_in(key_of[20], 71), 0)
    weight_rows = draw_weight_rows(jax.random.fold_in(key_of[20], 71), 0)
    bias_cols = centred(key_of[6], (12, D), 0.5, 3.0, ((1, 4),), jnp.float32)
    bias_rows = centred(key_of[7], (2, D), 0.5, 3.0, (), jnp.float32)
    first_cols = centred(key_of[8], (15, D, D), (0.11 * TOKENS ** 0.5), 80.0, ((1, 8), (2, 4)), jnp.float32)
    first_rows = centred(key_of[9], (5, D, D), (0.11 * TOKENS ** 0.5), 80.0, ((1, 4), (2, 8)), jnp.float32)
    first_bias_cols = centred(key_of[10], (12, D), (0.11 * TOKENS ** 0.5), 80.0, ((1, 4),), jnp.float32)
    first_bias_rows = centred(key_of[11], (2, D), (0.11 * TOKENS ** 0.5), 80.0, (), jnp.float32)
    second_cols = jnp.clip(jnp.exp(math.log(65.536) - 1.3862944 * jax.random.uniform(key_of[12], (15, D, D), jnp.float32) ** levels(key_of[12], (15, D, D), ((1, 8), (2, 4)), -0.2, 0.2)), 16.384, 65.536)
    second_rows = jnp.clip(jnp.exp(math.log(65.536) - 1.3862944 * jax.random.uniform(key_of[13], (5, D, D), jnp.float32) ** levels(key_of[13], (5, D, D), ((1, 4), (2, 8)), -0.2, 0.2)), 16.384, 65.536)
    second_bias_cols = jnp.clip(jnp.exp(math.log(65.536) - 1.3862944 * jax.random.uniform(key_of[14], (12, D), jnp.float32) ** levels(key_of[14], (12, D), ((1, 4),), -0.2, 0.2)), 16.384, 65.536)
    second_bias_rows = jnp.clip(jnp.exp(jax.random.uniform(key_of[15], (2, D), jnp.float32, math.log(16.384), math.log(65.536))), 16.384, 65.536)
    ema_cols = centred(key_of[16], (15, D, D), D ** -0.5, 0.1875, ((1, 8), (2, 4)), jnp.float32)
    ema_rows = centred(key_of[17], (5, D, D), D ** -0.5, 0.1875, ((1, 4), (2, 8)), jnp.float32)
    ema_bias_cols = centred(key_of[18], (12, D), 0.5, 3.0, ((1, 4),), jnp.float32)
    ema_bias_rows = centred(key_of[19], (2, D), 0.5, 3.0, (), jnp.float32)
    return {"tokens": tokens, "seg_ids": seg_ids, "time_steps": time_steps, "cotangent": cotangent, "weight_cols": weight_cols, "weight_rows": weight_rows, "bias_cols": bias_cols, "bias_rows": bias_rows, "first_cols": first_cols, "first_rows": first_rows, "first_bias_cols": first_bias_cols, "first_bias_rows": first_bias_rows, "second_cols": second_cols, "second_rows": second_rows, "second_bias_cols": second_bias_cols, "second_bias_rows": second_bias_rows, "ema_cols": ema_cols, "ema_rows": ema_rows, "ema_bias_cols": ema_bias_cols, "ema_bias_rows": ema_bias_rows}


highest = lax.Precision.HIGHEST
beta_one = 0.9
beta_two = 0.999
adam_eps = 1e-08
decay_rate = 0.1
rate_matrix = 0.05
rate_vector = 0.5
ema_keep = 0.7
norm_eps = 1e-06
neg_large = -1e+30

@jax.custom_vjp
def low(v):
    return lax.optimization_barrier(v.astype(jnp.bfloat16)).astype(jnp.float32)

@jax.custom_vjp
def low_back(v):
    return v

def low_keep(v):
    return (low(v), None)

def low_pass(kept, grad):
    return (grad,)

def back_keep(v):
    return (v, None)

def back_low(kept, grad):
    return (low(grad),)
low.defvjp(low_keep, low_pass)
low_back.defvjp(back_keep, back_low)

def embedding_table(step_values, width_all):
    half_width = width_all // 2
    frequency = jnp.exp(-math.log(10000.0) * jnp.arange(half_width, dtype=jnp.float32) / half_width)
    angles = step_values.astype(jnp.float32)[..., None] * frequency
    return jnp.concatenate([jnp.cos(angles), jnp.sin(angles)], axis=-1)

def layer_norm(values):
    centre = values - lax.optimization_barrier(jnp.mean(values, axis=-1, keepdims=True))
    return centre * lax.rsqrt(lax.optimization_barrier(jnp.mean(centre * centre, axis=-1, keepdims=True)) + norm_eps)

def modulate(values, shift_rows, scale_rows):
    return layer_norm(values) * (1.0 + scale_rows) + shift_rows

def gelu_tanh(values):
    return jax.nn.gelu(values, approximate=True)

def attend_block(query_block, seg_block, keys_row, values_row, seg_row):
    scores = jnp.einsum('qhd,khd->hqk', query_block, keys_row, precision=highest) * HEAD_DIM ** (-0.5)
    scores = low_back(scores)
    scores = jnp.where((seg_block[:, None] == seg_row[None, :])[None], scores, neg_large)
    row_max = lax.optimization_barrier(jnp.max(scores, axis=-1, keepdims=True))
    weights = jnp.exp(scores - row_max)
    prob_low = low(weights / lax.optimization_barrier(jnp.sum(weights, axis=-1, keepdims=True)))
    return jnp.einsum('hqk,khd->qhd', prob_low, values_row, precision=highest)

def row_forward(tokens_row, seg_row, steps_row, weight_cols, weight_rows, bias_cols, bias_rows):
    cols_low = low(weight_cols)
    rows_low = low(weight_rows)
    own_width = D // N_MP
    head_count = HEADS // N_MP
    block_count = ROW_LEN // QB
    time_rows = embedding_table(steps_row, D)
    time_low = low(time_rows)
    ada_input = low(jax.nn.silu(time_rows))
    modulation = jnp.einsum('ud,jde->uje', ada_input, cols_low[9:15], precision=highest) + bias_cols[6:12][None]
    onehot = (seg_row[:, None] == jnp.arange(UNITS, dtype=jnp.int32)[None, :]).astype(jnp.float32)

    def spread(lookup):
        return jnp.dot(onehot, lookup, precision=highest)
    shift_one, scale_one, gate_one, shift_two, scale_two, gate_two = [spread(modulation[:, column]) for column in range(6)]
    input_one = low(modulate(tokens_row, shift_one, scale_one))
    time_query = spread(jnp.dot(time_low, cols_low[3], precision=highest))
    time_value = spread(jnp.dot(time_low, cols_low[4], precision=highest))
    seg_blocks = seg_row.reshape(block_count, QB)
    attn_total = jnp.zeros((ROW_LEN, D), jnp.float32)
    for member in range(N_MP):
        column_range = slice(member * own_width, (member + 1) * own_width)
        own_input = low_back(input_one)
        queries = low_back(low(jnp.dot(own_input, cols_low[0][:, column_range], precision=highest) + time_query[:, column_range] + bias_cols[0][column_range]))
        keys_all = low_back(low(jnp.dot(own_input, cols_low[1][:, column_range], precision=highest)))
        values_all = low_back(low(jnp.dot(own_input, cols_low[2][:, column_range], precision=highest) + time_value[:, column_range] + bias_cols[1][column_range]))
        keys_heads = keys_all.reshape(ROW_LEN, head_count, HEAD_DIM)
        values_heads = values_all.reshape(ROW_LEN, head_count, HEAD_DIM)
        query_blocks = queries.reshape(block_count, QB, head_count, HEAD_DIM)

        def attend_part(blocked, keys_heads=keys_heads, values_heads=values_heads):
            return attend_block(blocked[0], blocked[1], keys_heads, values_heads, seg_row)
        mixed_out = lax.map(jax.checkpoint(attend_part), (query_blocks, seg_blocks)).reshape(ROW_LEN, own_width)
        mixed_out = low_back(low(mixed_out))
        attn_total = attn_total + low(jnp.dot(mixed_out, rows_low[0][column_range, :], precision=highest))
    attended = low_back(attn_total) + bias_rows[0]
    hidden_one = tokens_row + gate_one * attended
    input_two = low(modulate(hidden_one, shift_two, scale_two))
    mlp_total = jnp.zeros((ROW_LEN, D), jnp.float32)
    for member in range(N_MP):
        column_range = slice(member * own_width, (member + 1) * own_width)
        own_input = low_back(input_two)
        inner_act = jnp.einsum('ld,rde->lre', own_input, cols_low[5:9][:, :, column_range], precision=highest) + bias_cols[2:6][:, column_range][None]
        inner_act = low_back(inner_act)
        active = low(gelu_tanh(inner_act))
        mlp_total = mlp_total + low(jnp.einsum('lre,red->ld', active, rows_low[1:5][:, column_range, :], precision=highest))
    mlp_out = low_back(mlp_total) + bias_rows[1]
    return hidden_one + gate_two * mlp_out

def adam_step(weight, gradient, first_old, second_old, ema_old, step_rate):
    first_new = beta_one * first_old + (1.0 - beta_one) * gradient
    second_new = beta_two * second_old + (1.0 - beta_two) * gradient * gradient
    first_hat = first_new / (1.0 - beta_one ** STEP)
    second_hat = second_new / (1.0 - beta_two ** STEP)
    weight_new = weight - step_rate * (first_hat / (jnp.sqrt(second_hat) + adam_eps) + decay_rate * weight)
    ema_new = ema_keep * ema_old + (1.0 - ema_keep) * weight_new
    return (first_new, second_new, weight_new, ema_new)

def reference(tokens, seg_ids, time_steps, cotangent, weight_cols, weight_rows, bias_cols, bias_rows, first_cols, first_rows, first_bias_cols, first_bias_rows, second_cols, second_rows, second_bias_cols, second_bias_rows, ema_cols, ema_rows, ema_bias_cols, ema_bias_rows):
    rows_all = TOKENS // ROW_LEN
    token_rows = tokens.astype(jnp.float32).reshape(rows_all, ROW_LEN, D)
    cot_rows = cotangent.astype(jnp.float32).reshape(rows_all, ROW_LEN, D)
    seg_rows = seg_ids.reshape(rows_all, ROW_LEN)

    def one_row(running, inputs):
        row_tokens, row_seg, row_steps, row_cot = inputs

        def forward(values, cols_part, rows_part, bias_cols_part, bias_rows_part):
            return row_forward(values, row_seg, row_steps, cols_part, rows_part, bias_cols_part, bias_rows_part)
        output, pullback = jax.vjp(forward, row_tokens, weight_cols, weight_rows, bias_cols, bias_rows)
        grad_list = pullback(row_cot)
        running = tuple((total_old + addend for total_old, addend in zip(running, grad_list[1:])))
        return (running, (output, grad_list[0]))
    zero_grads = (jnp.zeros_like(weight_cols), jnp.zeros_like(weight_rows), jnp.zeros_like(bias_cols), jnp.zeros_like(bias_rows))
    totals, (outputs, input_grads) = lax.scan(one_row, zero_grads, (token_rows, seg_rows, time_steps, cot_rows))
    cols_new = adam_step(weight_cols, totals[0], first_cols, second_cols, ema_cols, rate_matrix)
    rows_new = adam_step(weight_rows, totals[1], first_rows, second_rows, ema_rows, rate_matrix)
    bias_cols_state = adam_step(bias_cols, totals[2], first_bias_cols, second_bias_cols, ema_bias_cols, rate_vector)
    bias_rows_state = adam_step(bias_rows, totals[3], first_bias_rows, second_bias_rows, ema_bias_rows, rate_vector)
    out_tokens = outputs.reshape(TOKENS, D).astype(jnp.bfloat16)
    input_grad = input_grads.reshape(TOKENS, D)
    return (out_tokens, input_grad, cols_new[0], cols_new[1], cols_new[2], cols_new[3], rows_new[0], rows_new[1], rows_new[2], rows_new[3], bias_cols_state[0], bias_cols_state[1], bias_cols_state[2], bias_cols_state[3], bias_rows_state[0], bias_rows_state[1], bias_rows_state[2], bias_rows_state[3])
```

```python
import math

import jax
import jax.numpy as jnp
from jax import lax
from jax.experimental import pallas as pl
from jax.experimental.pallas import tpu as pltpu
from jax.sharding import PartitionSpec as P

HEAD_DIM = 72
STEP = 10
UNIT = 64
REACH = 192


highest = lax.Precision.HIGHEST
beta_one = 0.9
beta_two = 0.999
adam_eps = 1e-08
decay_rate = 0.1
rate_matrix = 0.05
rate_vector = 0.5
ema_keep = 0.7
norm_eps = 1e-06
neg_large = -1e30
score_scale = HEAD_DIM**-0.5
low = jnp.bfloat16
wide = jnp.float32

DOT_NN = (((1,), (0,)), ((), ()))
DOT_NT = (((1,), (1,)), ((), ()))
DOT_TN = (((0,), (0,)), ((), ()))

CORE_SWAP = [(i, i ^ 1) for i in range(4)]
CHIP_SWAP = [(i, i ^ 2) for i in range(4)]


def dot_as(left, right, dims):
    return lax.dot_general(left, right, dims, preferred_element_type=wide)


def ring_order(count):
    return list(range(0, count, 2)) + list(range(count - 1, 0, -2))


def ring_perms(count):
    order = ring_order(count)
    onward = [(order[i], order[(i + 1) % count]) for i in range(count)]
    return onward, [(b, a) for a, b in onward]


def ring_place(count):
    order = ring_order(count)
    spots = [order.index(i) for i in range(count)]
    return jnp.array(order), jnp.array(spots)[lax.axis_index("dp")]


def ring_gather(shard, count):
    if count not in (4, 8):
        return lax.all_gather(shard, "dp", axis=0, tiled=True)
    rows = shard.shape[0]
    half = rows // 2
    onward, backward = ring_perms(count)
    order, spot = ring_place(count)

    def put(whole, piece, back, offset=0):
        at = order[(spot + back) % count] * rows + offset
        return lax.dynamic_update_slice_in_dim(whole, piece, at, 0)

    whole = jnp.zeros((count * rows,) + shard.shape[1:], shard.dtype)
    whole = put(whole, shard, 0)
    ahead = behind = shard
    for hop in range(1, count // 2):
        ahead = lax.ppermute(ahead, "dp", onward)
        behind = lax.ppermute(behind, "dp", backward)
        whole = put(whole, ahead, -hop)
        whole = put(whole, behind, hop)
    ahead = lax.ppermute(ahead[:half], "dp", onward)
    behind = lax.ppermute(behind[half:], "dp", backward)
    whole = put(whole, ahead, count // 2)
    return put(whole, behind, count // 2, half)


def ring_scatter(parts, count):
    if count not in (4, 8):
        return lax.psum_scatter(parts.astype(low), "dp", scatter_dimension=0, tiled=True).astype(
            wide
        )
    rows = parts.shape[0] // count
    half = rows // 2
    onward, backward = ring_perms(count)
    order, spot = ring_place(count)

    def chunk(ahead, start, stop):
        at = order[(spot + ahead) % count] * rows + start
        return lax.dynamic_slice_in_dim(parts, at, stop - start, 0).astype(wide)

    def travel(perm, sign, hops, start, stop):
        running = chunk(sign * hops, start, stop).astype(low)
        for hop in range(hops - 1, 0, -1):
            running = lax.ppermute(running, "dp", perm).astype(wide)
            running = (running + chunk(sign * hop, start, stop)).astype(low)
        return lax.ppermute(running, "dp", perm).astype(wide)

    long, short = count // 2, count // 2 - 1
    first = travel(onward, 1, long, 0, half) + travel(backward, -1, short, 0, half)
    second = travel(onward, 1, short, half, rows) + travel(backward, -1, long, half, rows)
    return jnp.concatenate([first, second], 0) + chunk(0, 0, rows)


def share_steps(steps, count):
    if count not in (4, 8):
        return lax.all_gather(steps, "dp", axis=0, tiled=True)
    blank = jnp.zeros((count,) + steps.shape, steps.dtype)
    known = lax.dynamic_update_slice_in_dim(blank, steps[None], lax.axis_index("dp"), 0)
    reach = 1
    while reach < count:
        known = known + lax.ppermute(known, "dp", [(i, i ^ reach) for i in range(count)])
        reach *= 2
    return known.reshape((count * steps.shape[0],) + steps.shape[1:])


def group_scatter(kept, sent):
    half = kept + lax.ppermute(sent.astype(low), "mp", CORE_SWAP).astype(wide)
    quarter = half.shape[0] // 2
    got = lax.ppermute(half[quarter:].astype(low), "mp", CHIP_SWAP)
    return half[:quarter] + got.astype(wide)


def group_gather(own):
    chip = lax.ppermute(own, "mp", CHIP_SWAP)
    core = lax.ppermute(own, "mp", CORE_SWAP)
    both = lax.ppermute(chip, "mp", CORE_SWAP)
    return [own, chip, core, both]


def in_group_order(pieces, place):
    stacked = jnp.stack(pieces, 0)
    return [
        lax.dynamic_index_in_dim(stacked, jnp.bitwise_xor(place, j), 0, keepdims=False)
        for j in range(4)
    ]


def key_windows(row_len, block):
    return [
        (at, max(0, at - REACH), min(row_len, at + block + REACH))
        for at in range(0, row_len, block)
    ]


def attend_forward_kernel(place_ref, qkv_ref, seg_col_ref, seg_row_ref, out_ref, q_s, k_s, v_s, *, heads):
    row_len = qkv_ref.shape[0]
    width = heads * HEAD_DIM
    block = row_len // 4
    place = place_ref[0]
    for j in range(4):
        at = pl.multiple_of(jnp.bitwise_xor(place, j) * block, block)
        to = slice(j * block, (j + 1) * block)
        for h in range(heads):
            c = h * HEAD_DIM
            q_s[h, to, :] = qkv_ref[pl.ds(at, block), c : c + HEAD_DIM]
            k_s[h, to, :] = qkv_ref[pl.ds(at, block), width + c : width + c + HEAD_DIM]
            v_s[h, to, :] = qkv_ref[pl.ds(at, block), 2 * width + c : 2 * width + c + HEAD_DIM]
    for j, (at, start, stop) in enumerate(key_windows(row_len, block)):
        same = seg_col_ref[start:stop, :] == seg_row_ref[:, at : at + block]
        mixed = []
        for h in range(heads):
            scores = dot_as(k_s[h, start:stop, :], q_s[h, at : at + block, :], DOT_NT)
            scores = jnp.where(same, scores, neg_large)
            top = jnp.max(scores, axis=0, keepdims=True)
            weights = jnp.exp((scores - top) * score_scale)
            total = jnp.sum(weights, axis=0, keepdims=True)
            gathered = dot_as(v_s[h, start:stop, :], weights.astype(low), DOT_TN)
            mixed.append(gathered * (1.0 / total))
        to = pl.multiple_of(jnp.bitwise_xor(place, j) * block, block)
        out_ref[pl.ds(to, block), :] = jnp.concatenate(mixed, axis=0).T.astype(low)


def attend_backward_kernel(
    place_ref, qkv_ref, grad_ref, seg_col_ref, seg_row_ref, out_ref, q_s, k_s, v_s, g_s, dk_s, dv_s, *, heads
):
    row_len = qkv_ref.shape[0]
    width = heads * HEAD_DIM
    block = row_len // 4
    place = place_ref[0]
    dk_s[...] = jnp.zeros_like(dk_s)
    dv_s[...] = jnp.zeros_like(dv_s)
    for j in range(4):
        at = pl.multiple_of(jnp.bitwise_xor(place, j) * block, block)
        to = slice(j * block, (j + 1) * block)
        for h in range(heads):
            c = h * HEAD_DIM
            q_s[h, to, :] = qkv_ref[pl.ds(at, block), c : c + HEAD_DIM]
            k_s[h, to, :] = qkv_ref[pl.ds(at, block), width + c : width + c + HEAD_DIM]
            v_s[h, to, :] = qkv_ref[pl.ds(at, block), 2 * width + c : 2 * width + c + HEAD_DIM]
            g_s[h, to, :] = grad_ref[pl.ds(at, block), c : c + HEAD_DIM]
    for j, (at, start, stop) in enumerate(key_windows(row_len, block)):
        same = seg_col_ref[start:stop, :] == seg_row_ref[:, at : at + block]
        grads = []
        for h in range(heads):
            query = q_s[h, at : at + block, :]
            grad = g_s[h, at : at + block, :]
            keys = k_s[h, start:stop, :]
            scores = jnp.where(same, dot_as(keys, query, DOT_NT), neg_large)
            top = jnp.max(scores, axis=0, keepdims=True)
            weights = jnp.exp((scores - top) * score_scale)
            probs = weights * (1.0 / jnp.sum(weights, axis=0, keepdims=True))
            grad_probs = dot_as(v_s[h, start:stop, :], grad, DOT_NT)
            inner = jnp.sum(grad_probs * probs, axis=0, keepdims=True)
            grad_scores = (probs * (grad_probs - inner)).astype(low)
            dv_s[h, start:stop, :] += dot_as(probs.astype(low), grad, DOT_NN)
            dk_s[h, start:stop, :] += dot_as(grad_scores, query, DOT_NN)
            grads.append(dot_as(keys, grad_scores, DOT_TN) * score_scale)
        to = pl.multiple_of(jnp.bitwise_xor(place, j) * block, block)
        out_ref[pl.ds(to, block), 0:width] = jnp.concatenate(grads, axis=0).T.astype(low)
    for j in range(4):
        at = slice(j * block, (j + 1) * block)
        to = pl.multiple_of(jnp.bitwise_xor(place, j) * block, block)
        out_ref[pl.ds(to, block), width : 2 * width] = jnp.concatenate(
            [(dk_s[h, at, :] * score_scale).astype(low) for h in range(heads)], axis=1
        )
        out_ref[pl.ds(to, block), 2 * width : 3 * width] = jnp.concatenate(
            [dv_s[h, at, :].astype(low) for h in range(heads)], axis=1
        )


def in_vmem(count):
    return [pl.BlockSpec(memory_space=pltpu.SMEM)] + [pl.BlockSpec(memory_space=pltpu.VMEM)] * count


def attend_forward(place, qkv, seg_row):
    row_len, width = qkv.shape[0], qkv.shape[1] // 3
    heads = width // HEAD_DIM

    def body(*refs):
        attend_forward_kernel(*refs, heads=heads)

    return pl.pallas_call(
        body,
        out_shape=jax.ShapeDtypeStruct((row_len, width), low),
        in_specs=in_vmem(3),
        out_specs=pl.BlockSpec(memory_space=pltpu.VMEM),
        scratch_shapes=[pltpu.VMEM((heads, row_len, HEAD_DIM), low)] * 3,
        compiler_params=pltpu.CompilerParams(vmem_limit_bytes=32 * 2**20),
        cost_estimate=pl.CostEstimate(
            flops=4 * row_len * 640 * width, bytes_accessed=8 * row_len * width, transcendentals=heads * row_len * 640
        ),
        name="attend_forward",
    )(place, qkv, seg_row.reshape(row_len, 1), seg_row.reshape(1, row_len))


def attend_backward(place, qkv, grad, seg_row):
    row_len, width = qkv.shape[0], qkv.shape[1] // 3
    heads = width // HEAD_DIM

    def body(*refs):
        attend_backward_kernel(*refs, heads=heads)

    return pl.pallas_call(
        body,
        out_shape=jax.ShapeDtypeStruct((row_len, 3 * width), low),
        in_specs=in_vmem(4),
        out_specs=pl.BlockSpec(memory_space=pltpu.VMEM),
        scratch_shapes=[pltpu.VMEM((heads, row_len, HEAD_DIM), low)] * 4
        + [pltpu.VMEM((heads, row_len, HEAD_DIM), wide)] * 2,
        compiler_params=pltpu.CompilerParams(vmem_limit_bytes=40 * 2**20),
        cost_estimate=pl.CostEstimate(
            flops=10 * row_len * 640 * width, bytes_accessed=14 * row_len * width, transcendentals=heads * row_len * 640
        ),
        name="attend_backward",
    )(place, qkv, grad, seg_row.reshape(row_len, 1), seg_row.reshape(1, row_len))


def norm_parts(values):
    centre = values - jnp.mean(values, axis=-1, keepdims=True)
    inverse = lax.rsqrt(jnp.mean(centre * centre, axis=-1, keepdims=True) + norm_eps)
    return centre * inverse, inverse


def norm_back(normed, inverse, grad):
    return inverse * (
        grad
        - jnp.mean(grad, axis=-1, keepdims=True)
        - normed * jnp.mean(grad * normed, axis=-1, keepdims=True)
    )


def gelu_tanh(values):
    return jax.nn.gelu(values, approximate=True)


def adam_step(weight, gradient, first_old, second_old, ema_old, step_rate):
    first_new = beta_one * first_old + (1.0 - beta_one) * gradient
    second_new = beta_two * second_old + (1.0 - beta_two) * gradient * gradient
    first_hat = first_new / (1.0 - beta_one**STEP)
    second_hat = second_new / (1.0 - beta_two**STEP)
    weight_new = weight - step_rate * (
        first_hat / (jnp.sqrt(second_hat) + adam_eps) + decay_rate * weight
    )
    ema_new = ema_keep * ema_old + (1.0 - ema_keep) * weight_new
    return (first_new, second_new, weight_new, ema_new)


def per_device(
    tokens,
    seg_ids,
    time_steps,
    cotangent,
    weight_cols,
    weight_rows,
    bias_cols,
    bias_rows,
    first_cols,
    first_rows,
    first_bias_cols,
    first_bias_rows,
    second_cols,
    second_rows,
    second_bias_cols,
    second_bias_rows,
    ema_cols,
    ema_rows,
    ema_bias_cols,
    ema_bias_rows,
):
    own_width = weight_cols.shape[2]
    own_depth = weight_cols.shape[1]
    width = tokens.shape[1]
    rows = time_steps.shape[0]
    slots = time_steps.shape[1]
    row_len = tokens.shape[0] // rows
    units = row_len // UNIT
    quarter = row_len // 4
    quarter_units = units // 4
    dp_count = width // own_depth
    dp_place = lax.axis_index("dp")
    mp_place = lax.axis_index("mp")
    core, chip = mp_place % 2, mp_place // 2
    place = 2 * core + chip
    place_arg = place.reshape(1).astype(jnp.int32)

    cols_low = weight_cols.astype(low)
    rows_low = weight_rows.astype(low)
    own_qkv = jnp.concatenate([cols_low[0], cols_low[1], cols_low[2]], 1)
    own_rows = rows_low.transpose(2, 0, 1).reshape(own_depth, 5 * own_width)
    own_rest = jnp.concatenate([own_rows[:, :own_width]] + [cols_low[5 + i] for i in range(4)] + [own_rows[:, own_width:]], 1)
    w_qkv = ring_gather(own_qkv, dp_count)
    w_rest = lax.all_gather(own_rest, "dp", axis=0, tiled=True)
    w_out = w_rest[:, :own_width]
    w_up = w_rest[:, own_width : 5 * own_width]
    w_down = w_rest[:, 5 * own_width :]

    steps_all = share_steps(time_steps, dp_count).reshape(-1)
    half_width = width // 2
    feature = dp_place * own_depth + jnp.arange(own_depth)
    is_cos = feature < half_width
    index = jnp.where(is_cos, feature, feature - half_width).astype(wide)
    frequency = jnp.exp(-math.log(10000.0) * index / half_width)
    angles = steps_all.astype(wide)[:, None] * frequency[None, :]
    time_rows = jnp.where(is_cos[None, :], jnp.cos(angles), jnp.sin(angles))
    time_low = time_rows.astype(low)
    ada_low = jax.nn.silu(time_rows).astype(low)
    part_ada = jnp.einsum("sd,jde->sje", ada_low, cols_low[9:15], preferred_element_type=wide)
    part_time = jnp.einsum("sd,jde->sje", time_low, cols_low[3:5], preferred_element_type=wide)
    part_slots = jnp.concatenate([part_ada, part_time], 1).astype(low).reshape(-1, 8 * own_width)
    own_slots = ring_scatter(part_slots, dp_count).reshape(rows * slots, 8, own_width)
    own_mod = (own_slots[:, :6] + bias_cols[6:12][None]).astype(low)
    pieces = group_gather(own_mod)
    pieces = [pieces[0], pieces[2], pieces[1], pieces[3]]
    modulation = jnp.concatenate(in_group_order(pieces, mp_place), 2).astype(wide)
    modulation = modulation.reshape(rows, slots, 6 * width)
    zero_cols = jnp.zeros((rows * slots, own_width), wide)
    time_add = jnp.concatenate(
        [own_slots[:, 6] + bias_cols[0], zero_cols, own_slots[:, 7] + bias_cols[1]], 1
    ).reshape(rows, slots, 3 * own_width)

    def relative(values):
        return jnp.concatenate(
            [
                lax.dynamic_slice_in_dim(values, jnp.bitwise_xor(place, j) * (values.shape[0] // 4), values.shape[0] // 4, 0)
                for j in range(4)
            ],
            0,
        )

    seg_grid = seg_ids.reshape(rows, row_len)
    token_grid = tokens.reshape(rows, row_len, width)
    cot_grid = cotangent.reshape(rows, row_len, width)
    onehots, unit_mods, own_mods, tokens_rel, cots_rel = [], [], [], [], []
    inputs_one, qkvs, mixed = [], [], []
    for r in range(rows):
        unit_seg = relative(seg_grid[r].reshape(units, UNIT)[:, 0])
        onehot = (unit_seg[:, None] == jnp.arange(slots, dtype=jnp.int32)).astype(wide)
        unit_mod = jnp.dot(onehot, modulation[r], precision=highest).reshape(units, 6, 1, width)
        unit_add = jnp.dot(onehot, time_add[r], precision=highest)
        onehots.append(onehot)
        unit_mods.append(unit_mod)
        source = relative(token_grid[r])
        tokens_rel.append(source)
        cots_rel.append(relative(cot_grid[r]))
        normed, _ = norm_parts(source.astype(wide).reshape(units, UNIT, width))
        input_one = (normed * (1.0 + unit_mod[:, 1]) + unit_mod[:, 0]).astype(low)
        input_one = input_one.reshape(row_len, width)
        qkv = dot_as(input_one, w_qkv, DOT_NN).reshape(units, UNIT, 3 * own_width)
        qkv = (qkv + unit_add[:, None, :]).astype(low).reshape(row_len, 3 * own_width)
        inputs_one.append(input_one)
        qkvs.append(qkv)
        mixed.append(attend_forward(place_arg, qkv, seg_grid[r]))

    half = row_len // 2
    hidden_ones, attendeds, inputs_two = [], [], []
    for r in range(rows):
        sent = dot_as(mixed[r][half:], w_out, DOT_NT).astype(low)
        kept = dot_as(mixed[r][:half], w_out, DOT_NT)
        attended = group_scatter(kept, sent) + bias_rows[0]
        attended = attended.reshape(quarter_units, UNIT, width)
        own = unit_mods[r][:quarter_units]
        source = tokens_rel[r][:quarter].astype(wide).reshape(quarter_units, UNIT, width)
        hidden_one = source + own[:, 2] * attended
        normed, _ = norm_parts(hidden_one)
        input_two = (normed * (1.0 + own[:, 4]) + own[:, 3]).astype(low).reshape(quarter, width)
        hidden_ones.append(hidden_one)
        attendeds.append(attended)
        inputs_two.append(jnp.concatenate(group_gather(input_two), 0))

    bias_up = bias_cols[2:6].reshape(-1)
    out_rows, mlp_kept, grad_rows_low = [], [], []
    fields = [[] for _ in range(rows)]
    grad_w_up = grad_w_down = grad_w_out = grad_w_qkv = 0.0
    bias_up_grad = 0.0
    bias_row_two = bias_row_one = 0.0
    grad_hiddens, grad_attendeds = [], []
    for r in range(rows):
        own = unit_mods[r][:quarter_units]
        inner = dot_as(inputs_two[r], w_up, DOT_NN) + bias_up
        active = gelu_tanh(inner).astype(low)
        grad_mlp = (
            cots_rel[r].astype(wide).reshape(units, UNIT, width) * unit_mods[r][:, 5]
        ).reshape(row_len, width)
        grad_mlp_low = grad_mlp.astype(low)
        grad_active = dot_as(grad_mlp_low, w_down, DOT_NN)
        grad_inner = jax.vjp(gelu_tanh, inner)[1](grad_active)[0].astype(low)
        bias_up_grad = bias_up_grad + jnp.sum(grad_inner.astype(wide), axis=0)
        sent = dot_as(grad_inner[half:], w_up, DOT_NT).astype(low)
        kept = dot_as(grad_inner[:half], w_up, DOT_NT)
        grad_two = group_scatter(kept, sent).reshape(quarter_units, UNIT, width)
        grad_out = cots_rel[r][:quarter].astype(wide).reshape(quarter_units, UNIT, width)
        normed, inverse = norm_parts(hidden_ones[r])
        grad_hidden = grad_out + norm_back(normed, inverse, grad_two * (1.0 + own[:, 4]))
        grad_attended = grad_hidden * own[:, 2]
        grad_attendeds.append(
            jnp.concatenate(group_gather(grad_attended.astype(low).reshape(quarter, width)), 0)
        )
        bias_row_one = bias_row_one + jnp.sum(grad_attended, axis=(0, 1))
        grad_hiddens.append(grad_hidden)
        sent = dot_as(active[half:], w_down, DOT_NT).astype(low)
        kept = dot_as(active[:half], w_down, DOT_NT)
        mlp_out = (group_scatter(kept, sent) + bias_rows[1]).reshape(quarter_units, UNIT, width)
        out_own = (hidden_ones[r] + own[:, 5] * mlp_out).astype(low).reshape(quarter, width)
        out_rows.extend(in_group_order(group_gather(out_own), place))
        bias_row_two = bias_row_two + jnp.sum(grad_mlp[:quarter], axis=0)
        fields[r] = {
            2: jnp.sum(grad_hidden * attendeds[r], axis=1),
            3: jnp.sum(grad_two, axis=1),
            4: jnp.sum(grad_two * normed, axis=1),
            5: jnp.sum(grad_out * mlp_out, axis=1),
        }
        grad_w_up = grad_w_up + dot_as(inputs_two[r], grad_inner, DOT_TN)
        grad_w_down = grad_w_down + dot_as(grad_mlp_low, active, DOT_TN)

    time_sums = []
    input_rows = []
    for r in range(rows):
        grad_mixed = dot_as(grad_attendeds[r], w_out, DOT_NN).astype(low)
        grad_w_out = grad_w_out + dot_as(grad_attendeds[r], mixed[r], DOT_TN)
        grad_qkv = attend_backward(place_arg, qkvs[r], grad_mixed, seg_grid[r])
        sent = dot_as(grad_qkv[half:], w_qkv, DOT_NT).astype(low)
        kept = dot_as(grad_qkv[:half], w_qkv, DOT_NT)
        grad_one = group_scatter(kept, sent).reshape(quarter_units, UNIT, width)
        grad_w_qkv = grad_w_qkv + dot_as(inputs_one[r], grad_qkv, DOT_TN)
        own = unit_mods[r][:quarter_units]
        source = tokens_rel[r][:quarter].astype(wide).reshape(quarter_units, UNIT, width)
        normed, inverse = norm_parts(source)
        input_grad = grad_hiddens[r] + norm_back(normed, inverse, grad_one * (1.0 + own[:, 1]))
        input_rows.extend(
            in_group_order(group_gather(input_grad.astype(low).reshape(quarter, width)), place)
        )
        fields[r][0] = jnp.sum(grad_one, axis=1)
        fields[r][1] = jnp.sum(grad_one * normed, axis=1)
        unit_sums = jnp.sum(grad_qkv.astype(wide).reshape(units, UNIT, 3 * own_width), axis=1)
        slot_sums = jnp.dot(onehots[r].T, unit_sums, precision=highest)
        time_sums.append(
            jnp.stack([slot_sums[:, :own_width], slot_sums[:, 2 * own_width :]], 1)
        )
    out_tokens = jnp.concatenate(out_rows, 0)
    input_grads = jnp.concatenate(input_rows, 0).astype(wide)

    field_grid = jnp.stack(
        [jnp.stack([fields[r][f] for f in range(6)], 1) for r in range(rows)], 0
    ).astype(low)
    field_grid = field_grid.reshape(rows, quarter_units, 6, 2, 2, own_width)

    def side(values, which, axis):
        return lax.dynamic_index_in_dim(values, which, axis, keepdims=False)

    other = lax.ppermute(side(field_grid, 1 - chip, 3), "mp", CHIP_SWAP)
    field_grid = jnp.concatenate([side(field_grid, chip, 3), other], 1)
    other = lax.ppermute(side(field_grid, 1 - core, 3), "mp", CORE_SWAP)
    field_grid = jnp.concatenate([side(field_grid, core, 3), other], 1)
    slot_grads = [
        jnp.dot(onehots[r].T, field_grid[r].reshape(units, 6 * own_width).astype(wide), precision=highest)
        for r in range(rows)
    ]
    slot_grads = jnp.concatenate(
        [jnp.concatenate(slot_grads, 0), jnp.concatenate(time_sums, 0).reshape(rows * slots, 2 * own_width)], 1
    ).astype(low)
    bias_up_rows = jnp.zeros((8, 8 * own_width), low)
    bias_up_rows = bias_up_rows.at[0, : 4 * own_width].set(bias_up_grad.astype(low))
    slot_grads = ring_gather(jnp.concatenate([slot_grads, bias_up_rows], 0), dp_count)
    slot_grads = slot_grads.reshape(dp_count, rows * slots + 8, 8, own_width)
    bias_up_sum = jnp.sum(slot_grads[:, rows * slots, :4].astype(wide), axis=0)
    slot_grads = slot_grads[:, : rows * slots].reshape(dp_count * rows * slots, 8, own_width)
    ada_grad = jnp.einsum("sd,sje->jde", ada_low, slot_grads[:, :6], preferred_element_type=wide)
    time_grad = jnp.einsum("sd,sje->jde", time_low, slot_grads[:, 6:], preferred_element_type=wide)
    slot_sum = jnp.sum(slot_grads.astype(wide), axis=0)

    rest_parts = jnp.concatenate([grad_w_out, grad_w_up, grad_w_down], 1).astype(low)
    rest_sum = lax.psum_scatter(rest_parts, "dp", scatter_dimension=0, tiled=True).astype(wide)
    qkv_sum = ring_scatter(grad_w_qkv.astype(low), dp_count)

    def slabs(values):
        return [values[:, i * own_width : (i + 1) * own_width] for i in range(values.shape[1] // own_width)]

    grad_cols = jnp.concatenate(
        [
            jnp.stack(slabs(qkv_sum), 0),
            time_grad,
            jnp.stack(slabs(rest_sum[:, own_width : 5 * own_width]), 0),
            ada_grad,
        ],
        0,
    )
    rows_sum = jnp.concatenate([rest_sum[:, :own_width], rest_sum[:, 5 * own_width :]], 1)
    grad_rows = rows_sum.reshape(own_depth, 5, own_width).transpose(1, 2, 0)
    bias_cols_sum = jnp.concatenate([slot_sum[6:8], bias_up_sum, slot_sum[:6]], 0)
    bias_rows_sum = lax.psum(jnp.stack([bias_row_one, bias_row_two], 0), ("dp", "mp"))

    cols_state = adam_step(weight_cols, grad_cols, first_cols, second_cols, ema_cols, rate_matrix)
    rows_state = adam_step(weight_rows, grad_rows, first_rows, second_rows, ema_rows, rate_matrix)
    bias_cols_state = adam_step(
        bias_cols, bias_cols_sum, first_bias_cols, second_bias_cols, ema_bias_cols, rate_vector
    )
    bias_rows_state = adam_step(
        bias_rows, bias_rows_sum, first_bias_rows, second_bias_rows, ema_bias_rows, rate_vector
    )
    return (out_tokens, input_grads) + cols_state + rows_state + bias_cols_state + bias_rows_state


def solution(mesh):
    cols, rows, bias = P(None, "dp", "mp"), P(None, "mp", "dp"), P(None, "mp")
    state = (cols, rows, bias, P())
    placed = (P("dp", None), P("dp"), P("dp", None), P("dp", None)) + state * 4
    given = (P("dp", None), P("dp", None)) + (cols,) * 4 + (rows,) * 4 + (bias,) * 4 + (P(),) * 4
    return jax.shard_map(
        per_device, mesh=mesh, in_specs=placed, out_specs=given, check_vma=False
    )
```

```python
import math

import jax
import jax.numpy as jnp
from jax import lax
from jax.experimental import pallas as pl
from jax.experimental.pallas import tpu as pltpu
from jax.sharding import PartitionSpec as P

HEAD_DIM = 72
STEP = 10
UNIT = 64
REACH = 192


highest = lax.Precision.HIGHEST
beta_one = 0.9
beta_two = 0.999
adam_eps = 1e-08
decay_rate = 0.1
rate_matrix = 0.05
rate_vector = 0.5
ema_keep = 0.7
norm_eps = 1e-06
neg_large = -1e30
score_scale = HEAD_DIM**-0.5
low = jnp.bfloat16
wide = jnp.float32

DOT_NN = (((1,), (0,)), ((), ()))
DOT_NT = (((1,), (1,)), ((), ()))
DOT_TN = (((0,), (0,)), ((), ()))

CORE_SWAP = [(i, i ^ 1) for i in range(4)]
CHIP_SWAP = [(i, i ^ 2) for i in range(4)]


def dot_as(left, right, dims):
    return lax.dot_general(left, right, dims, preferred_element_type=wide)


def ring_order(count):
    return list(range(0, count, 2)) + list(range(count - 1, 0, -2))


def ring_perms(count):
    order = ring_order(count)
    onward = [(order[i], order[(i + 1) % count]) for i in range(count)]
    return onward, [(b, a) for a, b in onward]


def ring_place(count):
    order = ring_order(count)
    spots = [order.index(i) for i in range(count)]
    return jnp.array(order), jnp.array(spots)[lax.axis_index("dp")]


def ring_pieces(shard, count):
    rows = shard.shape[0]
    cut = rows // 32 * 16
    onward, backward = ring_perms(count)
    order, spot = ring_place(count)
    pieces, rows_at = [shard], [order[spot] * rows]
    ahead = behind = shard
    for hop in range(1, count // 2):
        ahead = lax.ppermute(ahead, "dp", onward)
        behind = lax.ppermute(behind, "dp", backward)
        pieces += [ahead, behind]
        rows_at += [order[(spot - hop) % count] * rows, order[(spot + hop) % count] * rows]
    far = order[(spot + count // 2) % count] * rows
    pieces += [
        lax.ppermute(ahead[:cut], "dp", onward),
        lax.ppermute(behind[cut:], "dp", backward),
    ]
    return pieces, jnp.stack(rows_at + [far, far + cut]).astype(jnp.int32)


def place_kernel(at_ref, *refs):
    count = len(refs) // 2 - 1
    pieces, out_ref, sems = refs[:-2], refs[-2], refs[-1]
    copies = [
        pltpu.make_async_copy(
            piece, out_ref.at[pl.ds(pl.multiple_of(at_ref[i], 16), piece.shape[0])], sems.at[i]
        )
        for i, piece in enumerate(pieces)
    ]
    for copy in copies:
        copy.start()
    for copy in copies:
        copy.wait()


def ring_gather(shard, count):
    if count not in (4, 8):
        return lax.all_gather(shard, "dp", axis=0, tiled=True)
    pieces, at = ring_pieces(shard, count)
    return place_pieces(at, pieces)


def ring_scatter(parts, count, split=True):
    if count not in (4, 8):
        return lax.psum_scatter(parts.astype(low), "dp", scatter_dimension=0, tiled=True).astype(
            wide
        )
    rows = parts.shape[0] // count
    half = rows // 2
    onward, backward = ring_perms(count)
    order, spot = ring_place(count)

    def chunk(ahead, start, stop):
        at = order[(spot + ahead) % count] * rows + start
        return lax.dynamic_slice_in_dim(parts, at, stop - start, 0).astype(wide)

    def travel(perm, sign, hops, start, stop):
        running = chunk(sign * hops, start, stop).astype(low)
        for hop in range(hops - 1, 0, -1):
            running = lax.ppermute(running, "dp", perm).astype(wide)
            running = (running + chunk(sign * hop, start, stop)).astype(low)
        return lax.ppermute(running, "dp", perm).astype(wide)

    long, short = count // 2, count // 2 - 1
    if not split:
        both = travel(onward, 1, long, 0, rows) + travel(backward, -1, short, 0, rows)
        return both + chunk(0, 0, rows)
    first = travel(onward, 1, long, 0, half) + travel(backward, -1, short, 0, half)
    second = travel(onward, 1, short, half, rows) + travel(backward, -1, long, half, rows)
    return jnp.concatenate([first, second], 0) + chunk(0, 0, rows)


def share_steps(steps, count):
    if count not in (4, 8):
        return lax.all_gather(steps, "dp", axis=0, tiled=True)
    blank = jnp.zeros((count,) + steps.shape, steps.dtype)
    known = lax.dynamic_update_slice_in_dim(blank, steps[None], lax.axis_index("dp"), 0)
    reach = 1
    while reach < count:
        known = known + lax.ppermute(known, "dp", [(i, i ^ reach) for i in range(count)])
        reach *= 2
    return known.reshape((count * steps.shape[0],) + steps.shape[1:])


def group_scatter(kept, sent):
    quarter = kept.shape[0] // 2
    got = lax.ppermute(sent, "mp", CORE_SWAP)
    passed = (kept[quarter:] + got[quarter:].astype(wide)).astype(low)
    return kept, got, lax.ppermute(passed, "mp", CHIP_SWAP)


def group_gather(own):
    chip = lax.ppermute(own, "mp", CHIP_SWAP)
    core = lax.ppermute(own, "mp", CORE_SWAP)
    both = lax.ppermute(chip, "mp", CORE_SWAP)
    return [own, chip, core, both]


def in_group_order(pieces, place):
    stacked = jnp.stack(pieces, 0)
    return [
        lax.dynamic_index_in_dim(stacked, jnp.bitwise_xor(place, j), 0, keepdims=False)
        for j in range(4)
    ]


def key_windows(row_len, block):
    return [
        (at, max(0, at - REACH), min(row_len, at + block + REACH))
        for at in range(0, row_len, block)
    ]


def relative_at(place, j, block):
    return pl.multiple_of(jnp.bitwise_xor(place, j) * block, block)


def attend_forward_kernel(
    place_ref, qkv_ref, seg_col_ref, seg_row_ref, w_ref, out_ref, kept_ref, sent_ref, q_s, k_s, v_s, *, heads
):
    row_len = qkv_ref.shape[0]
    width = heads * HEAD_DIM
    block = row_len // 4
    place = place_ref[0]
    for j in range(4):
        at = relative_at(place, j, block)
        to = slice(j * block, (j + 1) * block)
        for h in range(heads):
            c = h * HEAD_DIM
            q_s[h, to, :] = qkv_ref[pl.ds(at, block), c : c + HEAD_DIM]
            k_s[h, to, :] = qkv_ref[pl.ds(at, block), width + c : width + c + HEAD_DIM]
            v_s[h, to, :] = qkv_ref[pl.ds(at, block), 2 * width + c : 2 * width + c + HEAD_DIM]
    for j, (at, start, stop) in enumerate(key_windows(row_len, block)):
        same = seg_col_ref[start:stop, :] == seg_row_ref[:, at : at + block]
        mixed = []
        for h in range(heads):
            scores = dot_as(k_s[h, start:stop, :], q_s[h, at : at + block, :], DOT_NT)
            scores = jnp.where(same, scores, neg_large)
            top = jnp.max(scores, axis=0, keepdims=True)
            weights = jnp.exp((scores - top) * score_scale)
            total = jnp.sum(weights, axis=0, keepdims=True)
            gathered = dot_as(v_s[h, start:stop, :], weights.astype(low), DOT_TN)
            mixed.append(gathered * (1.0 / total))
        out_ref[pl.ds(relative_at(place, j, block), block), :] = (
            jnp.concatenate(mixed, axis=0).T.astype(low)
        )
    w_out = w_ref[:, 3 * width :]
    half = row_len // 2
    kept_ref[...] = dot_as(out_ref[:half, :], w_out, DOT_NT)
    sent_ref[...] = dot_as(out_ref[half:, :], w_out, DOT_NT).astype(low)


def attend_backward_kernel(
    place_ref, qkv_ref, g0_ref, g1_ref, g2_ref, g3_ref, seg_col_ref, seg_row_ref, w_ref,
    out_ref, kept_ref, sent_ref, sums_ref, q_s, k_s, v_s, g_s, dk_s, dv_s, *, heads
):
    row_len = qkv_ref.shape[0]
    width = heads * HEAD_DIM
    block = row_len // 4
    place = place_ref[0]
    dk_s[...] = jnp.zeros_like(dk_s)
    dv_s[...] = jnp.zeros_like(dv_s)
    w_out = w_ref[:, 3 * width :]
    for j, g_ref in enumerate((g0_ref, g1_ref, g2_ref, g3_ref)):
        grad = dot_as(g_ref[...], w_out, DOT_NN).astype(low)
        at = relative_at(place, j, block)
        for h in range(heads):
            g_s[h, pl.ds(at, block), :] = grad[:, h * HEAD_DIM : (h + 1) * HEAD_DIM]
    for j in range(4):
        at = relative_at(place, j, block)
        to = slice(j * block, (j + 1) * block)
        for h in range(heads):
            c = h * HEAD_DIM
            q_s[h, to, :] = qkv_ref[pl.ds(at, block), c : c + HEAD_DIM]
            k_s[h, to, :] = qkv_ref[pl.ds(at, block), width + c : width + c + HEAD_DIM]
            v_s[h, to, :] = qkv_ref[pl.ds(at, block), 2 * width + c : 2 * width + c + HEAD_DIM]
    for j, (at, start, stop) in enumerate(key_windows(row_len, block)):
        same = seg_col_ref[start:stop, :] == seg_row_ref[:, at : at + block]
        grads = []
        for h in range(heads):
            query = q_s[h, at : at + block, :]
            grad = g_s[h, at : at + block, :]
            keys = k_s[h, start:stop, :]
            scores = jnp.where(same, dot_as(keys, query, DOT_NT), neg_large)
            top = jnp.max(scores, axis=0, keepdims=True)
            weights = jnp.exp((scores - top) * score_scale)
            probs = weights * (1.0 / jnp.sum(weights, axis=0, keepdims=True))
            grad_probs = dot_as(v_s[h, start:stop, :], grad, DOT_NT)
            inner = jnp.sum(grad_probs * probs, axis=0, keepdims=True)
            grad_scores = (probs * (grad_probs - inner)).astype(low)
            dv_s[h, start:stop, :] += dot_as(probs.astype(low), grad, DOT_NN)
            dk_s[h, start:stop, :] += dot_as(grad_scores, query, DOT_NN)
            grads.append(dot_as(keys, grad_scores, DOT_TN) * score_scale)
        out_ref[pl.ds(relative_at(place, j, block), block), 0:width] = (
            jnp.concatenate(grads, axis=0).T.astype(low)
        )
    for j in range(4):
        at = slice(j * block, (j + 1) * block)
        to = relative_at(place, j, block)
        out_ref[pl.ds(to, block), width : 2 * width] = jnp.concatenate(
            [(dk_s[h, at, :] * score_scale).astype(low) for h in range(heads)], axis=1
        )
        out_ref[pl.ds(to, block), 2 * width : 3 * width] = jnp.concatenate(
            [dv_s[h, at, :].astype(low) for h in range(heads)], axis=1
        )
    half = row_len // 2
    w_qkv = w_ref[:, : 3 * width]
    kept_ref[...] = dot_as(out_ref[:half, :], w_qkv, DOT_NT)
    sent_ref[...] = dot_as(out_ref[half:, :], w_qkv, DOT_NT).astype(low)
    for u in range(row_len // UNIT):
        sums_ref[u : u + 1, :] = jnp.sum(
            out_ref[u * UNIT : (u + 1) * UNIT, :].astype(wide), axis=0, keepdims=True
        )


SMEM_SPEC = pl.BlockSpec(memory_space=pltpu.SMEM)
VMEM_SPEC = pl.BlockSpec(memory_space=pltpu.VMEM)


def shape_of(shape, kind):
    return jax.ShapeDtypeStruct(shape, kind)


def attend_forward(place, qkv, seg_row, weights):
    row_len, width = qkv.shape[0], qkv.shape[1] // 3
    heads = width // HEAD_DIM
    full = weights.shape[0]

    def body(*refs):
        attend_forward_kernel(*refs, heads=heads)

    return pl.pallas_call(
        body,
        out_shape=(
            shape_of((row_len, width), low),
            shape_of((row_len // 2, full), wide),
            shape_of((row_len // 2, full), low),
        ),
        in_specs=[SMEM_SPEC] + [VMEM_SPEC] * 4,
        out_specs=(VMEM_SPEC,) * 3,
        scratch_shapes=[pltpu.VMEM((heads, row_len, HEAD_DIM), low)] * 3,
        compiler_params=pltpu.CompilerParams(vmem_limit_bytes=40 * 2**20),
        cost_estimate=pl.CostEstimate(
            flops=4 * row_len * 640 * width + 2 * row_len * width * full,
            bytes_accessed=8 * row_len * width + 5 * row_len * full,
            transcendentals=heads * row_len * 640,
        ),
        name="attend_forward",
    )(place, qkv, seg_row.reshape(row_len, 1), seg_row.reshape(1, row_len), weights)


def attend_backward(place, qkv, grads, seg_row, weights):
    row_len, width = qkv.shape[0], qkv.shape[1] // 3
    heads = width // HEAD_DIM
    full = weights.shape[0]

    def body(*refs):
        attend_backward_kernel(*refs, heads=heads)

    return pl.pallas_call(
        body,
        out_shape=(
            shape_of((row_len, 3 * width), low),
            shape_of((row_len // 2, full), wide),
            shape_of((row_len // 2, full), low),
            shape_of((row_len // UNIT, 3 * width), wide),
        ),
        in_specs=[SMEM_SPEC] + [VMEM_SPEC] * 8,
        out_specs=(VMEM_SPEC,) * 4,
        scratch_shapes=[pltpu.VMEM((heads, row_len, HEAD_DIM), low)] * 4
        + [pltpu.VMEM((heads, row_len, HEAD_DIM), wide)] * 2,
        compiler_params=pltpu.CompilerParams(vmem_limit_bytes=48 * 2**20),
        cost_estimate=pl.CostEstimate(
            flops=10 * row_len * 640 * width + 8 * row_len * width * full,
            bytes_accessed=14 * row_len * width + 8 * row_len * full,
            transcendentals=heads * row_len * 640,
        ),
        name="attend_backward",
    )(place, qkv, *grads, seg_row.reshape(row_len, 1), seg_row.reshape(1, row_len), weights)


def norm_parts(values):
    centre = values - jnp.mean(values, axis=-1, keepdims=True)
    inverse = lax.rsqrt(jnp.mean(centre * centre, axis=-1, keepdims=True) + norm_eps)
    return centre * inverse, inverse


def norm_back(normed, inverse, grad):
    return inverse * (
        grad
        - jnp.mean(grad, axis=-1, keepdims=True)
        - normed * jnp.mean(grad * normed, axis=-1, keepdims=True)
    )


def unit_rows(ref):
    return [(u, slice(u * UNIT, (u + 1) * UNIT)) for u in range(ref.shape[0] // UNIT)]


def column(values, index, width):
    return values[:, index * width : (index + 1) * width]


def open_kernel(place_ref, x_ref, tab_ref, add_ref, w_ref, a_ref, qkv_ref):
    width = x_ref.shape[1]
    for u, at in unit_rows(x_ref):
        normed, _ = norm_parts(x_ref[at, :].astype(wide))
        table = tab_ref[0, u : u + 1, :]
        a_ref[at, :] = (normed * (1.0 + column(table, 1, width)) + column(table, 0, width)).astype(low)
    qkv = dot_as(a_ref[...], w_ref[:, : qkv_ref.shape[1]], DOT_NN)
    for u, at in unit_rows(x_ref):
        qkv_ref[at, :] = (qkv[at, :] + add_ref[0, u : u + 1, :]).astype(low)


def first_kernel(place_ref, x_ref, kept_ref, got_ref, passed_ref, bias_ref, tab_ref, att_ref, hid_ref, a_ref):
    width = x_ref.shape[1]
    for u, at in unit_rows(x_ref):
        table = tab_ref[0, u : u + 1, :]
        attended = kept_ref[at, :] + got_ref[at, :].astype(wide) + passed_ref[at, :].astype(wide)
        attended = attended + bias_ref[0:1, :]
        hidden = x_ref[at, :].astype(wide) + column(table, 0, width) * attended
        normed, _ = norm_parts(hidden)
        att_ref[at, :] = attended
        hid_ref[at, :] = hidden
        a_ref[at, :] = (normed * (1.0 + column(table, 2, width)) + column(table, 1, width)).astype(low)


def down_back_kernel(place_ref, cot_ref, tab_ref, w_ref, grad_ref, dm_ref):
    width = cot_ref.shape[1]
    for u, at in unit_rows(cot_ref):
        table = tab_ref[0, u : u + 1, :]
        grad_ref[at, :] = (cot_ref[at, :].astype(wide) * column(table, 3, width)).astype(low)
    dm_ref[...] = dot_as(grad_ref[...], w_ref[:, w_ref.shape[1] // 2 :], DOT_NN).astype(low)


def gelu_both(values):
    scale = math.sqrt(2.0 / math.pi)
    square = values * values
    turned = jnp.tanh(scale * values * (1.0 + 0.044715 * square))
    upper = 0.5 * (1.0 + turned)
    slope = upper + 0.5 * values * (1.0 - turned * turned) * scale * (1.0 + 3 * 0.044715 * square)
    return values * upper, slope


def up_kernel(
    a0_ref, a1_ref, a2_ref, a3_ref, dm_ref, bias_ref, w_ref, m_ref, dz_ref, kept_ref, sent_ref, sums_ref, a_s
):
    step = pl.program_id(0)
    for j, piece in enumerate((a0_ref, a1_ref, a2_ref, a3_ref)):

        @pl.when(step == j)
        def _(piece=piece):
            a_s[...] = piece[...]

    w_up = w_ref[:, : w_ref.shape[1] // 2]
    inner = dot_as(a_s[...], w_up, DOT_NN) + bias_ref[...]
    active, slope = gelu_both(inner)
    m_ref[...] = active.astype(low)
    grad = (dm_ref[...].astype(wide) * slope).astype(low)
    dz_ref[...] = grad
    sums_ref[0] = jnp.sum(grad.astype(wide).reshape(-1, 8, grad.shape[1]), axis=0)
    back = dot_as(grad, w_up, DOT_NT)

    @pl.when(step < 2)
    def _():
        kept_ref[...] = back

    @pl.when(step >= 2)
    def _():
        sent_ref[...] = back.astype(low)


def down_kernel(m_ref, w_ref, kept_ref, sent_ref):
    step = pl.program_id(0)
    out = dot_as(m_ref[...], w_ref[:, w_ref.shape[1] // 2 :], DOT_NT)

    @pl.when(step < 2)
    def _():
        kept_ref[...] = out

    @pl.when(step >= 2)
    def _():
        sent_ref[...] = out.astype(low)


def second_kernel(
    place_ref, cot_ref, kept_ref, got_ref, passed_ref, hid_ref, att_ref, tab_ref, gh_ref, ga_ref, sums_ref
):
    width = cot_ref.shape[1]
    bias = jnp.zeros((1, width), wide)
    sums_ref[...] = jnp.zeros_like(sums_ref)
    for u, at in unit_rows(cot_ref):
        table = tab_ref[0, u : u + 1, :]
        grad_two = kept_ref[at, :] + got_ref[at, :].astype(wide) + passed_ref[at, :].astype(wide)
        normed, inverse = norm_parts(hid_ref[at, :])
        grad = cot_ref[at, :].astype(wide) + norm_back(
            normed, inverse, grad_two * (1.0 + column(table, 2, width))
        )
        grad_att = grad * column(table, 0, width)
        gh_ref[at, :] = grad
        ga_ref[at, :] = grad_att.astype(low)
        bias = bias + jnp.sum(grad_att, axis=0, keepdims=True)
        sums_ref[u : u + 1, :] = jnp.sum(grad * att_ref[at, :], axis=0, keepdims=True)
        sums_ref[4 + u : 5 + u, :] = jnp.sum(grad_two, axis=0, keepdims=True)
        sums_ref[8 + u : 9 + u, :] = jnp.sum(grad_two * normed, axis=0, keepdims=True)
    sums_ref[12:13, :] = bias


def out_kernel(
    place_ref, cot_ref, kept_ref, got_ref, passed_ref, hid_ref, bias_ref, tab_ref, out_ref, sums_ref
):
    width = cot_ref.shape[1]
    bias = jnp.zeros((1, width), wide)
    sums_ref[...] = jnp.zeros_like(sums_ref)
    for u, at in unit_rows(cot_ref):
        gate = column(tab_ref[0, u : u + 1, :], 3, width)
        mlp = kept_ref[at, :] + got_ref[at, :].astype(wide) + passed_ref[at, :].astype(wide)
        mlp = mlp + bias_ref[1:2, :]
        out_ref[at, :] = (hid_ref[at, :] + gate * mlp).astype(low)
        cot = cot_ref[at, :].astype(wide)
        sums_ref[u : u + 1, :] = jnp.sum(cot * mlp, axis=0, keepdims=True)
        bias = bias + jnp.sum(cot, axis=0, keepdims=True) * gate
    sums_ref[4:5, :] = bias


def third_kernel(place_ref, x_ref, kept_ref, got_ref, passed_ref, gh_ref, tab_ref, out_ref, sums_ref):
    width = x_ref.shape[1]
    for u, at in unit_rows(x_ref):
        grad_one = kept_ref[at, :] + got_ref[at, :].astype(wide) + passed_ref[at, :].astype(wide)
        normed, inverse = norm_parts(x_ref[at, :].astype(wide))
        table = tab_ref[0, u : u + 1, :]
        back = norm_back(normed, inverse, grad_one * (1.0 + column(table, 1, width)))
        out_ref[at, :] = (gh_ref[at, :] + back).astype(low)
        sums_ref[u : u + 1, :] = jnp.sum(grad_one, axis=0, keepdims=True)
        sums_ref[4 + u : 5 + u, :] = jnp.sum(grad_one * normed, axis=0, keepdims=True)


def row_call(body, name, place, args, in_specs, out_specs, out_shape, grid=1, scratch=(), flops=0):
    moved = sum(math.prod(a.shape) * a.dtype.itemsize for a in args)
    moved += sum(math.prod(o.shape) * o.dtype.itemsize for o in out_shape)
    prefetch = () if place is None else (place,)
    return pl.pallas_call(
        body,
        grid_spec=pltpu.PrefetchScalarGridSpec(
            num_scalar_prefetch=len(prefetch),
            grid=(grid,),
            in_specs=in_specs,
            out_specs=out_specs,
            scratch_shapes=scratch,
        ),
        out_shape=out_shape,
        compiler_params=pltpu.CompilerParams(vmem_limit_bytes=44 * 2**20),
        cost_estimate=pl.CostEstimate(flops=flops, bytes_accessed=moved, transcendentals=0),
        name=name,
    )(*prefetch, *args)


def block_spec(shape, index):
    return pl.BlockSpec(shape, index)


def fixed_spec(shape):
    return pl.BlockSpec(shape, lambda *_: (0,) * len(shape))


def weight_grad(pairs, name):
    depth = pairs[0][0][0][0].shape[1]
    tile = depth // 3
    widths = [pair[0][1].shape[1] for pair in pairs]
    args, specs, plan = [], [], []
    flops = 0
    for pair in pairs:
        rows = []
        for left, right in pair:
            rows.append((len(args), len(left)))
            args += list(left) + [right]
            specs += [pl.BlockSpec((piece.shape[0], tile), lambda i: (0, i)) for piece in left]
            specs.append(fixed_spec(right.shape))
            flops += 2 * depth * math.prod(right.shape)
        plan.append(rows)

    def body(*refs):
        out_ref = refs[-1]
        at = 0
        for rows, cols in zip(plan, widths):
            total = None
            for first, count in rows:
                left = [ref[...] for ref in refs[first : first + count]]
                left = left[0] if count == 1 else jnp.concatenate(left, axis=0)
                part = dot_as(left, refs[first + count][...], DOT_TN)
                total = part if total is None else total + part
            out_ref[:, at : at + cols] = total.astype(low)
            at += cols

    return pl.pallas_call(
        body,
        grid=(3,),
        in_specs=specs,
        out_specs=pl.BlockSpec((tile, sum(widths)), lambda i: (i, 0)),
        out_shape=shape_of((depth, sum(widths)), low),
        compiler_params=pltpu.CompilerParams(vmem_limit_bytes=52 * 2**20),
        cost_estimate=pl.CostEstimate(
            flops=flops,
            bytes_accessed=sum(2 * math.prod(a.shape) for a in args) + 2 * depth * sum(widths),
            transcendentals=0,
        ),
        name=name,
    )(*args)


def widen_pieces(place, pieces, rows):
    quarter, width = pieces[0].shape

    def body(place_ref, *refs):
        step = pl.program_id(0)
        for i, piece in enumerate(refs[:-1]):

            @pl.when(step == i)
            def _(piece=piece):
                refs[-1][...] = piece[...].astype(wide)

    return row_call(
        body,
        "widen_pieces",
        place,
        pieces,
        [fixed_spec((quarter, width))] * len(pieces),
        (
            pl.BlockSpec(
                (quarter, width), lambda i, p: (i // 4 * 4 + jnp.bitwise_xor(p[0], i % 4), 0)
            ),
        ),
        (shape_of((len(pieces) * quarter, width), wide),),
        grid=len(pieces),
    )[0]


def place_pieces(at, pieces):
    rows = sum(piece.shape[0] for piece in pieces)
    whole = (rows,) + pieces[0].shape[1:]
    return pl.pallas_call(
        place_kernel,
        out_shape=jax.ShapeDtypeStruct(whole, pieces[0].dtype),
        in_specs=[SMEM_SPEC] + [VMEM_SPEC] * len(pieces),
        out_specs=pl.BlockSpec(memory_space=pl.ANY),
        scratch_shapes=[pltpu.SemaphoreType.DMA((len(pieces),))],
        compiler_params=pltpu.CompilerParams(vmem_limit_bytes=24 * 2**20),
        cost_estimate=pl.CostEstimate(
            flops=0, bytes_accessed=4 * math.prod(whole), transcendentals=0
        ),
        name="place_pieces",
    )(at, *pieces)


def adam_step(weight, gradient, first_old, second_old, ema_old, step_rate):
    first_new = beta_one * first_old + (1.0 - beta_one) * gradient
    second_new = beta_two * second_old + (1.0 - beta_two) * gradient * gradient
    first_hat = first_new / (1.0 - beta_one**STEP)
    second_hat = second_new / (1.0 - beta_two**STEP)
    weight_new = weight - step_rate * (
        first_hat / (jnp.sqrt(second_hat) + adam_eps) + decay_rate * weight
    )
    ema_new = ema_keep * ema_old + (1.0 - ema_keep) * weight_new
    return (first_new, second_new, weight_new, ema_new)


def after(value, *others):
    return lax.optimization_barrier((value,) + others)[0]


def per_device(
    tokens,
    seg_ids,
    time_steps,
    cotangent,
    weight_cols,
    weight_rows,
    bias_cols,
    bias_rows,
    first_cols,
    first_rows,
    first_bias_cols,
    first_bias_rows,
    second_cols,
    second_rows,
    second_bias_cols,
    second_bias_rows,
    ema_cols,
    ema_rows,
    ema_bias_cols,
    ema_bias_rows,
):
    own_width = weight_cols.shape[2]
    own_depth = weight_cols.shape[1]
    width = tokens.shape[1]
    rows = time_steps.shape[0]
    slots = time_steps.shape[1]
    token_count = tokens.shape[0]
    row_len = token_count // rows
    units = row_len // UNIT
    quarter = row_len // 4
    own_units = units // 4
    dp_count = width // own_depth
    dp_place = lax.axis_index("dp")
    mp_place = lax.axis_index("mp")
    core, chip = mp_place % 2, mp_place // 2
    place = (2 * core + chip).astype(jnp.int32)
    place_arg = place.reshape(1)

    steps_all = share_steps(time_steps, dp_count).reshape(-1)
    cols_low = weight_cols.astype(low)
    own_rows = weight_rows.astype(low).transpose(2, 0, 1).reshape(own_depth, 5 * own_width)
    own_first = jnp.concatenate([cols_low[0], cols_low[1], cols_low[2], own_rows[:, :own_width]], 1)
    own_rest = jnp.concatenate([cols_low[5 + i] for i in range(4)] + [own_rows[:, own_width:]], 1)
    w_first = ring_gather(own_first, dp_count)
    w_rest = ring_gather(after(own_rest, w_first), dp_count)

    half_width = width // 2
    feature = dp_place * own_depth + jnp.arange(own_depth)
    is_cos = feature < half_width
    index = jnp.where(is_cos, feature, feature - half_width).astype(wide)
    frequency = jnp.exp(-math.log(10000.0) * index / half_width)
    angles = steps_all.astype(wide)[:, None] * frequency[None, :]
    time_rows = jnp.where(is_cos[None, :], jnp.cos(angles), jnp.sin(angles))
    time_low = time_rows.astype(low)
    ada_low = jax.nn.silu(time_rows).astype(low)

    def slot_products(left, maps):
        flat = jnp.concatenate([maps[j] for j in range(maps.shape[0])], 1)
        return dot_as(left, flat, DOT_NN).astype(low)

    def spread_columns(own, biases):
        count = biases.shape[0]
        own = (own.reshape(-1, count, own_width) + biases[None]).astype(low)
        pieces = group_gather(own)
        pieces = [pieces[0], pieces[2], pieces[1], pieces[3]]
        return jnp.concatenate(in_group_order(pieces, mp_place), 2).astype(wide)

    near = jnp.concatenate(
        [slot_products(ada_low, cols_low[9:11]), slot_products(time_low, cols_low[3:5])], 1
    )
    near = ring_scatter(near, dp_count, split=False)
    far = slot_products(after(ada_low, near), cols_low[11:15])
    far = ring_scatter(far, dp_count, split=False)
    near_mod = spread_columns(near[:, : 2 * own_width], bias_cols[6:8])
    far_mod = spread_columns(far, bias_cols[8:12])
    time_add = jnp.concatenate(
        [
            near[:, 2 * own_width : 3 * own_width] + bias_cols[0],
            jnp.zeros((rows * slots, own_width), wide),
            near[:, 3 * own_width :] + bias_cols[1],
        ],
        1,
    )

    seg_grid = seg_ids.reshape(rows, row_len)
    unit_seg = seg_grid.reshape(rows, 4, own_units, UNIT)[:, :, :, 0]
    unit_seg = jnp.stack(
        [lax.dynamic_index_in_dim(unit_seg, jnp.bitwise_xor(place, j), 1, keepdims=False) for j in range(4)],
        1,
    ).reshape(rows, units)
    onehot = (unit_seg[:, :, None] == jnp.arange(slots, dtype=jnp.int32)).astype(wide)

    def by_unit(table):
        out = jnp.einsum("rus,rsx->rux", onehot, table.reshape(rows, slots, -1), precision=highest)
        return out.reshape(rows, 4, own_units, out.shape[-1])

    near_tab, far_tab, add_tab = by_unit(near_mod), by_unit(far_mod), by_unit(time_add)

    block = (quarter, width)
    tab_block = lambda tab, j: pl.BlockSpec((1,) + tab.shape[2:], j)
    qkv_width = 3 * own_width
    half = row_len // 2
    lows = lambda *shape: shape_of(shape, low)
    wides = lambda *shape: shape_of(shape, wide)

    def own_block(r):
        return pl.BlockSpec(block, lambda i, p: (r * 4 + p[0], 0))

    def moved_block(r):
        return pl.BlockSpec(block, lambda i, p: (r * 4 + jnp.bitwise_xor(p[0], i), 0))

    here = pl.BlockSpec(block, lambda i, p: (0, 0))
    step_block = pl.BlockSpec(block, lambda i, p: (i, 0))

    inputs_one, qkvs, mixed, parts = [], [], [], []
    for r in range(rows):
        a_one, qkv = row_call(
            open_kernel,
            "open_row",
            place_arg,
            (tokens, near_tab[r], add_tab[r], w_first),
            [
                moved_block(r),
                tab_block(near_tab, lambda i, p: (i, 0, 0)),
                tab_block(add_tab, lambda i, p: (i, 0, 0)),
                fixed_spec(w_first.shape),
            ],
            (step_block, pl.BlockSpec((quarter, qkv_width), lambda i, p: (i, 0))),
            (lows(row_len, width), lows(row_len, qkv_width)),
            grid=4,
            flops=2 * row_len * width * qkv_width,
        )
        inputs_one.append(a_one)
        qkvs.append(qkv)
        out, kept, sent = attend_forward(place_arg, qkv, seg_grid[r], w_first)
        mixed.append(out)
        parts.append(group_scatter(kept, sent))

    down_grads = []
    for r in range(rows):
        down_grads.append(
            row_call(
                down_back_kernel,
                "down_back",
                place_arg,
                (cotangent, far_tab[r], w_rest),
                [moved_block(r), tab_block(far_tab, lambda i, p: (i, 0, 0)), fixed_spec(w_rest.shape)],
                (step_block, step_block),
                (lows(row_len, width), lows(row_len, width)),
                grid=4,
                flops=2 * row_len * width * width,
            )
        )

    attendeds, hiddens, inputs_two = [], [], []
    for r in range(rows):
        attended, hidden, a_two = row_call(
            first_kernel,
            "first_norm",
            place_arg,
            (tokens, *parts[r], bias_rows, far_tab[r]),
            [own_block(r), here, here, here, fixed_spec(bias_rows.shape), tab_block(far_tab, lambda i, p: (0, 0, 0))],
            (here, here, here),
            (wides(*block), wides(*block), lows(*block)),
        )
        attendeds.append(attended)
        hiddens.append(hidden)
        inputs_two.append(group_gather(a_two))

    bias_up = bias_cols[2:6].reshape(1, -1)
    hidden_width = bias_up.shape[1]
    actives, inner_grads, up_parts, up_sums = [], [], [], 0.0
    for r in range(rows):
        active, inner_grad, kept, sent, sums = row_call(
            up_kernel,
            "up_and_back",
            None,
            (*inputs_two[r], down_grads[r][1], bias_up, w_rest),
            [fixed_spec(block)] * 4
            + [pl.BlockSpec(block, lambda i: (i, 0)), fixed_spec(bias_up.shape), fixed_spec(w_rest.shape)],
            (
                pl.BlockSpec((quarter, hidden_width), lambda i: (i, 0)),
                pl.BlockSpec((quarter, hidden_width), lambda i: (i, 0)),
                pl.BlockSpec(block, lambda i: (jnp.minimum(i, 1), 0)),
                pl.BlockSpec(block, lambda i: (jnp.maximum(i - 2, 0), 0)),
                pl.BlockSpec((1, 8, hidden_width), lambda i: (i, 0, 0)),
            ),
            (
                lows(row_len, hidden_width),
                lows(row_len, hidden_width),
                wides(half, width),
                lows(half, width),
                wides(4, 8, hidden_width),
            ),
            grid=4,
            scratch=[pltpu.VMEM(block, low)],
            flops=4 * row_len * width * hidden_width,
        )
        actives.append(active)
        inner_grads.append(inner_grad)
        up_parts.append(group_scatter(kept, sent))
        up_sums = up_sums + jnp.sum(sums, axis=(0, 1))

    grad_hiddens, grad_attendeds, second_sums = [], [], []
    for r in range(rows):
        grad_hidden, grad_attended, sums = row_call(
            second_kernel,
            "second_norm",
            place_arg,
            (cotangent, *up_parts[r], hiddens[r], attendeds[r], far_tab[r]),
            [own_block(r)] + [here] * 5 + [tab_block(far_tab, lambda i, p: (0, 0, 0))],
            (here, here, fixed_spec((16, width))),
            (wides(*block), lows(*block), wides(16, width)),
        )
        grad_hiddens.append(grad_hidden)
        grad_attendeds.append(group_gather(grad_attended))
        second_sums.append(sums)

    out_pieces, out_sums = [], []
    for r in range(rows):
        kept, sent = row_call(
            down_kernel,
            "down",
            None,
            (actives[r], w_rest),
            [pl.BlockSpec((quarter, hidden_width), lambda i: (i, 0)), fixed_spec(w_rest.shape)],
            (
                pl.BlockSpec(block, lambda i: (jnp.minimum(i, 1), 0)),
                pl.BlockSpec(block, lambda i: (jnp.maximum(i - 2, 0), 0)),
            ),
            (wides(half, width), lows(half, width)),
            grid=4,
            flops=2 * row_len * width * hidden_width,
        )
        out_own, sums = row_call(
            out_kernel,
            "out_tokens",
            place_arg,
            (cotangent, *group_scatter(kept, sent), hiddens[r], bias_rows, far_tab[r]),
            [own_block(r)] + [here] * 4 + [fixed_spec(bias_rows.shape), tab_block(far_tab, lambda i, p: (0, 0, 0))],
            (here, fixed_spec((8, width))),
            (lows(*block), wides(8, width)),
        )
        out_pieces.extend(group_gather(out_own))
        out_sums.append(sums)

    rest_grad = weight_grad(
        [
            [(inputs_two[r], inner_grads[r]) for r in range(rows)],
            [([down_grads[r][0]], actives[r]) for r in range(rows)],
        ],
        "grad_rest",
    )
    rest_sum = lax.psum_scatter(rest_grad, "dp", scatter_dimension=0, tiled=True).astype(wide)

    qkv_grads, one_parts, time_sums = [], [], []
    for r in range(rows):
        qkv_grad, kept, sent, sums = attend_backward(
            place_arg, qkvs[r], grad_attendeds[r], seg_grid[r], w_first
        )
        qkv_grads.append(qkv_grad)
        one_parts.append(group_scatter(kept, sent))
        time_sums.append(sums)
    first_grad = weight_grad(
        [
            [([inputs_one[r]], qkv_grads[r]) for r in range(rows)],
            [(grad_attendeds[r], mixed[r]) for r in range(rows)],
        ],
        "grad_first",
    )
    first_sum = ring_scatter(first_grad, dp_count)

    input_pieces, third_sums = [], []
    for r in range(rows):
        input_own, sums = row_call(
            third_kernel,
            "third_norm",
            place_arg,
            (tokens, *one_parts[r], grad_hiddens[r], near_tab[r]),
            [own_block(r)] + [here] * 4 + [tab_block(near_tab, lambda i, p: (0, 0, 0))],
            (here, fixed_spec((8, width))),
            (lows(*block), wides(8, width)),
        )
        input_pieces.extend(group_gather(input_own))
        third_sums.append(sums)

    at = jnp.stack(
        [(r * 4 + jnp.bitwise_xor(place, j)) * quarter for r in range(rows) for j in range(4)]
    ).astype(jnp.int32)
    out_tokens = place_pieces(at, out_pieces)
    input_grads = widen_pieces(place_arg, input_pieces, rows)

    def side(values, which, axis):
        return lax.dynamic_index_in_dim(values, which, axis, keepdims=False)

    def exchange(values):
        values = values.astype(low).reshape(-1, 2, 2, own_width)
        other = lax.ppermute(side(values, 1 - chip, 1), "mp", CHIP_SWAP)
        values = jnp.stack([side(values, chip, 1), other], 0)
        other = lax.ppermute(side(values, 1 - core, 2), "mp", CORE_SWAP)
        values = jnp.stack([side(values, core, 2), other], 0)
        return values.reshape(4, -1, own_width).astype(wide)

    def to_slots(fields):
        fields = fields.reshape(rows, units, -1)
        return jnp.einsum("rus,rux->rsx", onehot, fields, precision=highest).reshape(rows * slots, -1)

    count = 4 * own_units
    far_rows = jnp.stack(
        [jnp.concatenate([second_sums[r][:12], out_sums[r][:4]], 0) for r in range(rows)], 0
    )
    bias_part = jnp.stack(
        [sum(second_sums[r][12] for r in range(rows)), sum(out_sums[r][4] for r in range(rows))], 0
    )
    swapped = exchange(jnp.concatenate([far_rows.reshape(rows * count, width), bias_part], 0))
    far_fields = swapped[:, : rows * count].reshape(4, rows, 4, own_units, own_width)
    far_fields = far_fields.transpose(1, 0, 3, 2, 4)
    bias_part = jnp.sum(swapped[:, rows * count :], axis=0)
    extra = jnp.zeros((16, 4 * own_width), wide).at[0].set(up_sums)
    extra = extra.at[1, : 2 * own_width].set(bias_part.reshape(-1))
    far_all = ring_gather(jnp.concatenate([to_slots(far_fields), extra], 0).astype(low), dp_count)
    far_all = far_all.reshape(dp_count, rows * slots + 16, 4 * own_width)
    extra = jnp.sum(far_all[:, rows * slots :].astype(wide), axis=0)
    far_all = far_all[:, : rows * slots].reshape(-1, 4 * own_width)
    bias_up_sum = extra[0].reshape(4, own_width)
    bias_rows_own = group_gather(extra[1, : 2 * own_width].reshape(2, own_width).astype(low))
    bias_rows_own = [bias_rows_own[0], bias_rows_own[2], bias_rows_own[1], bias_rows_own[3]]
    bias_rows_sum = jnp.concatenate(in_group_order(bias_rows_own, mp_place), 1).astype(wide)

    near_rows = jnp.stack(third_sums, 0)
    near_fields = exchange(near_rows.reshape(rows * 2 * own_units, width))
    near_fields = near_fields.reshape(4, rows, 2, own_units, own_width).transpose(1, 0, 3, 2, 4)
    time_fields = jnp.stack(time_sums, 0).reshape(rows, units, 3, own_width)[:, :, 0::2]
    near_slots = jnp.concatenate([to_slots(near_fields), to_slots(time_fields)], 1).astype(low)
    near_all = ring_gather(near_slots, dp_count)

    def map_grads(left, right):
        out = dot_as(left, right, DOT_TN).reshape(own_depth, -1, own_width)
        return out.transpose(1, 0, 2)

    far_sum = jnp.sum(far_all.astype(wide), axis=0).reshape(4, own_width)
    near_sum = jnp.sum(near_all.astype(wide), axis=0).reshape(4, own_width)

    def slabs(values):
        return values.reshape(own_depth, -1, own_width).transpose(1, 0, 2)

    grad_cols = jnp.concatenate(
        [
            slabs(first_sum[:, :qkv_width]),
            map_grads(time_low, near_all[:, 2 * own_width :]),
            slabs(rest_sum[:, : 4 * own_width]),
            map_grads(ada_low, near_all[:, : 2 * own_width]),
            map_grads(ada_low, far_all),
        ],
        0,
    )
    rows_sum = jnp.concatenate([first_sum[:, qkv_width:], rest_sum[:, 4 * own_width :]], 1)
    grad_rows = rows_sum.reshape(own_depth, 5, own_width).transpose(1, 2, 0)
    bias_cols_sum = jnp.concatenate([near_sum[2:4], bias_up_sum, near_sum[:2], far_sum], 0)

    cols_state = adam_step(weight_cols, grad_cols, first_cols, second_cols, ema_cols, rate_matrix)
    rows_state = adam_step(weight_rows, grad_rows, first_rows, second_rows, ema_rows, rate_matrix)
    bias_cols_state = adam_step(
        bias_cols, bias_cols_sum, first_bias_cols, second_bias_cols, ema_bias_cols, rate_vector
    )
    bias_rows_state = adam_step(
        bias_rows, bias_rows_sum, first_bias_rows, second_bias_rows, ema_bias_rows, rate_vector
    )
    return (out_tokens, input_grads) + cols_state + rows_state + bias_cols_state + bias_rows_state


def solution(mesh):
    cols, rows, bias = P(None, "dp", "mp"), P(None, "mp", "dp"), P(None, "mp")
    state = (cols, rows, bias, P())
    placed = (P("dp", None), P("dp"), P("dp", None), P("dp", None)) + state * 4
    given = (P("dp", None), P("dp", None)) + (cols,) * 4 + (rows,) * 4 + (bias,) * 4 + (P(),) * 4
    return jax.shard_map(
        per_device, mesh=mesh, in_specs=placed, out_specs=given, check_vma=False
    )
```

```python
import math

import jax
import jax.numpy as jnp
from jax import lax
from jax.experimental import pallas as pl
from jax.experimental.pallas import tpu as pltpu
from jax.sharding import PartitionSpec as P

HEAD_DIM = 72
STEP = 10
UNIT = 64
REACH = 192


highest = lax.Precision.HIGHEST
beta_one = 0.9
beta_two = 0.999
adam_eps = 1e-08
decay_rate = 0.1
rate_matrix = 0.05
rate_vector = 0.5
ema_keep = 0.7
norm_eps = 1e-06
neg_large = -1e30
score_scale = HEAD_DIM**-0.5
low = jnp.bfloat16
wide = jnp.float32

DOT_NN = (((1,), (0,)), ((), ()))
DOT_NT = (((1,), (1,)), ((), ()))
DOT_TN = (((0,), (0,)), ((), ()))

COST = 10
VMEM_GRANT = 58 * 2**20
SMEM_SPEC = pl.BlockSpec(memory_space=pltpu.SMEM)

CORE_SWAP = [(i, i ^ 1) for i in range(4)]
CHIP_SWAP = [(i, i ^ 2) for i in range(4)]


def dot_as(left, right, dims):
    return lax.dot_general(left, right, dims, preferred_element_type=wide)


def ring_order(count):
    return list(range(0, count, 2)) + list(range(count - 1, 0, -2))


def ring_perms(count):
    order = ring_order(count)
    onward = [(order[i], order[(i + 1) % count]) for i in range(count)]
    return onward, [(b, a) for a, b in onward]


def ring_place(count):
    order = ring_order(count)
    spots = [order.index(i) for i in range(count)]
    return jnp.array(order), jnp.array(spots)[lax.axis_index("dp")]


def ring_start(shard, count):
    onward, backward = ring_perms(count)
    return lax.ppermute(shard, "dp", onward), lax.ppermute(shard, "dp", backward)


def ring_finish(ahead, behind, count):
    onward, backward = ring_perms(count)
    cut = ahead.shape[0] // 32 * 16
    return lax.ppermute(ahead[:cut], "dp", onward), lax.ppermute(behind[cut:], "dp", backward)


def ring_places(rows, count):
    order, spot = ring_place(count)
    at = [order[spot] * rows]
    for hop in range(1, count // 2):
        at += [order[(spot - hop) % count] * rows, order[(spot + hop) % count] * rows]
    far = order[(spot + count // 2) % count] * rows
    return jnp.stack(at + [far, far + rows // 32 * 16]).astype(jnp.int32)


def place_kernel(at_ref, *refs):
    pieces, (out_ref, held, sem_in, sem_out) = refs[:-4], refs[-4:]
    arrive, leave = [], []
    base = 0
    for i, piece in enumerate(pieces):
        count = piece.shape[0]
        spot = held.at[pl.ds(base, count)]
        arrive.append(pltpu.make_async_copy(piece, spot, sem_in.at[i]))
        to = out_ref.at[pl.ds(pl.multiple_of(at_ref[i], 16), count)]
        leave.append(pltpu.make_async_copy(spot, to, sem_out.at[i]))
        base += count
    for copy in arrive:
        copy.start()
    for first, second in zip(arrive, leave):
        first.wait()
        second.start()
    for copy in leave:
        copy.wait()


def place_pieces(at, pieces):
    whole = (sum(piece.shape[0] for piece in pieces),) + pieces[0].shape[1:]
    return pl.pallas_call(
        place_kernel,
        out_shape=jax.ShapeDtypeStruct(whole, pieces[0].dtype),
        in_specs=[SMEM_SPEC] + [pl.BlockSpec(memory_space=pl.ANY)] * len(pieces),
        out_specs=pl.BlockSpec(memory_space=pl.ANY),
        scratch_shapes=[pltpu.VMEM(whole, pieces[0].dtype)]
        + [pltpu.SemaphoreType.DMA((len(pieces),))] * 2,
        compiler_params=pltpu.CompilerParams(vmem_limit_bytes=VMEM_GRANT),
        cost_estimate=pl.CostEstimate(
            flops=0, bytes_accessed=4 * COST * math.prod(whole), transcendentals=0
        ),
        name="place_pieces",
    )(at, *pieces)


class RingSum:
    def __init__(self, parts, count):
        self.parts, self.rows = parts, parts.shape[0] // count
        self.onward, self.backward = ring_perms(count)
        self.order, self.spot = ring_place(count)
        self.count, self.left = count, count // 2 - 1
        self.send(self.chunk(count // 2), self.chunk(1 - count // 2))

    def chunk(self, ahead):
        at = self.order[(self.spot + ahead) % self.count] * self.rows
        return lax.dynamic_slice_in_dim(self.parts, at, self.rows, 0).astype(wide)

    def send(self, ahead, behind):
        self.ahead = lax.ppermute(ahead.astype(low), "dp", self.onward)
        if behind is not None:
            self.behind = lax.ppermute(behind.astype(low), "dp", self.backward)

    def hop(self, token):
        if not self.left:
            return token
        token, ahead, behind = lax.optimization_barrier((token, self.ahead, self.behind))
        self.behind = behind
        ahead = ahead.astype(wide) + self.chunk(self.left)
        if self.left > 1:
            behind = behind.astype(wide) + self.chunk(1 - self.left)
        else:
            behind = None
        self.send(ahead, behind)
        self.left -= 1
        return token

    def total(self):
        return self.ahead.astype(wide) + self.behind.astype(wide) + self.chunk(0)


def halving_hop(parts, step, count):
    pairs = parts.reshape((parts.shape[0] // 2, 2) + parts.shape[1:])
    bit = lax.axis_index("dp") // step % 2
    sent = lax.dynamic_index_in_dim(pairs, 1 - bit, 1, keepdims=False).astype(low)
    kept = lax.dynamic_index_in_dim(pairs, bit, 1, keepdims=False).astype(wide)
    got = lax.ppermute(sent, "dp", [(i, i ^ step) for i in range(count)])
    return kept + got.astype(wide)


def doubling_gather(shard, count, between):
    if count not in (4, 8):
        return lax.all_gather(shard, "dp", axis=0, tiled=True)
    spot = lax.axis_index("dp")
    known = shard[None]
    step = count // 2
    while step:
        known = lax.optimization_barrier((known, between[0]))[0]
        between = between[1:]
        got = lax.ppermute(known, "dp", [(i, i ^ step) for i in range(count)])
        second = spot // step % 2 == 1
        known = jnp.stack([jnp.where(second, got, known), jnp.where(second, known, got)], 1)
        known = known.reshape((-1,) + shard.shape)
        step //= 2
    return known.reshape((-1,) + shard.shape[1:])


def share_hop(known, reach, count):
    return known + lax.ppermute(known, "dp", [(i, i ^ reach) for i in range(count)])


def group_scatter(kept, sent):
    quarter = kept.shape[0] // 2
    got = lax.ppermute(sent, "mp", CORE_SWAP)
    passed = (kept[quarter:] + got[quarter:].astype(wide)).astype(low)
    return (kept, got, lax.ppermute(passed, "mp", CHIP_SWAP)), passed


def group_gather(own, between=None):
    chip = lax.ppermute(own, "mp", CHIP_SWAP)
    if between is not None:
        chip = lax.optimization_barrier((chip, between))[0]
    core = lax.ppermute(own, "mp", CORE_SWAP)
    both = lax.ppermute(chip, "mp", CORE_SWAP)
    return [own, chip, core, both]


def in_group_order(pieces, place):
    stacked = jnp.stack(pieces, 0)
    return [
        lax.dynamic_index_in_dim(stacked, jnp.bitwise_xor(place, j), 0, keepdims=False)
        for j in range(4)
    ]


def key_windows(row_len, block):
    return [
        (at, max(0, at - REACH), min(row_len, at + block + REACH))
        for at in range(0, row_len, block)
    ]


def relative_at(place, j, block):
    return pl.multiple_of(jnp.bitwise_xor(place, j) * block, block)


def attend_forward_kernel(
    place_ref, qkv_ref, seg_col_ref, seg_row_ref, w_ref, out_ref, kept_ref, sent_ref, q_s, k_s, v_s, *, heads
):
    row_len = qkv_ref.shape[0]
    width = heads * HEAD_DIM
    block = row_len // 4
    place = place_ref[0]
    for j in range(4):
        at = relative_at(place, j, block)
        to = slice(j * block, (j + 1) * block)
        for h in range(heads):
            c = h * HEAD_DIM
            q_s[h, to, :] = qkv_ref[pl.ds(at, block), c : c + HEAD_DIM]
            k_s[h, to, :] = qkv_ref[pl.ds(at, block), width + c : width + c + HEAD_DIM]
            v_s[h, to, :] = qkv_ref[pl.ds(at, block), 2 * width + c : 2 * width + c + HEAD_DIM]
    for j, (at, start, stop) in enumerate(key_windows(row_len, block)):
        same = seg_col_ref[start:stop, :] == seg_row_ref[:, at : at + block]
        mixed = []
        for h in range(heads):
            scores = dot_as(k_s[h, start:stop, :], q_s[h, at : at + block, :], DOT_NT)
            scores = jnp.where(same, scores, neg_large)
            top = jnp.max(scores, axis=0, keepdims=True)
            weights = jnp.exp((scores - top) * score_scale)
            total = jnp.sum(weights, axis=0, keepdims=True)
            gathered = dot_as(v_s[h, start:stop, :], weights.astype(low), DOT_TN)
            mixed.append(gathered * (1.0 / total))
        out_ref[pl.ds(relative_at(place, j, block), block), :] = (
            jnp.concatenate(mixed, axis=0).T.astype(low)
        )
    w_out = w_ref[:, 3 * width :]
    half = row_len // 2
    kept_ref[...] = dot_as(out_ref[:half, :], w_out, DOT_NT)
    sent_ref[...] = dot_as(out_ref[half:, :], w_out, DOT_NT).astype(low)


def attend_backward_kernel(
    place_ref, qkv_ref, g0_ref, g1_ref, g2_ref, g3_ref, seg_col_ref, seg_row_ref, w_ref,
    out_ref, kept_ref, sent_ref, sums_ref, q_s, k_s, v_s, g_s, dk_s, dv_s, *, heads
):
    row_len = qkv_ref.shape[0]
    width = heads * HEAD_DIM
    block = row_len // 4
    place = place_ref[0]
    dk_s[...] = jnp.zeros_like(dk_s)
    dv_s[...] = jnp.zeros_like(dv_s)
    w_out = w_ref[:, 3 * width :]
    for j, g_ref in enumerate((g0_ref, g1_ref, g2_ref, g3_ref)):
        grad = dot_as(g_ref[...], w_out, DOT_NN).astype(low)
        at = relative_at(place, j, block)
        for h in range(heads):
            g_s[h, pl.ds(at, block), :] = grad[:, h * HEAD_DIM : (h + 1) * HEAD_DIM]
    for j in range(4):
        at = relative_at(place, j, block)
        to = slice(j * block, (j + 1) * block)
        for h in range(heads):
            c = h * HEAD_DIM
            q_s[h, to, :] = qkv_ref[pl.ds(at, block), c : c + HEAD_DIM]
            k_s[h, to, :] = qkv_ref[pl.ds(at, block), width + c : width + c + HEAD_DIM]
            v_s[h, to, :] = qkv_ref[pl.ds(at, block), 2 * width + c : 2 * width + c + HEAD_DIM]
    for j, (at, start, stop) in enumerate(key_windows(row_len, block)):
        same = seg_col_ref[start:stop, :] == seg_row_ref[:, at : at + block]
        grads = []
        for h in range(heads):
            query = q_s[h, at : at + block, :]
            grad = g_s[h, at : at + block, :]
            keys = k_s[h, start:stop, :]
            scores = jnp.where(same, dot_as(keys, query, DOT_NT), neg_large)
            top = jnp.max(scores, axis=0, keepdims=True)
            weights = jnp.exp((scores - top) * score_scale)
            probs = weights * (1.0 / jnp.sum(weights, axis=0, keepdims=True))
            grad_probs = dot_as(v_s[h, start:stop, :], grad, DOT_NT)
            inner = jnp.sum(grad_probs * probs, axis=0, keepdims=True)
            grad_scores = (probs * (grad_probs - inner)).astype(low)
            dv_s[h, start:stop, :] += dot_as(probs.astype(low), grad, DOT_NN)
            dk_s[h, start:stop, :] += dot_as(grad_scores, query, DOT_NN)
            grads.append(dot_as(keys, grad_scores, DOT_TN) * score_scale)
        out_ref[pl.ds(relative_at(place, j, block), block), 0:width] = (
            jnp.concatenate(grads, axis=0).T.astype(low)
        )
    for j in range(4):
        at = slice(j * block, (j + 1) * block)
        to = relative_at(place, j, block)
        out_ref[pl.ds(to, block), width : 2 * width] = jnp.concatenate(
            [(dk_s[h, at, :] * score_scale).astype(low) for h in range(heads)], axis=1
        )
        out_ref[pl.ds(to, block), 2 * width : 3 * width] = jnp.concatenate(
            [dv_s[h, at, :].astype(low) for h in range(heads)], axis=1
        )
    half = row_len // 2
    w_qkv = w_ref[:, : 3 * width]
    kept_ref[...] = dot_as(out_ref[:half, :], w_qkv, DOT_NT)
    sent_ref[...] = dot_as(out_ref[half:, :], w_qkv, DOT_NT).astype(low)
    for u in range(row_len // UNIT):
        sums_ref[u : u + 1, :] = jnp.sum(
            out_ref[u * UNIT : (u + 1) * UNIT, :].astype(wide), axis=0, keepdims=True
        )


def shape_of(shape, kind):
    return jax.ShapeDtypeStruct(shape, kind)


def attend_forward(place, qkv, seg_row, weights):
    row_len, width = qkv.shape[0], qkv.shape[1] // 3
    heads = width // HEAD_DIM
    full = weights.shape[0]
    args = (qkv, seg_row.reshape(row_len, 1), seg_row.reshape(1, row_len), weights)
    shapes = (
        shape_of((row_len, width), low),
        shape_of((row_len // 2, full), wide),
        shape_of((row_len // 2, full), low),
    )

    def body(*refs):
        attend_forward_kernel(*refs, heads=heads)

    return row_call(
        body,
        "attend_forward",
        place,
        args,
        [fixed_spec(arg.shape) for arg in args],
        tuple(fixed_spec(shape.shape) for shape in shapes),
        shapes,
        scratch=[pltpu.VMEM((heads, row_len, HEAD_DIM), low)] * 3,
        flops=4 * row_len * 640 * width + 2 * row_len * width * full,
        exps=heads * row_len * 640,
    )


def attend_backward(place, qkv, grads, seg_row, weights):
    row_len, width = qkv.shape[0], qkv.shape[1] // 3
    heads = width // HEAD_DIM
    full = weights.shape[0]
    args = (qkv, *grads, seg_row.reshape(row_len, 1), seg_row.reshape(1, row_len), weights)
    shapes = (
        shape_of((row_len, 3 * width), low),
        shape_of((row_len // 2, full), wide),
        shape_of((row_len // 2, full), low),
        shape_of((row_len // UNIT, 3 * width), wide),
    )

    def body(*refs):
        attend_backward_kernel(*refs, heads=heads)

    return row_call(
        body,
        "attend_backward",
        place,
        args,
        [fixed_spec(arg.shape) for arg in args],
        tuple(fixed_spec(shape.shape) for shape in shapes),
        shapes,
        scratch=[pltpu.VMEM((heads, row_len, HEAD_DIM), low)] * 4
        + [pltpu.VMEM((heads, row_len, HEAD_DIM), wide)] * 2,
        flops=10 * row_len * 640 * width + 8 * row_len * width * full,
        exps=heads * row_len * 640,
    )


def norm_parts(values):
    centre = values - jnp.mean(values, axis=-1, keepdims=True)
    inverse = lax.rsqrt(jnp.mean(centre * centre, axis=-1, keepdims=True) + norm_eps)
    return centre * inverse, inverse


def norm_back(normed, inverse, grad):
    return inverse * (
        grad
        - jnp.mean(grad, axis=-1, keepdims=True)
        - normed * jnp.mean(grad * normed, axis=-1, keepdims=True)
    )


def unit_rows(ref):
    return [(u, slice(u * UNIT, (u + 1) * UNIT)) for u in range(ref.shape[0] // UNIT)]


def column(values, index, width):
    return values[:, index * width : (index + 1) * width]


def open_kernel(
    place_ref, x0_ref, x1_ref, tab0_ref, tab1_ref, add0_ref, add1_ref, w_ref, a_ref, qkv_ref
):
    width = x0_ref.shape[1]
    quarter = x0_ref.shape[0]
    for j, (x_ref, tab_ref) in enumerate(((x0_ref, tab0_ref), (x1_ref, tab1_ref))):
        for u, at in unit_rows(x_ref):
            normed, _ = norm_parts(x_ref[at, :].astype(wide))
            table = tab_ref[0, u : u + 1, :]
            out = normed * (1.0 + column(table, 1, width)) + column(table, 0, width)
            a_ref[j * quarter + u * UNIT : j * quarter + (u + 1) * UNIT, :] = out.astype(low)
    qkv = dot_as(a_ref[...], w_ref[:, : qkv_ref.shape[1]], DOT_NN)
    for j, add_ref in enumerate((add0_ref, add1_ref)):
        for u in range(quarter // UNIT):
            at = slice(j * quarter + u * UNIT, j * quarter + (u + 1) * UNIT)
            qkv_ref[at, :] = (qkv[at, :] + add_ref[0, u : u + 1, :]).astype(low)


def first_kernel(place_ref, x_ref, kept_ref, got_ref, passed_ref, bias_ref, tab_ref, att_ref, hid_ref, a_ref):
    width = x_ref.shape[1]
    for u, at in unit_rows(x_ref):
        table = tab_ref[0, u : u + 1, :]
        attended = kept_ref[at, :] + got_ref[at, :].astype(wide) + passed_ref[at, :].astype(wide)
        attended = attended + bias_ref[0:1, :]
        hidden = x_ref[at, :].astype(wide) + column(table, 0, width) * attended
        normed, _ = norm_parts(hidden)
        att_ref[at, :] = attended
        hid_ref[at, :] = hidden
        a_ref[at, :] = (normed * (1.0 + column(table, 2, width)) + column(table, 1, width)).astype(low)


def down_back_kernel(place_ref, cot0_ref, cot1_ref, tab0_ref, tab1_ref, w_ref, grad_ref, dm_ref):
    width = cot0_ref.shape[1]
    quarter = cot0_ref.shape[0]
    for j, (cot_ref, tab_ref) in enumerate(((cot0_ref, tab0_ref), (cot1_ref, tab1_ref))):
        for u, at in unit_rows(cot_ref):
            gate = column(tab_ref[0, u : u + 1, :], 3, width)
            out = (cot_ref[at, :].astype(wide) * gate).astype(low)
            grad_ref[j * quarter + u * UNIT : j * quarter + (u + 1) * UNIT, :] = out
    dm_ref[...] = dot_as(grad_ref[...], w_ref[...], DOT_NN).astype(low)


def gelu_both(values):
    scale = math.sqrt(2.0 / math.pi)
    square = values * values
    turned = jnp.tanh(scale * values * (1.0 + 0.044715 * square))
    upper = 0.5 * (1.0 + turned)
    slope = upper + 0.5 * values * (1.0 - turned * turned) * scale * (1.0 + 3 * 0.044715 * square)
    return values * upper, slope


def up_kernel(
    place_ref, a0_ref, a1_ref, a2_ref, a3_ref, dm_ref, bias_ref, w_ref, m_ref, dz_ref, kept_ref, sent_ref, sums_ref, a_s
):
    step = pl.program_id(0)
    quarter = a0_ref.shape[0]
    for j, piece in enumerate((a0_ref, a1_ref, a2_ref, a3_ref)):

        @pl.when(step == j // 2)
        def _(piece=piece, j=j):
            a_s[j % 2 * quarter : (j % 2 + 1) * quarter, :] = piece[...]

    sums = jnp.zeros(sums_ref.shape[1:], wide)
    for j in range(2):
        at = slice(j * quarter, (j + 1) * quarter)
        inner = dot_as(a_s[at, :], w_ref[...], DOT_NN) + bias_ref[...]
        active, slope = gelu_both(inner)
        m_ref[at, :] = active.astype(low)
        grad = (dm_ref[at, :].astype(wide) * slope).astype(low)
        dz_ref[at, :] = grad
        sums = sums + jnp.sum(grad.astype(wide).reshape(-1, 8, grad.shape[1]), axis=0)
    sums_ref[0] = sums
    back = dot_as(dz_ref[...], w_ref[...], DOT_NT)

    @pl.when(step == 0)
    def _():
        kept_ref[...] = back

    @pl.when(step == 1)
    def _():
        sent_ref[...] = back.astype(low)


def down_kernel(place_ref, m_ref, w_ref, kept_ref, sent_ref):
    step = pl.program_id(0)
    out = dot_as(m_ref[...], w_ref[...], DOT_NT)

    @pl.when(step == 0)
    def _():
        kept_ref[...] = out

    @pl.when(step == 1)
    def _():
        sent_ref[...] = out.astype(low)


def second_kernel(
    place_ref, cot_ref, kept_ref, got_ref, passed_ref, hid_ref, att_ref, tab_ref, gh_ref, ga_ref, sums_ref
):
    width = cot_ref.shape[1]
    bias = jnp.zeros((1, width), wide)
    sums_ref[...] = jnp.zeros_like(sums_ref)
    for u, at in unit_rows(cot_ref):
        table = tab_ref[0, u : u + 1, :]
        grad_two = kept_ref[at, :] + got_ref[at, :].astype(wide) + passed_ref[at, :].astype(wide)
        normed, inverse = norm_parts(hid_ref[at, :])
        grad = cot_ref[at, :].astype(wide) + norm_back(
            normed, inverse, grad_two * (1.0 + column(table, 2, width))
        )
        grad_att = grad * column(table, 0, width)
        gh_ref[at, :] = grad
        ga_ref[at, :] = grad_att.astype(low)
        bias = bias + jnp.sum(grad_att, axis=0, keepdims=True)
        sums_ref[u : u + 1, :] = jnp.sum(grad * att_ref[at, :], axis=0, keepdims=True)
        sums_ref[4 + u : 5 + u, :] = jnp.sum(grad_two, axis=0, keepdims=True)
        sums_ref[8 + u : 9 + u, :] = jnp.sum(grad_two * normed, axis=0, keepdims=True)
    sums_ref[12:13, :] = bias


def out_kernel(
    place_ref, cot_ref, kept_ref, got_ref, passed_ref, hid_ref, bias_ref, tab_ref, out_ref, sums_ref
):
    width = cot_ref.shape[1]
    bias = jnp.zeros((1, width), wide)
    sums_ref[...] = jnp.zeros_like(sums_ref)
    for u, at in unit_rows(cot_ref):
        gate = column(tab_ref[0, u : u + 1, :], 3, width)
        mlp = kept_ref[at, :] + got_ref[at, :].astype(wide) + passed_ref[at, :].astype(wide)
        mlp = mlp + bias_ref[1:2, :]
        out_ref[at, :] = (hid_ref[at, :] + gate * mlp).astype(low)
        cot = cot_ref[at, :].astype(wide)
        sums_ref[u : u + 1, :] = jnp.sum(cot * mlp, axis=0, keepdims=True)
        bias = bias + jnp.sum(cot, axis=0, keepdims=True) * gate
    sums_ref[4:5, :] = bias


def third_kernel(place_ref, x_ref, kept_ref, got_ref, passed_ref, gh_ref, tab_ref, out_ref, sums_ref):
    width = x_ref.shape[1]
    for u, at in unit_rows(x_ref):
        grad_one = kept_ref[at, :] + got_ref[at, :].astype(wide) + passed_ref[at, :].astype(wide)
        normed, inverse = norm_parts(x_ref[at, :].astype(wide))
        table = tab_ref[0, u : u + 1, :]
        back = norm_back(normed, inverse, grad_one * (1.0 + column(table, 1, width)))
        out_ref[at, :] = (gh_ref[at, :] + back).astype(low)
        sums_ref[u : u + 1, :] = jnp.sum(grad_one, axis=0, keepdims=True)
        sums_ref[4 + u : 5 + u, :] = jnp.sum(grad_one * normed, axis=0, keepdims=True)


def row_call(body, name, place, args, in_specs, out_specs, out_shape, grid=1, scratch=(), flops=0, exps=0, aliases=None):
    moved = sum(math.prod(a.shape) * a.dtype.itemsize for a in args)
    shapes = out_shape if isinstance(out_shape, tuple) else (out_shape,)
    moved += sum(math.prod(o.shape) * o.dtype.itemsize for o in shapes)
    return pl.pallas_call(
        body,
        grid_spec=pltpu.PrefetchScalarGridSpec(
            num_scalar_prefetch=1,
            grid=(grid,),
            in_specs=in_specs,
            out_specs=out_specs,
            scratch_shapes=scratch,
        ),
        out_shape=out_shape,
        input_output_aliases=aliases or {},
        compiler_params=pltpu.CompilerParams(vmem_limit_bytes=VMEM_GRANT),
        cost_estimate=pl.CostEstimate(
            flops=COST * flops, bytes_accessed=COST * moved, transcendentals=COST * exps
        ),
        name=name,
    )(place, *args)


def block_spec(shape, index):
    return pl.BlockSpec(shape, index)


def fixed_spec(shape):
    return pl.BlockSpec(shape, lambda *_: (0,) * len(shape))


def unit_tables(mp_arg, onehot, pieces, fields):
    units, slots = onehot.shape
    own = pieces[0].shape[1]

    def body(mp_ref, hot_ref, *refs):
        out_ref = refs[-1]
        mp_place = mp_ref[0]
        for i, piece in enumerate(refs[:-1]):
            for j in range(4):

                @pl.when(jnp.bitwise_xor(mp_place, i) == j)
                def _(piece=piece, j=j):
                    for f in range(fields):
                        at = f * 4 * own + j * own
                        out_ref[:, at : at + own] = dot_as(
                            hot_ref[...], piece[f * slots : (f + 1) * slots, :], DOT_NN
                        )

    return row_call(
        body,
        "unit_tables",
        mp_arg,
        (onehot, *pieces),
        [fixed_spec(onehot.shape)] + [fixed_spec(pieces[0].shape)] * 4,
        fixed_spec((units, fields * 4 * own)),
        shape_of((units, fields * 4 * own), wide),
        flops=8 * units * slots * own * fields,
    )


def weight_grad(place, pairs, name):
    depth = pairs[0][0][0][0].shape[1]
    tile = depth // 3
    widths = [pair[0][1].shape[1] for pair in pairs]
    args, specs, plan = [], [], []
    flops = 0
    for pair in pairs:
        rows = []
        for left, right in pair:
            rows.append((len(args), len(left)))
            args += list(left) + [right]
            specs += [pl.BlockSpec((piece.shape[0], tile), lambda i, p: (0, i)) for piece in left]
            specs.append(fixed_spec(right.shape))
            flops += 2 * depth * math.prod(right.shape)
        plan.append(rows)

    def body(place_ref, *refs):
        out_ref = refs[-1]
        at = 0
        for rows, cols in zip(plan, widths):
            total = None
            for first, count in rows:
                left = [ref[...] for ref in refs[first : first + count]]
                left = left[0] if count == 1 else jnp.concatenate(left, axis=0)
                part = dot_as(left, refs[first + count][...], DOT_TN)
                total = part if total is None else total + part
            out_ref[:, at : at + cols] = total.astype(low)
            at += cols

    return row_call(
        body,
        name,
        place,
        args,
        specs,
        pl.BlockSpec((tile, sum(widths)), lambda i, p: (i, 0)),
        shape_of((depth, sum(widths)), low),
        grid=3,
        flops=flops,
    )


def widen_row(place, pieces, row, rows, before):
    quarter, width = pieces[0].shape

    def body(place_ref, *refs):
        step = pl.program_id(0)
        for i, piece in enumerate(refs[:4]):

            @pl.when(step == i)
            def _(piece=piece):
                refs[-1][...] = piece[...].astype(wide)

    return row_call(
        body,
        "widen_row",
        place,
        tuple(pieces) + before,
        [fixed_spec((quarter, width))] * 4 + [pl.BlockSpec(memory_space=pl.ANY)] * len(before),
        pl.BlockSpec((quarter, width), lambda i, p: (row * 4 + jnp.bitwise_xor(p[0], i), 0)),
        shape_of((rows * 4 * quarter, width), wide),
        grid=4,
        aliases={5: 0} if before else None,
    )


def adam_step(weight, gradient, first_old, second_old, ema_old, step_rate):
    first_new = beta_one * first_old + (1.0 - beta_one) * gradient
    second_new = beta_two * second_old + (1.0 - beta_two) * gradient * gradient
    first_hat = first_new * (1.0 / (1.0 - beta_one**STEP))
    second_hat = second_new * (1.0 / (1.0 - beta_two**STEP))
    weight_new = weight - step_rate * (
        first_hat / (jnp.sqrt(second_hat) + adam_eps) + decay_rate * weight
    )
    ema_new = ema_keep * ema_old + (1.0 - ema_keep) * weight_new
    return (first_new, second_new, weight_new, ema_new)


def adam_slabs(token, plan, grads, make_grad, groups, before, name):
    slab = groups[0][0].shape[1:]
    count, held = len(plan), 4 * len(groups)
    turns = [[i for i, (which, _) in enumerate(plan) if which == g] for g in range(len(groups))]
    ids = [plan[max([i for i in mine if i <= n], default=mine[0])][1] for mine in turns for n in range(count)]
    ids = lax.optimization_barrier((jnp.array(ids, jnp.int32), token))[0]

    def block(group):
        return pl.BlockSpec((1,) + slab, lambda i, ids: (ids[group * count + i], 0, 0))

    def body(ids_ref, *refs):
        grad_refs, state_refs = refs[: len(grads)], refs[len(grads) : len(grads) + held]
        out_refs, grad_s = refs[-held - 1 : -1], refs[-1]
        step = pl.program_id(0)
        for n in range(count):

            @pl.when(step == n)
            def _(n=n):
                grad_s[...] = make_grad(n, grad_refs)

        for group, mine in enumerate(turns):

            @pl.when((step >= mine[0]) & (step <= mine[-1]))
            def _(group=group):
                weight, *old = [ref[0] for ref in state_refs[4 * group : 4 * group + 4]]
                new = adam_step(weight, grad_s[...], *old, rate_matrix)
                for ref, value in zip(out_refs[4 * group : 4 * group + 4], new):
                    ref[0] = value

    flat = [x for group in groups for x in group]
    specs = [block(g) for g in range(len(groups)) for _ in range(4)]
    kept, aliases = [], {}
    for g, arrays in enumerate(before):
        for i, x in enumerate(arrays or ()):
            aliases[1 + len(grads) + held + len(kept)] = 4 * g + i
            kept.append(x)
    return row_call(
        body,
        name,
        ids,
        (*grads, *flat, *kept),
        [fixed_spec(grad.shape) for grad in grads]
        + specs
        + [pl.BlockSpec(memory_space=pl.ANY)] * len(kept),
        tuple(specs),
        tuple(shape_of(x.shape, wide) for x in flat),
        grid=count,
        scratch=[pltpu.VMEM(slab, wide)],
        aliases=aliases,
    )


def per_device(
    tokens,
    seg_ids,
    time_steps,
    cotangent,
    weight_cols,
    weight_rows,
    bias_cols,
    bias_rows,
    first_cols,
    first_rows,
    first_bias_cols,
    first_bias_rows,
    second_cols,
    second_rows,
    second_bias_cols,
    second_bias_rows,
    ema_cols,
    ema_rows,
    ema_bias_cols,
    ema_bias_rows,
):
    own_width = weight_cols.shape[2]
    own_depth = weight_cols.shape[1]
    width = tokens.shape[1]
    rows = time_steps.shape[0]
    slots = time_steps.shape[1]
    token_count = tokens.shape[0]
    row_len = token_count // rows
    units = row_len // UNIT
    quarter = row_len // 4
    own_units = units // 4
    dp_count = width // own_depth
    dp_place = lax.axis_index("dp")
    slot_count = rows * slots
    mp_place = lax.axis_index("mp")
    core, chip = mp_place % 2, mp_place // 2
    place = (2 * core + chip).astype(jnp.int32)
    place_arg = place.reshape(1)

    def tied(*others):
        return lax.optimization_barrier((place_arg,) + others)[0]

    ring = dp_count in (4, 8)
    cols_low = weight_cols.astype(low)
    own_rows = weight_rows.astype(low).transpose(2, 0, 1).reshape(own_depth, 5 * own_width)
    own_first = jnp.concatenate([cols_low[0], cols_low[1], cols_low[2], own_rows[:, :own_width]], 1)
    own_rest = jnp.concatenate([cols_low[5 + i] for i in range(4)] + [own_rows[:, own_width:]], 1)

    half_width = width // 2
    feature = dp_place * own_depth + jnp.arange(own_depth)
    is_cos = feature < half_width
    index = jnp.where(is_cos, feature, feature - half_width).astype(wide)
    frequency = jnp.exp(-math.log(10000.0) * index / half_width)

    def embed(steps):
        angles = steps.astype(wide)[:, None] * frequency[None, :]
        table = jnp.where(is_cos[None, :], jnp.cos(angles), jnp.sin(angles))
        return table.astype(low), jax.nn.silu(table).astype(low)

    def slot_products(left, maps):
        out = jnp.stack([dot_as(left, maps[j], DOT_NN).astype(low) for j in range(maps.shape[0])], 0)
        return out.reshape(-1, dp_count, rows * slots, own_width).transpose(1, 0, 2, 3)

    def near_products(time_low, ada_low):
        return jnp.concatenate(
            [slot_products(ada_low, cols_low[9:11]), slot_products(time_low, cols_low[3:5])], 1
        )

    if ring:
        known = jnp.zeros((dp_count,) + time_steps.shape, time_steps.dtype)
        known = lax.dynamic_update_slice_in_dim(known, time_steps[None], dp_place, 0)
        onward, backward = ring_perms(dp_count)
        ahead, behind = ring_start(own_first, dp_count)
        pieces = [own_first, ahead, behind]
        known = share_hop(known, 1, dp_count)
        known = share_hop(known, 2, dp_count)
        known, ahead, behind = lax.optimization_barrier((known, ahead, behind))
        if dp_count == 8:
            ahead = lax.ppermute(ahead, "dp", onward)
            behind = lax.ppermute(behind, "dp", backward)
            pieces += [ahead, behind]
            known = share_hop(known, 4, dp_count)
        time_low, ada_low = embed(known.reshape(-1))
        near = near_products(time_low, ada_low)
        near, ahead, behind = lax.optimization_barrier((near, ahead, behind))
        if dp_count == 8:
            ahead = lax.ppermute(ahead, "dp", onward)
            behind = lax.ppermute(behind, "dp", backward)
            pieces += [ahead, behind]
        near = halving_hop(near, 1, dp_count)
        near = halving_hop(near, 2, dp_count)
        near, ahead, behind, own_rest = lax.optimization_barrier((near, ahead, behind, own_rest))
        pieces += ring_finish(ahead, behind, dp_count)
        rest_pieces = [own_rest, *ring_start(own_rest, dp_count)]
        if dp_count == 8:
            near = halving_hop(near, 4, dp_count)
        near = near[0]
        w_first = place_pieces(ring_places(own_depth, dp_count), pieces)
    else:
        w_first = lax.all_gather(own_first, "dp", axis=0, tiled=True)
        rest_pieces = [lax.all_gather(own_rest, "dp", axis=0, tiled=True)]
        time_low, ada_low = embed(lax.all_gather(time_steps, "dp", axis=0, tiled=True).reshape(-1))
        near = near_products(time_low, ada_low)
        near = lax.psum_scatter(near, "dp", scatter_dimension=0, tiled=True)[0].astype(wide)

    seg_grid = seg_ids.reshape(rows, row_len)
    unit_seg = seg_grid.reshape(rows, units, UNIT)[:, :, 0]
    onehot = unit_seg[:, :, None] == jnp.arange(slots, dtype=jnp.int32)
    blocks = onehot[:, :, None, :] & (jnp.arange(rows)[:, None] == jnp.arange(rows))[:, None, :, None]
    blocks = blocks.reshape(rows * units, rows * slots)
    mp_arg = mp_place.astype(jnp.int32).reshape(1)

    def tables(own, biases):
        fields = own.shape[0]
        own = (own + biases[:, None, :]).astype(low).reshape(-1, own_width)
        pieces = group_gather(own)
        pieces = [pieces[0], pieces[2], pieces[1], pieces[3]]
        out = unit_tables(mp_arg, blocks.astype(low), pieces, fields)
        return out.reshape(rows, 4, own_units, fields * width)

    far = [slot_products(lax.optimization_barrier((ada_low, near))[0], cols_low[11:15])]

    def far_hop(token):
        if not ring:
            return token
        token, held = lax.optimization_barrier((token, far[-1]))
        if held.shape[0] > 1:
            far.append(halving_hop(held, dp_count // held.shape[0], dp_count))
        return token

    near_tab = tables(near[:2], bias_cols[6:8])
    time_add = jnp.concatenate(
        [near[2] + bias_cols[0], jnp.zeros((rows * slots, own_width), wide), near[3] + bias_cols[1]], 1
    )
    add_tab = jnp.dot(blocks.astype(wide), time_add, precision=highest)
    add_tab = add_tab.reshape(rows, 4, own_units, 3 * own_width)

    block, half_block = (quarter, width), (row_len // 2, width)
    qkv_width = 3 * own_width
    half = row_len // 2
    lows = lambda *shape: shape_of(shape, low)
    wides = lambda *shape: shape_of(shape, wide)

    def own_block(r):
        return pl.BlockSpec(block, lambda i, p: (r * 4 + p[0], 0))

    def moved_blocks(r):
        return [
            pl.BlockSpec(block, lambda i, p: (r * 4 + jnp.bitwise_xor(p[0], 2 * i), 0)),
            pl.BlockSpec(block, lambda i, p: (r * 4 + jnp.bitwise_xor(p[0], 2 * i + 1), 0)),
        ]

    def moved_tables(tab):
        shape = (1,) + tab.shape[2:]
        return [
            pl.BlockSpec(shape, lambda i, p: (jnp.bitwise_xor(p[0], 2 * i), 0, 0)),
            pl.BlockSpec(shape, lambda i, p: (jnp.bitwise_xor(p[0], 2 * i + 1), 0, 0)),
        ]

    def own_table(tab):
        return pl.BlockSpec((1,) + tab.shape[2:], lambda i, p: (p[0], 0, 0))

    here = fixed_spec(block)
    half_step = pl.BlockSpec(half_block, lambda i, p: (i, 0))
    half_fixed = fixed_spec(half_block)

    def open_row(r, token):
        return row_call(
            open_kernel,
            "open_row",
            token,
            (tokens, tokens, near_tab[r], near_tab[r], add_tab[r], add_tab[r], w_first),
            moved_blocks(r) + moved_tables(near_tab) + moved_tables(add_tab) + [fixed_spec(w_first.shape)],
            (half_step, pl.BlockSpec((half, qkv_width), lambda i, p: (i, 0))),
            (lows(row_len, width), lows(row_len, qkv_width)),
            grid=2,
            flops=2 * row_len * width * qkv_width,
        )

    def rest_hop(token):
        if not ring:
            return token
        token, ahead, behind = lax.optimization_barrier((token, *rest_pieces[-2:]))
        hops = (len(rest_pieces) - 1) // 2
        if hops < dp_count // 2 - 1:
            rest_pieces.append(lax.ppermute(ahead, "dp", onward))
            rest_pieces.append(lax.ppermute(behind, "dp", backward))
        elif hops < dp_count // 2:
            rest_pieces.extend(ring_finish(ahead, behind, dp_count))
        return token

    inputs_one, qkvs, mixed, parts = [], [], [], []
    token = rest_hop(far_hop(place_arg))
    for r in range(rows):
        a_one, qkv = open_row(r, token)
        token = far_hop(tied(qkv, *[part[1] for part in parts]))
        inputs_one.append(a_one)
        qkvs.append(qkv)
        out, kept, sent = attend_forward(token, qkv, seg_grid[r], w_first)
        token = rest_hop(tied(sent))
        if r == 0:
            token = far_hop(token)
        mixed.append(out)
        parts.append(group_scatter(kept, sent))
    far = far[-1] if ring else lax.psum_scatter(
        far[0].reshape(-1, own_width), "dp", scatter_dimension=0, tiled=True
    )
    far = far.astype(wide).reshape(4, rows * slots, own_width)
    far_tab = tables(far, bias_cols[8:12])

    attendeds, hiddens, inputs_two, down_grads = [], [], [], []

    def first_norm(r, token):
        attended, hidden, a_two = row_call(
            first_kernel,
            "first_norm",
            token,
            (tokens, *parts[r][0], bias_rows, far_tab[r]),
            [own_block(r), here, here, here, fixed_spec(bias_rows.shape), own_table(far_tab)],
            (here, here, here),
            (wides(*block), wides(*block), lows(*block)),
        )
        attendeds.append(attended)
        hiddens.append(hidden)
        inputs_two.append(group_gather(a_two))
        return tied(a_two)

    def down_back(r, token):
        grads = row_call(
            down_back_kernel,
            "down_back",
            token,
            (cotangent, cotangent, far_tab[r], far_tab[r], w_rest),
            moved_blocks(r) + moved_tables(far_tab) + [w_down_spec],
            (half_step, half_step),
            (lows(row_len, width), lows(row_len, width)),
            grid=2,
            flops=2 * row_len * width * width,
        )
        down_grads.append(grads)
        return tied(grads[1])

    token = first_norm(0, token)
    token = tied(inputs_two[0][0], *[part[1] for part in parts[1:]])
    w_rest = place_pieces(ring_places(own_depth, dp_count), rest_pieces) if ring else rest_pieces[0]
    w_down_spec = pl.BlockSpec((width, w_rest.shape[1] // 2), lambda i, p: (0, 1))
    w_up_spec = pl.BlockSpec((width, w_rest.shape[1] // 2), lambda i, p: (0, 0))
    for r in range(rows):
        token = down_back(r, token)
    for r in range(1, rows):
        token = first_norm(r, token)

    bias_up = bias_cols[2:6].reshape(1, -1)
    hidden_width = bias_up.shape[1]
    actives, inner_grads, up_parts, up_sums, down_parts = [], [], [], 0.0, []
    for r in range(rows):
        active, inner_grad, kept, sent, sums = row_call(
            up_kernel,
            "up_and_back",
            token,
            (*inputs_two[r], down_grads[r][1], bias_up, w_rest),
            [here] * 4 + [half_step, fixed_spec(bias_up.shape), w_up_spec],
            (
                pl.BlockSpec((half, hidden_width), lambda i, p: (i, 0)),
                pl.BlockSpec((half, hidden_width), lambda i, p: (i, 0)),
                half_fixed,
                half_fixed,
                pl.BlockSpec((1, 8, hidden_width), lambda i, p: (i, 0, 0)),
            ),
            (
                lows(row_len, hidden_width),
                lows(row_len, hidden_width),
                wides(half, width),
                lows(half, width),
                wides(2, 8, hidden_width),
            ),
            grid=2,
            scratch=[pltpu.VMEM(half_block, low)],
            flops=4 * row_len * width * hidden_width,
        )
        token = tied(sent, *[x for part in up_parts for x in part[0][2:]], *[part[1] for part in down_parts])
        actives.append(active)
        inner_grads.append(inner_grad)
        up_parts.append(group_scatter(kept, sent))
        up_sums = up_sums + jnp.sum(sums, axis=(0, 1))
        kept, sent = row_call(
            down_kernel,
            "down",
            token,
            (active, w_rest),
            [pl.BlockSpec((half, hidden_width), lambda i, p: (i, 0)), w_down_spec],
            (half_fixed, half_fixed),
            (wides(half, width), lows(half, width)),
            grid=2,
            flops=2 * row_len * width * hidden_width,
        )
        token = tied(sent, up_parts[-1][1], *[part[0][2] for part in down_parts])
        down_parts.append(group_scatter(kept, sent))

    grad_hiddens, grad_attendeds, second_sums = [], [], []

    def second_norm(r, token):
        grad_hidden, grad_attended, sums = row_call(
            second_kernel,
            "second_norm",
            token,
            (cotangent, *up_parts[r][0], hiddens[r], attendeds[r], far_tab[r]),
            [own_block(r)] + [here] * 5 + [own_table(far_tab)],
            (here, here, fixed_spec((16, width))),
            (wides(*block), lows(*block), wides(16, width)),
        )
        grad_hiddens.append(grad_hidden)
        grad_attendeds.append(grad_attended)
        second_sums.append(sums)
        return tied(grad_attended)

    token = second_norm(0, token)
    rest_grad = weight_grad(
        token,
        [
            [(inputs_two[r], inner_grads[r]) for r in range(rows)],
            [([down_grads[r][0]], actives[r]) for r in range(rows)],
        ],
        "grad_rest",
    )
    rest_ring = RingSum(rest_grad, dp_count) if ring else None
    token = tied(rest_grad, down_parts[-1][1])
    grad_attendeds[0] = group_gather(grad_attendeds[0], token)
    for r in range(1, rows):
        token = second_norm(r, token)
        grad_attendeds[r] = group_gather(grad_attendeds[r])

    out_pieces, out_sums = [], []

    def out_row(r, token):
        out_own, sums = row_call(
            out_kernel,
            "out_tokens",
            token,
            (cotangent, *down_parts[r][0], hiddens[r], bias_rows, far_tab[r]),
            [own_block(r)] + [here] * 4 + [fixed_spec(bias_rows.shape), own_table(far_tab)],
            (here, fixed_spec((8, width))),
            (lows(*block), wides(8, width)),
        )
        out_pieces.extend(group_gather(out_own))
        out_sums.append(sums)
        return tied(out_own)

    qkv_grads, one_parts, time_sums = [], [], []
    for r in range(rows):
        qkv_grad, kept, sent, sums = attend_backward(
            token, qkvs[r], grad_attendeds[r], seg_grid[r], w_first
        )
        token = tied(sent)
        if ring:
            token = rest_ring.hop(token)
        qkv_grads.append(qkv_grad)
        one_parts.append(group_scatter(kept, sent))
        time_sums.append(sums)
        if r == 0:
            for n in range(rows):
                token = out_row(n, token)
            token = tied(token, one_parts[0][1])

    def exchange(values, between):
        values = values.astype(low)

        def part(held, which, columns):
            return lax.dynamic_slice_in_dim(held, which * columns, columns, 1)

        other = lax.ppermute(part(values, 1 - chip, 2 * own_width), "mp", CHIP_SWAP)
        values = jnp.concatenate([part(values, chip, 2 * own_width), other], 0)
        values = lax.optimization_barrier((values, between))[0]
        other = lax.ppermute(part(values, 1 - core, own_width), "mp", CORE_SWAP)
        return jnp.concatenate([part(values, core, own_width), other], 0)

    by_place = jnp.stack(
        [
            lax.dynamic_index_in_dim(
                onehot.reshape(rows, 4, own_units, slots), jnp.bitwise_xor(place, j), 1, keepdims=False
            )
            for j in range(4)
        ],
        0,
    )

    def slot_matrix(fields, spare, kept_rows):
        same_row = jnp.eye(rows, dtype=bool)
        same_field = jnp.eye(fields, dtype=bool)
        full = (
            by_place.transpose(3, 0, 1, 2)[None, None, :, :, :, None, :]
            & same_row[None, :, None, None, :, None, None]
            & same_field[:, None, None, None, None, :, None]
        )
        full = full.reshape(fields * rows * slots, 4, rows * fields * own_units)
        full = jnp.pad(full, ((0, kept_rows), (0, 0), (0, spare)))
        if spare:
            extra = jnp.arange(spare)
            full = full.at[fields * rows * slots + extra, :, rows * fields * own_units + extra].set(True)
        return full.reshape(full.shape[0], -1).astype(low)

    far_rows = []
    for r in range(rows):
        far_rows += [second_sums[r][:12], out_sums[r][:4]]
    bias_part = [
        sum(second_sums[r][12:13] for r in range(rows)),
        sum(out_sums[r][4:5] for r in range(rows)),
    ]
    far_swapped = exchange(jnp.concatenate(far_rows + bias_part, 0), token)

    first_grad = weight_grad(
        token,
        [
            [([inputs_one[r]], qkv_grads[r]) for r in range(rows)],
            [(grad_attendeds[r], mixed[r]) for r in range(rows)],
        ],
        "grad_first",
    )
    ring_sum = RingSum(first_grad, dp_count) if ring else None
    token = tied(first_grad, one_parts[-1][1])
    after_first = token

    input_pieces, third_sums = [], []

    def third_norm(r, token):
        input_own, sums = row_call(
            third_kernel,
            "third_norm",
            token,
            (tokens, *one_parts[r][0], grad_hiddens[r], near_tab[r]),
            [own_block(r)] + [here] * 4 + [own_table(near_tab)],
            (here, fixed_spec((8, width))),
            (lows(*block), wides(8, width)),
        )
        input_pieces.append(group_gather(input_own))
        third_sums.append(sums)
        return tied(input_own)

    def ring_hop(token):
        return ring_sum.hop(token) if ring else token

    for r in range(rows - 1):
        token = third_norm(r, token)
    if ring:
        token = rest_ring.hop(token)
    after_third = token
    at = jnp.stack(
        [(r * 4 + jnp.bitwise_xor(place, j)) * quarter for r in range(rows) for j in range(4)]
    ).astype(jnp.int32)
    at = lax.optimization_barrier((at, token))[0]
    out_tokens = place_pieces(at, out_pieces)
    token = ring_hop(tied(out_tokens))
    after_place = token
    token = third_norm(rows - 1, token)

    far_slots = dot_as(slot_matrix(4, 2, 16), far_swapped, DOT_NN)
    far_slots = lax.dynamic_update_slice(
        far_slots, up_sums.reshape(4, own_width), (4 * slot_count + 2, 0)
    ).astype(low)
    far_all = doubling_gather(far_slots, dp_count, (after_first, after_third, after_place))
    far_all = far_all.reshape(dp_count, -1, own_width)
    far_sum = jnp.sum(far_all.astype(wide), axis=0)
    far_biases = jnp.sum(far_sum[: 4 * slot_count].reshape(4, slot_count, own_width), axis=1)
    bias_up_sum = far_sum[4 * slot_count + 2 : 4 * slot_count + 6]
    bias_rows_own = group_gather(far_sum[4 * slot_count : 4 * slot_count + 2].astype(low))
    bias_rows_own = [bias_rows_own[0], bias_rows_own[2], bias_rows_own[1], bias_rows_own[3]]
    bias_rows_sum = jnp.concatenate(in_group_order(bias_rows_own, mp_place), 1).astype(wide)

    def columns_of(ref, at):
        return column(ref[...], at, own_width).astype(wide)

    def map_grad(left, right, field):
        right = right[:, field * slot_count : (field + 1) * slot_count, :]
        return dot_as(left[...], right.reshape(-1, own_width), DOT_TN)

    cols_state = (weight_cols, first_cols, second_cols, ema_cols)
    rows_state = [x.transpose(0, 2, 1) for x in (weight_rows, first_rows, second_rows, ema_rows)]

    if ring:
        rest_sum = rest_ring.total()
    else:
        rest_sum = lax.psum_scatter(rest_grad, "dp", scatter_dimension=0, tiled=True)

    near_rows = jnp.concatenate(third_sums, 0)
    cols_new = adam_slabs(
        token,
        [(0, i) for i in (5, 6, 7, 8)],
        (rest_sum,),
        lambda n, refs: columns_of(refs[0], n),
        [cols_state],
        [None],
        "adam_up",
    )
    token = ring_hop(tied(cols_new[0]))
    near_swapped = exchange(near_rows, token)
    rows_new = adam_slabs(
        token,
        [(0, i) for i in (1, 2, 3, 4)],
        (rest_sum,),
        lambda n, refs: columns_of(refs[0], 4 + n),
        [rows_state],
        [None],
        "adam_down",
    )
    token = ring_hop(tied(rows_new[0]))
    after_down = token
    cols_new = adam_slabs(
        token,
        [(0, i) for i in (11, 12, 13, 14)],
        (ada_low, far_all),
        lambda n, refs: map_grad(refs[0], refs[1], n),
        [cols_state],
        [cols_new],
        "adam_far",
    )
    token = tied(cols_new[0])
    after_far = token
    input_grads = ()
    for r in range(rows):
        input_grads = (widen_row(token, input_pieces[r], r, rows, input_grads),)
        token = tied(input_grads[0])
        if r == 0:
            after_widen = token

    unit_sums = jnp.concatenate(time_sums, 0)
    moved = by_place.transpose(1, 0, 2, 3).reshape(rows, units, slots)
    moved = moved[:, :, None, :] & jnp.eye(rows, dtype=bool)[:, None, :, None]
    moved = moved.reshape(rows * units, slot_count).astype(wide)
    time_slots = lax.dot_general(moved, unit_sums, DOT_TN, precision=highest)
    near_slots = jnp.concatenate(
        [
            dot_as(slot_matrix(2, 0, 0), near_swapped, DOT_NN),
            time_slots[:, :own_width],
            time_slots[:, 2 * own_width :],
        ],
        0,
    ).astype(low)
    near_all = doubling_gather(near_slots, dp_count, (after_down, after_far, after_widen))
    near_all = near_all.reshape(dp_count, -1, own_width)
    near_sum = jnp.sum(near_all.astype(wide).reshape(dp_count, 4, slot_count, own_width), axis=(0, 2))
    bias_cols_sum = jnp.concatenate([near_sum[2:4], bias_up_sum, near_sum[:2], far_biases], 0)
    if ring:
        first_sum = ring_sum.total()
    else:
        first_sum = lax.psum_scatter(first_grad, "dp", scatter_dimension=0, tiled=True)

    def late_grad(n, refs):
        ada, time, near, first = refs
        if n < 4:
            return map_grad(ada if n < 2 else time, near, n)
        return columns_of(first, n - 4)

    new = adam_slabs(
        token,
        [(0, i) for i in (9, 10, 3, 4, 0, 1, 2)] + [(1, 0)],
        (ada_low, time_low, near_all, first_sum),
        late_grad,
        [cols_state, rows_state],
        [cols_new, rows_new],
        "adam_late",
    )
    cols_new, rows_new = new[:4], [x.transpose(0, 2, 1) for x in new[4:]]
    bias_cols_new = adam_step(
        bias_cols, bias_cols_sum, first_bias_cols, second_bias_cols, ema_bias_cols, rate_vector
    )
    bias_rows_new = adam_step(
        bias_rows, bias_rows_sum, first_bias_rows, second_bias_rows, ema_bias_rows, rate_vector
    )
    return (out_tokens, input_grads[0], *cols_new, *rows_new, *bias_cols_new, *bias_rows_new)


def solution(mesh):
    cols, rows, bias = P(None, "dp", "mp"), P(None, "mp", "dp"), P(None, "mp")
    state = (cols, rows, bias, P())
    placed = (P("dp", None), P("dp"), P("dp", None), P("dp", None)) + state * 4
    given = (P("dp", None), P("dp", None)) + (cols,) * 4 + (rows,) * 4 + (bias,) * 4 + (P(),) * 4
    return jax.shard_map(
        per_device, mesh=mesh, in_specs=placed, out_specs=given, check_vma=False
    )
```

```python
import math

import jax
import jax.numpy as jnp
from jax import lax
from jax.experimental import pallas as pl
from jax.experimental.pallas import tpu as pltpu
from jax.sharding import PartitionSpec as P

HEAD_DIM = 72
STEP = 10
UNIT = 64
REACH = 192


highest = lax.Precision.HIGHEST
beta_one = 0.9
beta_two = 0.999
adam_eps = 1e-08
decay_rate = 0.1
rate_matrix = 0.05
rate_vector = 0.5
ema_keep = 0.7
norm_eps = 1e-06
neg_large = -1e30
score_scale = HEAD_DIM**-0.5
low = jnp.bfloat16
wide = jnp.float32

DOT_NN = (((1,), (0,)), ((), ()))
DOT_NT = (((1,), (1,)), ((), ()))
DOT_TN = (((0,), (0,)), ((), ()))

COST = 0
VMEM_GRANT = 58 * 2**20
SMEM_SPEC = pl.BlockSpec(memory_space=pltpu.SMEM)

CORE_SWAP = [(i, i ^ 1) for i in range(4)]
CHIP_SWAP = [(i, i ^ 2) for i in range(4)]


def dot_as(left, right, dims):
    return lax.dot_general(left, right, dims, preferred_element_type=wide)


def ring_order(count):
    return list(range(0, count, 2)) + list(range(count - 1, 0, -2))


def ring_perms(count):
    order = ring_order(count)
    onward = [(order[i], order[(i + 1) % count]) for i in range(count)]
    return onward, [(b, a) for a, b in onward]


def ring_spot(count):
    me = lax.axis_index("dp")
    return jnp.where(me % 2 == 0, me // 2, count - 1 - me // 2)


def ring_at(spot, count):
    spot = spot % count
    return jnp.where(spot < count // 2, 2 * spot, 2 * (count - 1 - spot) + 1)


def ring_places(rows, count):
    spot = ring_spot(count)
    back = [0]
    for hop in range(1, count // 2):
        back += [-hop, hop]
    at = ring_at(spot + jnp.array(back + [count // 2] * 2), count) * rows
    return (at + jnp.array([0] * len(back) + [0, rows // 32 * 16])).astype(jnp.int32)


def place_kernel(at_ref, *refs):
    pieces, (out_ref, held, sem_in, sem_out) = refs[:-4], refs[-4:]
    arrive, leave = [], []
    base = 0
    for i, piece in enumerate(pieces):
        count = piece.shape[0]
        spot = held.at[pl.ds(base, count)]
        arrive.append(pltpu.make_async_copy(piece, spot, sem_in.at[i]))
        to = out_ref.at[pl.ds(pl.multiple_of(at_ref[i], 16), count)]
        leave.append(pltpu.make_async_copy(spot, to, sem_out.at[i]))
        base += count
    for copy in arrive:
        copy.start()
    for first, second in zip(arrive, leave):
        first.wait()
        second.start()
    for copy in leave:
        copy.wait()


def place_pieces(chain, at, pieces):
    whole = (sum(piece.shape[0] for piece in pieces),) + pieces[0].shape[1:]
    at = chain.tie(at)
    out = pl.pallas_call(
        place_kernel,
        out_shape=jax.ShapeDtypeStruct(whole, pieces[0].dtype),
        in_specs=[SMEM_SPEC] + [pl.BlockSpec(memory_space=pl.ANY)] * len(pieces),
        out_specs=pl.BlockSpec(memory_space=pl.ANY),
        scratch_shapes=[pltpu.VMEM(whole, pieces[0].dtype)]
        + [pltpu.SemaphoreType.DMA((len(pieces),))] * 2,
        compiler_params=pltpu.CompilerParams(vmem_limit_bytes=VMEM_GRANT),
        cost_estimate=pl.CostEstimate(
            flops=0, bytes_accessed=int(4 * COST * math.prod(whole)) + 1, transcendentals=0
        ),
        name="place_pieces",
    )(at, *pieces)
    return chain.close(out)


class Chain:
    def __init__(self, token):
        self.token = token

        self.landing = []

    def tie(self, *arrays):
        self.token, *arrays = lax.optimization_barrier((self.token, *arrays))
        return arrays[0] if len(arrays) == 1 else tuple(arrays)

    def land(self, *transfers):
        self.landing += transfers

    def close(self, *arrays):
        landing, self.landing = self.landing, []
        values = self.tie(*arrays, *[getattr(held, name) for held, name in landing])
        values = values if isinstance(values, tuple) else (values,)
        for (held, name), value in zip(landing, values[len(arrays) :]):
            setattr(held, name, value)
        return values[0] if len(arrays) == 1 else values[: len(arrays)]


class RingSum:
    def __init__(self, parts, count):
        self.parts, self.count = parts, count
        self.left = count // 2 - 1 if count in (4, 8) else 0
        if self.left:
            self.rows = parts.shape[0] // count
            self.onward, self.backward = ring_perms(count)
            self.spot = ring_spot(count)
            self.send(self.chunk(count // 2), self.chunk(1 - count // 2))

    def chunk(self, ahead):
        at = ring_at(self.spot + ahead, self.count) * self.rows
        return lax.dynamic_slice_in_dim(self.parts, at, self.rows, 0).astype(wide)

    def send(self, ahead, behind):
        self.ahead = lax.ppermute(ahead.astype(low), "dp", self.onward)
        if behind is not None:
            self.behind = lax.ppermute(behind.astype(low), "dp", self.backward)

    def flying(self):
        return [(self, "ahead"), (self, "behind")] if self.count in (4, 8) else []

    def hop(self):
        if not self.left:
            return
        ahead = self.ahead.astype(wide) + self.chunk(self.left)
        behind = None
        if self.left > 1:
            behind = self.behind.astype(wide) + self.chunk(1 - self.left)
        self.send(ahead, behind)
        self.left -= 1

    def total(self):
        if self.count not in (4, 8):
            return lax.psum_scatter(self.parts, "dp", scatter_dimension=0, tiled=True).astype(wide)
        return self.ahead.astype(wide) + self.behind.astype(wide) + self.chunk(0)


class GroupSum:
    def __init__(self, kept, sent):
        self.kept, self.got = kept, lax.ppermute(sent, "mp", CORE_SWAP)

    def cross(self):
        quarter = self.kept.shape[0] // 2
        passed = (self.kept[quarter:] + self.got[quarter:].astype(wide)).astype(low)
        self.last = lax.ppermute(passed, "mp", CHIP_SWAP)

    def terms(self):
        return self.kept, self.got, self.last


class GroupGather:
    def __init__(self, own):
        self.own = own
        self.chip = lax.ppermute(own, "mp", CHIP_SWAP)
        self.core = lax.ppermute(own, "mp", CORE_SWAP)

    def forward(self):
        self.both = lax.ppermute(self.chip, "mp", CORE_SWAP)

    def flying(self):
        return [(self, "chip"), (self, "core")]

    def pieces(self):
        return [self.own, self.chip, self.core, self.both]

    def in_order(self, mp_place):
        return in_group_order([self.own, self.core, self.chip, self.both], mp_place)


class DoublingGather:
    def __init__(self, shard, count):
        self.shard, self.count = shard, count
        self.known, self.step = shard[None], count // 2 if count in (4, 8) else 0
        self.send()

    def send(self):
        if self.step:
            swap = [(i, i ^ self.step) for i in range(self.count)]
            self.got = lax.ppermute(self.known, "dp", swap)

    def join(self, got):
        second = lax.axis_index("dp") // self.step % 2 == 1
        pair = [jnp.where(second, got, self.known), jnp.where(second, self.known, got)]
        self.known = jnp.stack(pair, 1).reshape((-1,) + self.shard.shape)
        self.step //= 2

    def flying(self):
        return [(self, "got")] if self.step else []

    def hop(self):
        if self.step > 1:
            self.join(self.got)
            self.send()

    def whole(self):
        if self.step:
            self.join(self.got)
        if self.count not in (4, 8):
            return lax.all_gather(self.shard, "dp", axis=0, tiled=False)
        return self.known


class HalvingSum:
    def __init__(self, parts, count):
        self.parts, self.count, self.step = parts, count, 1
        self.send()

    def send(self):
        pairs = self.parts.reshape((self.parts.shape[0] // 2, 2) + self.parts.shape[1:])
        bit = lax.axis_index("dp") // self.step % 2
        sent = lax.dynamic_index_in_dim(pairs, 1 - bit, 1, keepdims=False).astype(low)
        self.kept = lax.dynamic_index_in_dim(pairs, bit, 1, keepdims=False).astype(wide)
        swap = [(i, i ^ self.step) for i in range(self.count)]
        self.got = lax.ppermute(sent, "dp", swap)

    def flying(self):
        return [(self, "got")] if self.step < self.count else []

    def hop(self):
        if self.step < self.count:
            self.parts = self.kept + self.got.astype(wide)
            self.step *= 2
            if self.step < self.count:
                self.send()


class RingGather:
    def __init__(self, shard, count):
        self.count, self.left = count, count // 2 - 1
        self.onward, self.backward = ring_perms(count)
        self.pieces = [shard]
        self.send(shard, shard)

    def send(self, ahead, behind):
        self.ahead = lax.ppermute(ahead, "dp", self.onward)
        self.behind = lax.ppermute(behind, "dp", self.backward)

    def flying(self):
        return [(self, "ahead"), (self, "behind")]

    def hop(self):
        ahead, behind = self.ahead, self.behind
        self.pieces += [ahead, behind]
        if self.left > 1:
            self.send(ahead, behind)
        elif self.left == 1:
            cut = ahead.shape[0] // 32 * 16
            self.send(ahead[:cut], behind[cut:])
        self.left -= 1

    def place(self, chain):
        while self.left >= 0:
            self.hop()
        return place_pieces(chain, ring_places(self.pieces[0].shape[0], self.count), self.pieces)


def share_hop(known, reach, count):
    return known + lax.ppermute(known, "dp", [(i, i ^ reach) for i in range(count)])


def in_group_order(pieces, place):
    stacked = jnp.stack(pieces, 0)
    return [
        lax.dynamic_index_in_dim(stacked, jnp.bitwise_xor(place, j), 0, keepdims=False)
        for j in range(4)
    ]


def key_windows(row_len, block):
    return [
        (at, max(0, at - REACH), min(row_len, at + block + REACH))
        for at in range(0, row_len, block)
    ]


def relative_at(place, j, block):
    return pl.multiple_of(jnp.bitwise_xor(place, j) * block, block)


def attend_forward_kernel(
    place_ref, qkv_ref, seg_col_ref, seg_row_ref, w_ref, out_ref, kept_ref, sent_ref, q_s, k_s, v_s, *, heads
):
    row_len = qkv_ref.shape[0]
    width = heads * HEAD_DIM
    block = row_len // 4
    place = place_ref[0]
    for j in range(4):
        at = relative_at(place, j, block)
        to = slice(j * block, (j + 1) * block)
        for h in range(heads):
            c = h * HEAD_DIM
            q_s[h, to, :] = qkv_ref[pl.ds(at, block), c : c + HEAD_DIM]
            k_s[h, to, :] = qkv_ref[pl.ds(at, block), width + c : width + c + HEAD_DIM]
            v_s[h, to, :] = qkv_ref[pl.ds(at, block), 2 * width + c : 2 * width + c + HEAD_DIM]
    for j, (at, start, stop) in enumerate(key_windows(row_len, block)):
        same = seg_col_ref[start:stop, :] == seg_row_ref[:, at : at + block]
        mixed = []
        for h in range(heads):
            scores = dot_as(k_s[h, start:stop, :], q_s[h, at : at + block, :], DOT_NT)
            scores = jnp.where(same, scores, neg_large)
            top = jnp.max(scores, axis=0, keepdims=True)
            weights = jnp.exp((scores - top) * score_scale)
            total = jnp.sum(weights, axis=0, keepdims=True)
            gathered = dot_as(v_s[h, start:stop, :], weights.astype(low), DOT_TN)
            mixed.append(gathered * (1.0 / total))
        out_ref[pl.ds(relative_at(place, j, block), block), :] = (
            jnp.concatenate(mixed, axis=0).T.astype(low)
        )
    w_out = w_ref[:, 3 * width :]
    half = row_len // 2
    kept_ref[...] = dot_as(out_ref[:half, :], w_out, DOT_NT)
    sent_ref[...] = dot_as(out_ref[half:, :], w_out, DOT_NT).astype(low)


def attend_backward_kernel(
    place_ref, qkv_ref, g0_ref, g1_ref, g2_ref, g3_ref, seg_col_ref, seg_row_ref, w_ref,
    out_ref, kept_ref, sent_ref, sums_ref, q_s, k_s, v_s, g_s, dk_s, dv_s, *, heads
):
    row_len = qkv_ref.shape[0]
    width = heads * HEAD_DIM
    block = row_len // 4
    place = place_ref[0]
    dk_s[...] = jnp.zeros_like(dk_s)
    dv_s[...] = jnp.zeros_like(dv_s)
    w_out = w_ref[:, 3 * width :]
    for j, g_ref in enumerate((g0_ref, g1_ref, g2_ref, g3_ref)):
        grad = dot_as(g_ref[...], w_out, DOT_NN).astype(low)
        at = relative_at(place, j, block)
        for h in range(heads):
            g_s[h, pl.ds(at, block), :] = grad[:, h * HEAD_DIM : (h + 1) * HEAD_DIM]
    for j in range(4):
        at = relative_at(place, j, block)
        to = slice(j * block, (j + 1) * block)
        for h in range(heads):
            c = h * HEAD_DIM
            q_s[h, to, :] = qkv_ref[pl.ds(at, block), c : c + HEAD_DIM]
            k_s[h, to, :] = qkv_ref[pl.ds(at, block), width + c : width + c + HEAD_DIM]
            v_s[h, to, :] = qkv_ref[pl.ds(at, block), 2 * width + c : 2 * width + c + HEAD_DIM]
    for j, (at, start, stop) in enumerate(key_windows(row_len, block)):
        same = seg_col_ref[start:stop, :] == seg_row_ref[:, at : at + block]
        grads = []
        for h in range(heads):
            query = q_s[h, at : at + block, :]
            grad = g_s[h, at : at + block, :]
            keys = k_s[h, start:stop, :]
            scores = jnp.where(same, dot_as(keys, query, DOT_NT), neg_large)
            top = jnp.max(scores, axis=0, keepdims=True)
            weights = jnp.exp((scores - top) * score_scale)
            probs = weights * (1.0 / jnp.sum(weights, axis=0, keepdims=True))
            grad_probs = dot_as(v_s[h, start:stop, :], grad, DOT_NT)
            inner = jnp.sum(grad_probs * probs, axis=0, keepdims=True)
            grad_scores = (probs * (grad_probs - inner)).astype(low)
            dv_s[h, start:stop, :] += dot_as(probs.astype(low), grad, DOT_NN)
            dk_s[h, start:stop, :] += dot_as(grad_scores, query, DOT_NN)
            grads.append(dot_as(keys, grad_scores, DOT_TN) * score_scale)
        out_ref[pl.ds(relative_at(place, j, block), block), 0:width] = (
            jnp.concatenate(grads, axis=0).T.astype(low)
        )
    for j in range(4):
        at = slice(j * block, (j + 1) * block)
        to = relative_at(place, j, block)
        out_ref[pl.ds(to, block), width : 2 * width] = jnp.concatenate(
            [(dk_s[h, at, :] * score_scale).astype(low) for h in range(heads)], axis=1
        )
        out_ref[pl.ds(to, block), 2 * width : 3 * width] = jnp.concatenate(
            [dv_s[h, at, :].astype(low) for h in range(heads)], axis=1
        )
    half = row_len // 2
    w_qkv = w_ref[:, : 3 * width]
    kept_ref[...] = dot_as(out_ref[:half, :], w_qkv, DOT_NT)
    sent_ref[...] = dot_as(out_ref[half:, :], w_qkv, DOT_NT).astype(low)
    for u in range(row_len // UNIT):
        sums_ref[u : u + 1, :] = jnp.sum(
            out_ref[u * UNIT : (u + 1) * UNIT, :].astype(wide), axis=0, keepdims=True
        )


def shape_of(shape, kind):
    return jax.ShapeDtypeStruct(shape, kind)


def attend_forward(chain, qkv, seg_row, weights):
    row_len, width = qkv.shape[0], qkv.shape[1] // 3
    heads = width // HEAD_DIM
    full = weights.shape[0]
    args = (qkv, seg_row.reshape(row_len, 1), seg_row.reshape(1, row_len), weights)
    shapes = (
        shape_of((row_len, width), low),
        shape_of((row_len // 2, full), wide),
        shape_of((row_len // 2, full), low),
    )

    def body(*refs):
        attend_forward_kernel(*refs, heads=heads)

    return row_call(
        body,
        "attend_forward",
        chain,
        args,
        [fixed_spec(arg.shape) for arg in args],
        tuple(fixed_spec(shape.shape) for shape in shapes),
        shapes,
        scratch=[pltpu.VMEM((heads, row_len, HEAD_DIM), low)] * 3,
        flops=4 * row_len * 640 * width + 2 * row_len * width * full,
        exps=heads * row_len * 640,
    )


def attend_backward(chain, qkv, grads, seg_row, weights):
    row_len, width = qkv.shape[0], qkv.shape[1] // 3
    heads = width // HEAD_DIM
    full = weights.shape[0]
    args = (qkv, *grads, seg_row.reshape(row_len, 1), seg_row.reshape(1, row_len), weights)
    shapes = (
        shape_of((row_len, 3 * width), low),
        shape_of((row_len // 2, full), wide),
        shape_of((row_len // 2, full), low),
        shape_of((row_len // UNIT, 3 * width), wide),
    )

    def body(*refs):
        attend_backward_kernel(*refs, heads=heads)

    return row_call(
        body,
        "attend_backward",
        chain,
        args,
        [fixed_spec(arg.shape) for arg in args],
        tuple(fixed_spec(shape.shape) for shape in shapes),
        shapes,
        scratch=[pltpu.VMEM((heads, row_len, HEAD_DIM), low)] * 4
        + [pltpu.VMEM((heads, row_len, HEAD_DIM), wide)] * 2,
        flops=10 * row_len * 640 * width + 8 * row_len * width * full,
        exps=heads * row_len * 640,
    )


def norm_parts(values):
    centre = values - jnp.mean(values, axis=-1, keepdims=True)
    inverse = lax.rsqrt(jnp.mean(centre * centre, axis=-1, keepdims=True) + norm_eps)
    return centre * inverse, inverse


def norm_back(normed, inverse, grad):
    return inverse * (
        grad
        - jnp.mean(grad, axis=-1, keepdims=True)
        - normed * jnp.mean(grad * normed, axis=-1, keepdims=True)
    )


def unit_rows(ref):
    return [(u, slice(u * UNIT, (u + 1) * UNIT)) for u in range(ref.shape[0] // UNIT)]


def column(values, index, width):
    return values[:, index * width : (index + 1) * width]


def open_kernel(
    place_ref, x0_ref, x1_ref, tab0_ref, tab1_ref, add0_ref, add1_ref, w_ref, a_ref, qkv_ref
):
    width = x0_ref.shape[1]
    quarter = x0_ref.shape[0]
    for j, (x_ref, tab_ref) in enumerate(((x0_ref, tab0_ref), (x1_ref, tab1_ref))):
        for u, at in unit_rows(x_ref):
            normed, _ = norm_parts(x_ref[at, :].astype(wide))
            table = tab_ref[0, u : u + 1, :]
            out = normed * (1.0 + column(table, 1, width)) + column(table, 0, width)
            a_ref[j * quarter + u * UNIT : j * quarter + (u + 1) * UNIT, :] = out.astype(low)
    qkv = dot_as(a_ref[...], w_ref[:, : qkv_ref.shape[1]], DOT_NN)
    for j, add_ref in enumerate((add0_ref, add1_ref)):
        for u in range(quarter // UNIT):
            at = slice(j * quarter + u * UNIT, j * quarter + (u + 1) * UNIT)
            qkv_ref[at, :] = (qkv[at, :] + add_ref[0, u : u + 1, :]).astype(low)


def first_kernel(place_ref, x_ref, kept_ref, got_ref, passed_ref, bias_ref, tab_ref, att_ref, hid_ref, a_ref):
    width = x_ref.shape[1]
    for u, at in unit_rows(x_ref):
        table = tab_ref[0, u : u + 1, :]
        attended = kept_ref[at, :] + got_ref[at, :].astype(wide) + passed_ref[at, :].astype(wide)
        attended = attended + bias_ref[0:1, :]
        hidden = x_ref[at, :].astype(wide) + column(table, 0, width) * attended
        normed, _ = norm_parts(hidden)
        att_ref[at, :] = attended
        hid_ref[at, :] = hidden
        a_ref[at, :] = (normed * (1.0 + column(table, 2, width)) + column(table, 1, width)).astype(low)


def down_back_kernel(place_ref, cot0_ref, cot1_ref, tab0_ref, tab1_ref, w_ref, grad_ref, dm_ref):
    width = cot0_ref.shape[1]
    quarter = cot0_ref.shape[0]
    for j, (cot_ref, tab_ref) in enumerate(((cot0_ref, tab0_ref), (cot1_ref, tab1_ref))):
        for u, at in unit_rows(cot_ref):
            gate = column(tab_ref[0, u : u + 1, :], 3, width)
            out = (cot_ref[at, :].astype(wide) * gate).astype(low)
            grad_ref[j * quarter + u * UNIT : j * quarter + (u + 1) * UNIT, :] = out
    dm_ref[...] = dot_as(grad_ref[...], w_ref[...], DOT_NN).astype(low)


def gelu_both(values):
    scale = math.sqrt(2.0 / math.pi)
    square = values * values
    turned = jnp.tanh(scale * values * (1.0 + 0.044715 * square))
    upper = 0.5 * (1.0 + turned)
    slope = upper + 0.5 * values * (1.0 - turned * turned) * scale * (1.0 + 3 * 0.044715 * square)
    return values * upper, slope


def up_kernel(
    place_ref, a0_ref, a1_ref, a2_ref, a3_ref, dm_ref, bias_ref, w_ref, m_ref, dz_ref, kept_ref, sent_ref, sums_ref, a_s
):
    step = pl.program_id(0)
    quarter = a0_ref.shape[0]
    for j, piece in enumerate((a0_ref, a1_ref, a2_ref, a3_ref)):

        @pl.when(step == j // 2)
        def _(piece=piece, j=j):
            a_s[j % 2 * quarter : (j % 2 + 1) * quarter, :] = piece[...]

    sums = jnp.zeros(sums_ref.shape[1:], wide)
    for j in range(2):
        at = slice(j * quarter, (j + 1) * quarter)
        inner = dot_as(a_s[at, :], w_ref[...], DOT_NN) + bias_ref[...]
        active, slope = gelu_both(inner)
        m_ref[at, :] = active.astype(low)
        grad = (dm_ref[at, :].astype(wide) * slope).astype(low)
        dz_ref[at, :] = grad
        sums = sums + jnp.sum(grad.astype(wide).reshape(-1, 8, grad.shape[1]), axis=0)
    sums_ref[0] = sums
    back = dot_as(dz_ref[...], w_ref[...], DOT_NT)

    @pl.when(step == 0)
    def _():
        kept_ref[...] = back

    @pl.when(step == 1)
    def _():
        sent_ref[...] = back.astype(low)


def down_kernel(place_ref, m_ref, w_ref, kept_ref, sent_ref):
    step = pl.program_id(0)
    out = dot_as(m_ref[...], w_ref[...], DOT_NT)

    @pl.when(step == 0)
    def _():
        kept_ref[...] = out

    @pl.when(step == 1)
    def _():
        sent_ref[...] = out.astype(low)


def second_kernel(
    place_ref, cot_ref, kept_ref, got_ref, passed_ref, hid_ref, att_ref, tab_ref, gh_ref, ga_ref, sums_ref
):
    width = cot_ref.shape[1]
    bias = jnp.zeros((1, width), wide)
    sums_ref[...] = jnp.zeros_like(sums_ref)
    for u, at in unit_rows(cot_ref):
        table = tab_ref[0, u : u + 1, :]
        grad_two = kept_ref[at, :] + got_ref[at, :].astype(wide) + passed_ref[at, :].astype(wide)
        normed, inverse = norm_parts(hid_ref[at, :])
        grad = cot_ref[at, :].astype(wide) + norm_back(
            normed, inverse, grad_two * (1.0 + column(table, 2, width))
        )
        grad_att = grad * column(table, 0, width)
        gh_ref[at, :] = grad
        ga_ref[at, :] = grad_att.astype(low)
        bias = bias + jnp.sum(grad_att, axis=0, keepdims=True)
        sums_ref[u : u + 1, :] = jnp.sum(grad * att_ref[at, :], axis=0, keepdims=True)
        sums_ref[4 + u : 5 + u, :] = jnp.sum(grad_two, axis=0, keepdims=True)
        sums_ref[8 + u : 9 + u, :] = jnp.sum(grad_two * normed, axis=0, keepdims=True)
    sums_ref[12:13, :] = bias


def out_kernel(
    place_ref, cot_ref, kept_ref, got_ref, passed_ref, hid_ref, bias_ref, tab_ref, out_ref, sums_ref
):
    width = cot_ref.shape[1]
    bias = jnp.zeros((1, width), wide)
    sums_ref[...] = jnp.zeros_like(sums_ref)
    for u, at in unit_rows(cot_ref):
        gate = column(tab_ref[0, u : u + 1, :], 3, width)
        mlp = kept_ref[at, :] + got_ref[at, :].astype(wide) + passed_ref[at, :].astype(wide)
        mlp = mlp + bias_ref[1:2, :]
        out_ref[at, :] = (hid_ref[at, :] + gate * mlp).astype(low)
        cot = cot_ref[at, :].astype(wide)
        sums_ref[u : u + 1, :] = jnp.sum(cot * mlp, axis=0, keepdims=True)
        bias = bias + jnp.sum(cot, axis=0, keepdims=True) * gate
    sums_ref[4:5, :] = bias


def third_kernel(place_ref, x_ref, kept_ref, got_ref, passed_ref, gh_ref, tab_ref, out_ref, sums_ref):
    width = x_ref.shape[1]
    for u, at in unit_rows(x_ref):
        grad_one = kept_ref[at, :] + got_ref[at, :].astype(wide) + passed_ref[at, :].astype(wide)
        normed, inverse = norm_parts(x_ref[at, :].astype(wide))
        table = tab_ref[0, u : u + 1, :]
        back = norm_back(normed, inverse, grad_one * (1.0 + column(table, 1, width)))
        out_ref[at, :] = (gh_ref[at, :] + back).astype(low)
        sums_ref[u : u + 1, :] = jnp.sum(grad_one, axis=0, keepdims=True)
        sums_ref[4 + u : 5 + u, :] = jnp.sum(grad_one * normed, axis=0, keepdims=True)


def row_call(
    body, name, chain, args, in_specs, out_specs, out_shape, grid=1, scratch=(), flops=0, exps=0, aliases=None, prefetch=None
):
    moved = sum(math.prod(a.shape) * a.dtype.itemsize for a in args)
    shapes = out_shape if isinstance(out_shape, tuple) else (out_shape,)
    moved += sum(math.prod(o.shape) * o.dtype.itemsize for o in shapes)
    prefetch = chain.token if prefetch is None else chain.tie(prefetch)
    out = pl.pallas_call(
        body,
        grid_spec=pltpu.PrefetchScalarGridSpec(
            num_scalar_prefetch=1,
            grid=(grid,),
            in_specs=in_specs,
            out_specs=out_specs,
            scratch_shapes=scratch,
        ),
        out_shape=out_shape,
        input_output_aliases=aliases or {},
        compiler_params=pltpu.CompilerParams(vmem_limit_bytes=VMEM_GRANT),
        cost_estimate=pl.CostEstimate(
            flops=int(COST * flops) + 1, bytes_accessed=int(COST * moved) + 1, transcendentals=0
        ),
        name=name,
    )(prefetch, *args)
    return chain.close(*out) if isinstance(out_shape, tuple) else chain.close(out)


def fixed_spec(shape):
    return pl.BlockSpec(shape, lambda *_: (0,) * len(shape))


def unit_tables(chain, mp_arg, onehot, pieces, fields):
    units, slots = onehot.shape
    own = pieces[0].shape[1] // fields

    def body(mp_ref, hot_ref, *refs):
        out_ref = refs[-1]
        mp_place = mp_ref[0]
        for i, piece in enumerate(refs[:-1]):
            spread = dot_as(hot_ref[...], piece[...], DOT_NN)
            for j in range(4):

                @pl.when(jnp.bitwise_xor(mp_place, i) == j)
                def _(spread=spread, j=j):
                    for f in range(fields):
                        at = f * 4 * own + j * own
                        out_ref[:, at : at + own] = column(spread, f, own)

    return row_call(
        body,
        "unit_tables",
        chain,
        (onehot, *pieces),
        [fixed_spec(onehot.shape)] + [fixed_spec(pieces[0].shape)] * 4,
        fixed_spec((units, fields * 4 * own)),
        shape_of((units, fields * 4 * own), wide),
        flops=8 * units * slots * own * fields,
        prefetch=mp_arg,
    )


def weight_grad(chain, pairs, name):
    depth = pairs[0][0][0][0].shape[1]
    tile = depth // 3
    widths = [pair[0][1].shape[1] for pair in pairs]
    args, specs, plan = [], [], []
    flops = 0
    for pair in pairs:
        rows = []
        for left, right in pair:
            rows.append((len(args), len(left)))
            args += list(left) + [right]
            specs += [pl.BlockSpec((piece.shape[0], tile), lambda i, p: (0, i)) for piece in left]
            specs.append(fixed_spec(right.shape))
            flops += 2 * depth * math.prod(right.shape)
        plan.append(rows)

    def body(place_ref, *refs):
        out_ref = refs[-1]
        at = 0
        for rows, cols in zip(plan, widths):
            total = None
            for first, count in rows:
                left = [ref[...] for ref in refs[first : first + count]]
                left = left[0] if count == 1 else jnp.concatenate(left, axis=0)
                part = dot_as(left, refs[first + count][...], DOT_TN)
                total = part if total is None else total + part
            out_ref[:, at : at + cols] = total.astype(low)
            at += cols

    return row_call(
        body,
        name,
        chain,
        args,
        specs,
        pl.BlockSpec((tile, sum(widths)), lambda i, p: (i, 0)),
        shape_of((depth, sum(widths)), low),
        grid=3,
        flops=flops,
    )


def widen_row(chain, pieces, row, rows, before):
    quarter, width = pieces[0].shape

    def body(place_ref, *refs):
        step = pl.program_id(0)
        for i, piece in enumerate(refs[:4]):

            @pl.when(step == i)
            def _(piece=piece):
                refs[-1][...] = piece[...].astype(wide)

    return row_call(
        body,
        "widen_row",
        chain,
        tuple(pieces) + before,
        [fixed_spec((quarter, width))] * 4 + [pl.BlockSpec(memory_space=pl.ANY)] * len(before),
        pl.BlockSpec((quarter, width), lambda i, p: (row * 4 + jnp.bitwise_xor(p[0], i), 0)),
        shape_of((rows * 4 * quarter, width), wide),
        grid=4,
        aliases={5: 0} if before else None,
    )


def adam_step(weight, gradient, first_old, second_old, ema_old, step_rate):
    first_new = beta_one * first_old + (1.0 - beta_one) * gradient
    second_new = beta_two * second_old + (1.0 - beta_two) * gradient * gradient
    first_hat = first_new * (1.0 / (1.0 - beta_one**STEP))
    second_hat = second_new * (1.0 / (1.0 - beta_two**STEP))
    weight_new = weight - step_rate * (
        first_hat / (jnp.sqrt(second_hat) + adam_eps) + decay_rate * weight
    )
    ema_new = ema_keep * ema_old + (1.0 - ema_keep) * weight_new
    return (first_new, second_new, weight_new, ema_new)


def adam_slabs(chain, plan, grads, make_grad, groups, before, name):
    slab = groups[0][0].shape[1:]
    count, held = len(plan), 4 * len(groups)
    turns = [[i for i, (which, _) in enumerate(plan) if which == g] for g in range(len(groups))]
    ids = [plan[max([i for i in mine if i <= n], default=mine[0])][1] for mine in turns for n in range(count)]
    ids = jnp.array(ids, jnp.int32)

    def block(group):
        return pl.BlockSpec((1,) + slab, lambda i, ids: (ids[group * count + i], 0, 0))

    def body(ids_ref, *refs):
        grad_refs, state_refs = refs[: len(grads)], refs[len(grads) : len(grads) + held]
        out_refs, grad_s = refs[-held - 1 : -1], refs[-1]
        step = pl.program_id(0)
        for n in range(count):

            @pl.when(step == n)
            def _(n=n):
                grad_s[...] = make_grad(n, grad_refs)

        for group, mine in enumerate(turns):

            @pl.when((step >= mine[0]) & (step <= mine[-1]))
            def _(group=group):
                weight, *old = [ref[0] for ref in state_refs[4 * group : 4 * group + 4]]
                new = adam_step(weight, grad_s[...], *old, rate_matrix)
                for ref, value in zip(out_refs[4 * group : 4 * group + 4], new):
                    ref[0] = value

    flat = [x for group in groups for x in group]
    specs = [block(g) for g in range(len(groups)) for _ in range(4)]
    kept, aliases = [], {}
    for g, arrays in enumerate(before):
        for i, x in enumerate(arrays or ()):
            aliases[1 + len(grads) + held + len(kept)] = 4 * g + i
            kept.append(x)
    return row_call(
        body,
        name,
        chain,
        (*grads, *flat, *kept),
        [fixed_spec(grad.shape) for grad in grads]
        + specs
        + [pl.BlockSpec(memory_space=pl.ANY)] * len(kept),
        tuple(specs),
        tuple(shape_of(x.shape, wide) for x in flat),
        grid=count,
        scratch=[pltpu.VMEM(slab, wide)],
        aliases=aliases,
        prefetch=ids,
    )


def per_device(
    tokens,
    seg_ids,
    time_steps,
    cotangent,
    weight_cols,
    weight_rows,
    bias_cols,
    bias_rows,
    first_cols,
    first_rows,
    first_bias_cols,
    first_bias_rows,
    second_cols,
    second_rows,
    second_bias_cols,
    second_bias_rows,
    ema_cols,
    ema_rows,
    ema_bias_cols,
    ema_bias_rows,
):
    own_width = weight_cols.shape[2]
    own_depth = weight_cols.shape[1]
    width = tokens.shape[1]
    rows = time_steps.shape[0]
    slots = time_steps.shape[1]
    token_count = tokens.shape[0]
    row_len = token_count // rows
    units = row_len // UNIT
    quarter = row_len // 4
    own_units = units // 4
    dp_count = width // own_depth
    dp_place = lax.axis_index("dp")
    slot_count = rows * slots
    mp_place = lax.axis_index("mp")
    core, chip = mp_place % 2, mp_place // 2
    place = (2 * core + chip).astype(jnp.int32)
    place_arg = place.reshape(1)

    chain = Chain(place_arg)

    ring = dp_count in (4, 8)
    known = jnp.zeros((dp_count,) + time_steps.shape, time_steps.dtype)
    known = lax.dynamic_update_slice_in_dim(known, time_steps[None], dp_place, 0)
    known, weight_cols, weight_rows = lax.optimization_barrier((known, weight_cols, weight_rows))
    cols_low = weight_cols.astype(low)
    own_rows = weight_rows.astype(low).transpose(2, 0, 1).reshape(own_depth, 5 * own_width)
    own_first = jnp.concatenate([cols_low[0], cols_low[1], cols_low[2], own_rows[:, :own_width]], 1)
    own_rest = jnp.concatenate([cols_low[5 + i] for i in range(4)] + [own_rows[:, own_width:]], 1)

    half_width = width // 2
    feature = dp_place * own_depth + jnp.arange(own_depth)
    is_cos = feature < half_width
    index = jnp.where(is_cos, feature, feature - half_width).astype(wide)
    frequency = jnp.exp(-math.log(10000.0) * index / half_width)

    def embed(steps):
        angles = steps.astype(wide)[:, None] * frequency[None, :]
        table = jnp.where(is_cos[None, :], jnp.cos(angles), jnp.sin(angles))
        return table.astype(low), jax.nn.silu(table).astype(low)

    near_maps = [jnp.concatenate([cols_low[i], cols_low[i + 1]], 1) for i in (9, 3)]
    far_maps = jnp.concatenate([cols_low[i] for i in (11, 12, 13, 14)], 1)

    def slot_products(pairs):
        out = jnp.concatenate([dot_as(left, maps, DOT_NN).astype(low) for left, maps in pairs], 1)
        return out.reshape(dp_count, rows * slots, -1)

    if ring:
        first_gather = RingGather(own_first, dp_count)

        def beside(value):
            value, first_gather.ahead, first_gather.behind = lax.optimization_barrier(
                (value, first_gather.ahead, first_gather.behind)
            )
            if first_gather.left > 0:
                first_gather.hop()
            return value

        known = share_hop(known, 1, dp_count)
        known = beside(share_hop(known, 2, dp_count))
        if dp_count == 8:
            known = share_hop(known, 4, dp_count)
        time_low, ada_low = embed(known.reshape(-1))
        near = beside(slot_products([(ada_low, near_maps[0]), (time_low, near_maps[1])]))
        near = HalvingSum(near, dp_count)
        near.hop()
        if dp_count == 8:
            near.hop()
        own_rest = beside(own_rest)
        rest_gather = RingGather(own_rest, dp_count)
        near.hop()
        near = near.parts[0]
    else:
        w_first = lax.all_gather(own_first, "dp", axis=0, tiled=True)
        w_rest = lax.all_gather(own_rest, "dp", axis=0, tiled=True)
        time_low, ada_low = embed(lax.all_gather(time_steps, "dp", axis=0, tiled=True).reshape(-1))
        near = slot_products([(ada_low, near_maps[0]), (time_low, near_maps[1])])
        near = lax.psum_scatter(near, "dp", scatter_dimension=0, tiled=True)[0].astype(wide)

    seg_grid = seg_ids.reshape(rows, row_len)
    unit_seg = seg_grid.reshape(rows, units, UNIT)[:, :, 0]
    onehot = unit_seg[:, :, None] == jnp.arange(slots, dtype=jnp.int32)
    blocks = onehot[:, :, None, :] & (jnp.arange(rows)[:, None] == jnp.arange(rows))[:, None, :, None]
    blocks = blocks.reshape(rows * units, rows * slots)
    mp_arg = mp_place.astype(jnp.int32).reshape(1)

    def tables(spread, fields):
        spread.forward()
        pieces = [spread.own, spread.core, spread.chip, spread.both]
        out = unit_tables(chain, mp_arg, blocks.astype(low), pieces, fields)
        return out.reshape(rows, 4, own_units, -1)

    far = slot_products([(lax.optimization_barrier((ada_low, near))[0], far_maps)])
    near_mod = (near[:, : 2 * own_width] + bias_cols[6:8].reshape(1, -1)).astype(low)
    near_tab = tables(GroupGather(near_mod), 2)
    if ring:
        far = HalvingSum(far, dp_count)
        chain.land(*far.flying(), *rest_gather.flying())
        w_first = first_gather.place(chain)
        far.hop()
        rest_gather.hop()
    time_add = jnp.concatenate(
        [
            near[:, 2 * own_width : 3 * own_width] + bias_cols[0],
            jnp.zeros((rows * slots, own_width), wide),
            near[:, 3 * own_width :] + bias_cols[1],
        ],
        1,
    )
    add_tab = jnp.dot(blocks.astype(wide), time_add, precision=highest)
    add_tab = add_tab.reshape(rows, 4, own_units, 3 * own_width)

    block, half_block = (quarter, width), (row_len // 2, width)
    qkv_width = 3 * own_width
    half = row_len // 2
    lows = lambda *shape: shape_of(shape, low)
    wides = lambda *shape: shape_of(shape, wide)

    def own_block(r):
        return pl.BlockSpec(block, lambda i, p: (r * 4 + p[0], 0))

    def moved_blocks(r):
        return [
            pl.BlockSpec(block, lambda i, p: (r * 4 + jnp.bitwise_xor(p[0], 2 * i), 0)),
            pl.BlockSpec(block, lambda i, p: (r * 4 + jnp.bitwise_xor(p[0], 2 * i + 1), 0)),
        ]

    def moved_tables(tab):
        shape = (1,) + tab.shape[2:]
        return [
            pl.BlockSpec(shape, lambda i, p: (jnp.bitwise_xor(p[0], 2 * i), 0, 0)),
            pl.BlockSpec(shape, lambda i, p: (jnp.bitwise_xor(p[0], 2 * i + 1), 0, 0)),
        ]

    def own_table(tab):
        return pl.BlockSpec((1,) + tab.shape[2:], lambda i, p: (p[0], 0, 0))

    here = fixed_spec(block)
    half_step = pl.BlockSpec(half_block, lambda i, p: (i, 0))
    half_fixed = fixed_spec(half_block)

    def open_row(r):
        return row_call(
            open_kernel,
            "open_row",
            chain,
            (tokens, tokens, near_tab[r], near_tab[r], add_tab[r], add_tab[r], w_first),
            moved_blocks(r) + moved_tables(near_tab) + moved_tables(add_tab) + [fixed_spec(w_first.shape)],
            (half_step, pl.BlockSpec((half, qkv_width), lambda i, p: (i, 0))),
            (lows(row_len, width), lows(row_len, qkv_width)),
            grid=2,
            flops=2 * row_len * width * qkv_width,
        )

    inputs_one, qkvs, mixed, parts = [], [], [], []
    for r in range(rows):
        if r == 0 and ring:
            chain.land(*far.flying())
        if r:
            chain.land((parts[r - 1], "got"))
        if r == 1:
            chain.land(*far_gather.flying())
        a_one, qkv = open_row(r)
        inputs_one.append(a_one)
        qkvs.append(qkv)
        if r:
            parts[r - 1].cross()
        if r == 1:
            if ring:
                chain.land(*rest_gather.flying())
            far_tab = tables(far_gather, 4)
            if ring:
                rest_gather.hop()
                chain.land(*rest_gather.flying())
        if r == 0 and ring:
            far.hop()
            chain.land(*far.flying(), *rest_gather.flying())
        if r:
            chain.land((parts[r - 1], "last"))
        out, kept, sent = attend_forward(chain, qkv, seg_grid[r], w_first)
        mixed.append(out)
        parts.append(GroupSum(kept, sent))
        if r == 0:
            if ring:
                rest_gather.hop()
                far.hop()
                far = far.parts[0]
            else:
                far = lax.psum_scatter(far, "dp", scatter_dimension=0, tiled=True)[0].astype(wide)
            far_gather = GroupGather((far + bias_cols[8:12].reshape(1, -1)).astype(low))

    attendeds, hiddens, inputs_two, down_grads = [], [], [], []

    def first_norm(r):
        attended, hidden, a_two = row_call(
            first_kernel,
            "first_norm",
            chain,
            (tokens, *parts[r].terms(), bias_rows, far_tab[r]),
            [own_block(r), here, here, here, fixed_spec(bias_rows.shape), own_table(far_tab)],
            (here, here, here),
            (wides(*block), wides(*block), lows(*block)),
        )
        attendeds.append(attended)
        hiddens.append(hidden)
        inputs_two.append(GroupGather(a_two))

    def down_back(r):
        grads = row_call(
            down_back_kernel,
            "down_back",
            chain,
            (cotangent, cotangent, far_tab[r], far_tab[r], w_rest),
            moved_blocks(r) + moved_tables(far_tab) + [w_down_spec],
            (half_step, half_step),
            (lows(row_len, width), lows(row_len, width)),
            grid=2,
            flops=2 * row_len * width * width,
        )
        down_grads.append(grads)

    chain.land((parts[-1], "got"))
    first_norm(0)
    parts[-1].cross()
    if ring:
        w_rest = rest_gather.place(chain)
    w_down_spec = pl.BlockSpec((width, w_rest.shape[1] // 2), lambda i, p: (0, 1))
    w_up_spec = pl.BlockSpec((width, w_rest.shape[1] // 2), lambda i, p: (0, 0))
    chain.land(*inputs_two[0].flying())
    down_back(0)
    inputs_two[0].forward()
    chain.land((inputs_two[0], "both"), (parts[-1], "last"))
    down_back(1)
    first_norm(1)

    bias_up = bias_cols[2:6].reshape(1, -1)
    hidden_width = bias_up.shape[1]
    actives, inner_grads, up_parts, up_sums, down_parts = [], [], [], 0.0, []
    for r in range(rows):
        if r + 1 < rows:
            chain.land(*inputs_two[r + 1].flying())
        if r:
            chain.land((up_parts[r - 1], "last"), (down_parts[r - 1], "got"))
        active, inner_grad, kept, sent, sums = row_call(
            up_kernel,
            "up_and_back",
            chain,
            (*inputs_two[r].pieces(), down_grads[r][1], bias_up, w_rest),
            [here] * 4 + [half_step, fixed_spec(bias_up.shape), w_up_spec],
            (
                pl.BlockSpec((half, hidden_width), lambda i, p: (i, 0)),
                pl.BlockSpec((half, hidden_width), lambda i, p: (i, 0)),
                half_fixed,
                half_fixed,
                pl.BlockSpec((1, 8, hidden_width), lambda i, p: (i, 0, 0)),
            ),
            (
                lows(row_len, hidden_width),
                lows(row_len, hidden_width),
                wides(half, width),
                lows(half, width),
                wides(2, 8, hidden_width),
            ),
            grid=2,
            scratch=[pltpu.VMEM(half_block, low)],
            flops=4 * row_len * width * hidden_width,
        )
        actives.append(active)
        inner_grads.append(inner_grad)
        up_parts.append(GroupSum(kept, sent))
        up_sums = up_sums + jnp.sum(sums, axis=(0, 1))
        chain.land((up_parts[r], "got"))
        if r + 1 < rows:
            inputs_two[r + 1].forward()
            chain.land((inputs_two[r + 1], "both"))
        if r:
            down_parts[r - 1].cross()
            chain.land((down_parts[r - 1], "last"))
        kept, sent = row_call(
            down_kernel,
            "down",
            chain,
            (active, w_rest),
            [pl.BlockSpec((half, hidden_width), lambda i, p: (i, 0)), w_down_spec],
            (half_fixed, half_fixed),
            (wides(half, width), lows(half, width)),
            grid=2,
            flops=2 * row_len * width * hidden_width,
        )
        down_parts.append(GroupSum(kept, sent))
        up_parts[r].cross()

    grad_hiddens, grad_gathers, second_sums = [], [], []

    def second_norm(r):
        grad_hidden, grad_attended, sums = row_call(
            second_kernel,
            "second_norm",
            chain,
            (cotangent, *up_parts[r].terms(), hiddens[r], attendeds[r], far_tab[r]),
            [own_block(r)] + [here] * 5 + [own_table(far_tab)],
            (here, here, fixed_spec((16, width))),
            (wides(*block), lows(*block), wides(16, width)),
        )
        grad_hiddens.append(grad_hidden)
        grad_gathers.append(GroupGather(grad_attended))
        second_sums.append(sums)

    chain.land((down_parts[-1], "got"))
    second_norm(0)
    down_parts[-1].cross()
    chain.land((up_parts[-1], "last"), *grad_gathers[0].flying())
    rest_grad = weight_grad(
        chain,
        [
            [(inputs_two[r].pieces(), inner_grads[r]) for r in range(rows)],
            [([down_grads[r][0]], actives[r]) for r in range(rows)],
        ],
        "grad_rest",
    )
    rest_ring = RingSum(rest_grad, dp_count)
    grad_gathers[0].forward()
    chain.land((grad_gathers[0], "both"))
    second_norm(1)

    out_gathers, out_sums = [], []

    def out_row(r):
        out_own, sums = row_call(
            out_kernel,
            "out_tokens",
            chain,
            (cotangent, *down_parts[r].terms(), hiddens[r], bias_rows, far_tab[r]),
            [own_block(r)] + [here] * 4 + [fixed_spec(bias_rows.shape), own_table(far_tab)],
            (here, fixed_spec((8, width))),
            (lows(*block), wides(8, width)),
        )
        out_gathers.append(GroupGather(out_own))
        out_sums.append(sums)

    def part(held, which, columns):
        return lax.dynamic_slice_in_dim(held, which * columns, columns, 1)

    class Exchange:
        def __init__(self, values):
            values = values.astype(low)
            self.mine = part(values, chip, 2 * own_width)
            self.other = lax.ppermute(part(values, 1 - chip, 2 * own_width), "mp", CHIP_SWAP)

        def cross(self):
            values = self.whole()
            self.mine = part(values, core, own_width)
            self.other = lax.ppermute(part(values, 1 - core, own_width), "mp", CORE_SWAP)

        def whole(self):
            return jnp.concatenate([self.mine, self.other], 0)

    seg_place = unit_seg.reshape(rows, 4, own_units)
    seg_place = jnp.stack(
        [
            lax.dynamic_index_in_dim(seg_place, jnp.bitwise_xor(place, j), 1, keepdims=False)
            for j in range(4)
        ],
        0,
    )
    row_slots = seg_place + slots * jnp.arange(rows)[None, :, None]

    def field_slots(field):
        return row_slots + slot_count * field

    def slot_matrix(to, height):
        to = jnp.concatenate(to, 2).reshape(1, -1)
        return (jnp.arange(height)[:, None] == to).astype(low)

    def spare_slot(slot):
        return jnp.broadcast_to(jnp.array([slot, -1, -1, -1]), (4, rows, 4))

    chain.land(*rest_ring.flying())
    out_row(0)
    rest_ring.hop()
    qkv_grads, one_parts, time_sums = [], [], []

    def backward(r):
        qkv_grad, kept, sent, sums = attend_backward(
            chain, qkvs[r], grad_gathers[r].pieces(), seg_grid[r], w_first
        )
        qkv_grads.append(qkv_grad)
        one_parts.append(GroupSum(kept, sent))
        time_sums.append(sums)

    chain.land(*rest_ring.flying(), *grad_gathers[1].flying(), (down_parts[-1], "last"))
    backward(0)
    rest_ring.hop()
    grad_gathers[1].forward()
    chain.land((one_parts[0], "got"), (grad_gathers[1], "both"))
    out_row(1)
    one_parts[0].cross()
    far_swap = Exchange(jnp.concatenate([x for pair in zip(second_sums, out_sums) for x in pair], 0))
    chain.land(*rest_ring.flying(), (out_gathers[0], "chip"), (one_parts[0], "last"), (far_swap, "other"))
    backward(1)
    rest_ring.hop()
    far_swap.cross()
    out_gathers[0].forward()
    chain.land(*rest_ring.flying()[: 1 if dp_count == 8 else 2], (far_swap, "other"), (one_parts[1], "got"))
    chain.land((out_gathers[0], "both"), (out_gathers[1], "chip"))
    first_grad = weight_grad(
        chain,
        [
            [([inputs_one[r]], qkv_grads[r]) for r in range(rows)],
            [(grad_gathers[r].pieces(), mixed[r]) for r in range(rows)],
        ],
        "grad_first",
    )
    first_ring = RingSum(first_grad, dp_count)
    one_parts[1].cross()
    out_gathers[1].forward()
    spare = 4 * slot_count
    to = [field_slots(0), field_slots(1), field_slots(2), spare_slot(spare)]
    to += [field_slots(3), spare_slot(spare + 1)]
    far_slots = dot_as(slot_matrix(to, spare + 16), far_swap.whole(), DOT_NN)
    far_slots = lax.dynamic_update_slice(
        far_slots, up_sums.reshape(4, own_width), (spare + 2, 0)
    ).astype(low)
    far_gather = DoublingGather(far_slots, dp_count)

    input_gathers, third_sums = [], []

    def third_norm(r):
        input_own, sums = row_call(
            third_kernel,
            "third_norm",
            chain,
            (tokens, *one_parts[r].terms(), grad_hiddens[r], near_tab[r]),
            [own_block(r)] + [here] * 4 + [own_table(near_tab)],
            (here, fixed_spec((8, width))),
            (lows(*block), wides(8, width)),
        )
        input_gathers.append(GroupGather(input_own))
        third_sums.append(sums)

    chain.land(*far_gather.flying(), (out_gathers[0], "core"), (out_gathers[1], "core"), (out_gathers[1], "both"))
    third_norm(0)
    far_gather.hop()
    at = jnp.stack(
        [(r * 4 + jnp.bitwise_xor(place, j)) * quarter for r in range(rows) for j in range(4)]
    ).astype(jnp.int32)
    chain.land(*first_ring.flying(), (one_parts[1], "last"), *far_gather.flying())
    out_tokens = place_pieces(chain, at, [x for gather in out_gathers for x in gather.pieces()])
    first_ring.hop()
    far_gather.hop()
    third_norm(1)
    near_swap = Exchange(jnp.concatenate(third_sums, 0))

    def columns_of(ref, at):
        return column(ref[...], at, own_width).astype(wide)

    def map_grad(left, right, field):
        right = right[:, field * slot_count : (field + 1) * slot_count, :]
        return dot_as(left[...], right.reshape(-1, own_width), DOT_TN)

    cols_state = (weight_cols, first_cols, second_cols, ema_cols)
    rows_state = [x.transpose(0, 2, 1) for x in (weight_rows, first_rows, second_rows, ema_rows)]

    rest_sum = rest_ring.total()
    chain.land(*first_ring.flying(), *far_gather.flying(), (near_swap, "other"), (input_gathers[0], "chip"))
    cols_new = adam_slabs(
        chain,
        [(0, i) for i in (5, 6, 7, 8)],
        (rest_sum,),
        lambda n, refs: columns_of(refs[0], n),
        [cols_state],
        [None],
        "adam_up",
    )
    first_ring.hop()
    near_swap.cross()
    input_gathers[0].forward()
    chain.land(*first_ring.flying(), (near_swap, "other"), (input_gathers[1], "chip"), (input_gathers[0], "core"))
    rows_new = adam_slabs(
        chain,
        [(0, i) for i in (1, 2, 3, 4)],
        (rest_sum,),
        lambda n, refs: columns_of(refs[0], 4 + n),
        [rows_state],
        [None],
        "adam_down",
    )
    first_ring.hop()
    input_gathers[1].forward()
    unit_sums = jnp.concatenate(time_sums, 0)
    moved = row_slots.transpose(1, 0, 2).reshape(-1, 1) == jnp.arange(slot_count)[None, :]
    moved = moved.astype(wide)
    time_slots = lax.dot_general(moved, unit_sums, DOT_TN, precision=highest)
    near_slots = jnp.concatenate(
        [
            dot_as(
                slot_matrix([field_slots(0), field_slots(1)], 2 * slot_count), near_swap.whole(), DOT_NN
            ),
            time_slots[:, :own_width],
            time_slots[:, 2 * own_width :],
        ],
        0,
    ).astype(low)
    near_gather = DoublingGather(near_slots, dp_count)
    far_all = far_gather.whole()
    far_sum = jnp.sum(far_all.astype(wide), axis=0)
    far_biases = jnp.sum(far_sum[: 4 * slot_count].reshape(4, slot_count, own_width), axis=1)
    bias_up_sum = far_sum[4 * slot_count + 2 : 4 * slot_count + 6]
    bias_gather = GroupGather(far_sum[4 * slot_count : 4 * slot_count + 2].astype(low))
    chain.land(*near_gather.flying(), (input_gathers[0], "both"), (input_gathers[1], "core"), (bias_gather, "chip"))
    cols_new = adam_slabs(
        chain,
        [(0, i) for i in (11, 12, 13, 14)],
        (ada_low, far_all),
        lambda n, refs: map_grad(refs[0], refs[1], n),
        [cols_state],
        [cols_new],
        "adam_far",
    )
    near_gather.hop()
    bias_gather.forward()
    input_grads = ()
    for r in range(rows):
        if r == 0:
            chain.land(*near_gather.flying(), (input_gathers[1], "both"), *first_ring.flying()[: 1 if dp_count == 8 else 2])
        else:
            chain.land(*near_gather.flying(), (bias_gather, "core"), (bias_gather, "both"))
        input_grads = (widen_row(chain, input_gathers[r].pieces(), r, rows, input_grads),)
        near_gather.hop()

    near_all = near_gather.whole()
    near_sum = jnp.sum(near_all.astype(wide).reshape(dp_count, 4, slot_count, own_width), axis=(0, 2))
    bias_cols_sum = jnp.concatenate([near_sum[2:4], bias_up_sum, near_sum[:2], far_biases], 0)
    bias_rows_sum = jnp.concatenate(bias_gather.in_order(mp_place), 1).astype(wide)
    first_sum = first_ring.total()

    def late_grad(n, refs):
        ada, time, near, first = refs
        if n < 4:
            return map_grad(ada if n < 2 else time, near, n)
        return columns_of(first, n - 4)

    new = adam_slabs(
        chain,
        [(0, i) for i in (9, 10, 3, 4, 0, 1, 2)] + [(1, 0)],
        (ada_low, time_low, near_all, first_sum),
        late_grad,
        [cols_state, rows_state],
        [cols_new, rows_new],
        "adam_late",
    )
    cols_new, rows_new = new[:4], [x.transpose(0, 2, 1) for x in new[4:]]
    bias_cols_new = adam_step(
        bias_cols, bias_cols_sum, first_bias_cols, second_bias_cols, ema_bias_cols, rate_vector
    )
    bias_rows_new = adam_step(
        bias_rows, bias_rows_sum, first_bias_rows, second_bias_rows, ema_bias_rows, rate_vector
    )
    return (out_tokens, input_grads[0], *cols_new, *rows_new, *bias_cols_new, *bias_rows_new)


def solution(mesh):
    cols, rows, bias = P(None, "dp", "mp"), P(None, "mp", "dp"), P(None, "mp")
    state = (cols, rows, bias, P())
    placed = (P("dp", None), P("dp"), P("dp", None), P("dp", None)) + state * 4
    given = (P("dp", None), P("dp", None)) + (cols,) * 4 + (rows,) * 4 + (bias,) * 4 + (P(),) * 4
    return jax.shard_map(
        per_device, mesh=mesh, in_specs=placed, out_specs=given, check_vma=False
    )
```

```python
import math

import jax
import jax.numpy as jnp
from jax import lax
from jax.experimental import pallas as pl
from jax.experimental.pallas import tpu as pltpu
from jax.sharding import PartitionSpec as P

HEAD_DIM = 72
STEP = 10
UNIT = 64
REACH = 192


highest = lax.Precision.HIGHEST
beta_one = 0.9
beta_two = 0.999
adam_eps = 1e-08
decay_rate = 0.1
rate_matrix = 0.05
rate_vector = 0.5
ema_keep = 0.7
norm_eps = 1e-06
neg_large = -1e30
score_scale = HEAD_DIM**-0.5
low = jnp.bfloat16
wide = jnp.float32

DOT_NN = (((1,), (0,)), ((), ()))
DOT_NT = (((1,), (1,)), ((), ()))
DOT_TN = (((0,), (0,)), ((), ()))

COST = 0
VMEM_GRANT = 58 * 2**20
SMEM_SPEC = pl.BlockSpec(memory_space=pltpu.SMEM)

CORE_SWAP = [(i, i ^ 1) for i in range(4)]
CHIP_SWAP = [(i, i ^ 2) for i in range(4)]


def dot_as(left, right, dims):
    return lax.dot_general(left, right, dims, preferred_element_type=wide)


def ring_order(count):
    return list(range(0, count, 2)) + list(range(count - 1, 0, -2))


def ring_perms(count):
    order = ring_order(count)
    onward = [(order[i], order[(i + 1) % count]) for i in range(count)]
    return onward, [(b, a) for a, b in onward]


def ring_spot(count):
    me = lax.axis_index("dp")
    return jnp.where(me % 2 == 0, me // 2, count - 1 - me // 2)


def ring_at(spot, count):
    spot = spot % count
    return jnp.where(spot < count // 2, 2 * spot, 2 * (count - 1 - spot) + 1)


def ring_places(rows, count):
    spot = ring_spot(count)
    back = [0]
    for hop in range(1, count // 2):
        back += [-hop, hop]
    at = ring_at(spot + jnp.array(back + [count // 2] * 2), count) * rows
    return (at + jnp.array([0] * len(back) + [0, rows // 32 * 16])).astype(jnp.int32)


def place_pieces(chain, at, pieces, cuts=None):
    parts = [(n, *cut) for n, piece in enumerate(pieces) for cut in cuts or [(0, piece.shape[0])]]
    whole = (sum(count for _, _, count in parts),) + pieces[0].shape[1:]
    at = chain.tie(at)

    def body(at_ref, *refs):
        out_ref, held, sem_in, sem_out = refs[-4:]
        arrive, leave = [], []
        base = 0
        for i, (n, start, count) in enumerate(parts):
            spot = held.at[pl.ds(base, count)]
            piece = refs[n].at[pl.ds(start, count)]
            arrive.append(pltpu.make_async_copy(piece, spot, sem_in.at[i]))
            to = out_ref.at[pl.ds(pl.multiple_of(at_ref[i], 16), count)]
            leave.append(pltpu.make_async_copy(spot, to, sem_out.at[i]))
            base += count
        for copy in arrive:
            copy.start()
        for first, second in zip(arrive, leave):
            first.wait()
            second.start()
        for copy in leave:
            copy.wait()

    out = pl.pallas_call(
        body,
        out_shape=jax.ShapeDtypeStruct(whole, pieces[0].dtype),
        in_specs=[SMEM_SPEC] + [pl.BlockSpec(memory_space=pl.ANY)] * len(pieces),
        out_specs=pl.BlockSpec(memory_space=pl.ANY),
        scratch_shapes=[pltpu.VMEM(whole, pieces[0].dtype)]
        + [pltpu.SemaphoreType.DMA((len(parts),))] * 2,
        compiler_params=pltpu.CompilerParams(vmem_limit_bytes=VMEM_GRANT),
        cost_estimate=pl.CostEstimate(flops=1, bytes_accessed=1, transcendentals=0),
        name="place_pieces",
    )(at, *pieces)
    return chain.close(out)


class Chain:
    def __init__(self, token):
        self.token = token

        self.landing = []

    def tie(self, *arrays):
        self.token, *arrays = lax.optimization_barrier((self.token, *arrays))
        return arrays[0] if len(arrays) == 1 else tuple(arrays)

    def land(self, *transfers):
        self.landing += transfers

    def close(self, *arrays):
        landing, self.landing = self.landing, []
        values = self.tie(*arrays, *[getattr(held, name) for held, name in landing])
        values = values if isinstance(values, tuple) else (values,)
        for (held, name), value in zip(landing, values[len(arrays) :]):
            setattr(held, name, value)
        return values[0] if len(arrays) == 1 else values[: len(arrays)]


class RingSum:
    def __init__(self, parts, count):
        self.parts, self.count = parts, count
        self.left = count // 2 - 1 if count in (4, 8) else 0
        if self.left:
            self.rows = parts.shape[0] // count
            self.onward, self.backward = ring_perms(count)
            self.spot = ring_spot(count)
            self.send(self.chunk(count // 2), self.chunk(1 - count // 2))

    def chunk(self, ahead):
        at = ring_at(self.spot + ahead, self.count) * self.rows
        return lax.dynamic_slice_in_dim(self.parts, at, self.rows, 0).astype(wide)

    def send(self, ahead, behind):
        self.ahead = lax.ppermute(ahead.astype(low), "dp", self.onward)
        if behind is not None:
            self.behind = lax.ppermute(behind.astype(low), "dp", self.backward)

    def flying(self):
        return [(self, "ahead"), (self, "behind")] if self.count in (4, 8) else []

    def hop(self):
        if not self.left:
            return
        ahead = self.ahead.astype(wide) + self.chunk(self.left)
        behind = None
        if self.left > 1:
            behind = self.behind.astype(wide) + self.chunk(1 - self.left)
        self.send(ahead, behind)
        self.left -= 1

    def total(self):
        if self.count not in (4, 8):
            return lax.psum_scatter(self.parts, "dp", scatter_dimension=0, tiled=True).astype(wide)
        return self.ahead.astype(wide) + self.behind.astype(wide) + self.chunk(0)


class GroupSum:
    def __init__(self, kept, sent):
        self.kept, self.got = kept, lax.ppermute(sent, "mp", CORE_SWAP)

    def cross(self):
        quarter = self.kept.shape[0] // 2
        passed = (self.kept[quarter:] + self.got[quarter:].astype(wide)).astype(low)
        self.last = lax.ppermute(passed, "mp", CHIP_SWAP)

    def terms(self):
        return self.kept, self.got, self.last


class GroupGather:
    def __init__(self, own):
        self.own = own
        self.chip = lax.ppermute(own, "mp", CHIP_SWAP)
        self.core = lax.ppermute(own, "mp", CORE_SWAP)

    def forward(self):
        self.both = lax.ppermute(self.chip, "mp", CORE_SWAP)

    def flying(self):
        return [(self, "chip"), (self, "core")]

    def pieces(self):
        return [self.own, self.chip, self.core, self.both]

    def in_order(self, mp_place):
        return in_group_order([self.own, self.core, self.chip, self.both], mp_place)


class DoublingGather:
    def __init__(self, shard, count):
        self.shard, self.count = shard, count
        self.known, self.step = shard[None], count // 2 if count in (4, 8) else 0
        self.send()

    def send(self):
        if self.step:
            swap = [(i, i ^ self.step) for i in range(self.count)]
            self.got = lax.ppermute(self.known, "dp", swap)

    def join(self, got):
        second = lax.axis_index("dp") // self.step % 2 == 1
        pair = [jnp.where(second, got, self.known), jnp.where(second, self.known, got)]
        self.known = jnp.stack(pair, 1).reshape((-1,) + self.shard.shape)
        self.step //= 2

    def flying(self):
        return [(self, "got")] if self.step else []

    def hop(self):
        if self.step > 1:
            self.join(self.got)
            self.send()

    def whole(self):
        if self.step:
            self.join(self.got)
        if self.count not in (4, 8):
            return lax.all_gather(self.shard, "dp", axis=0, tiled=False)
        return self.known


class HalvingSum:
    def __init__(self, parts, count):
        self.parts, self.count, self.step = parts, count, 1
        self.send()

    def send(self):
        pairs = self.parts.reshape((self.parts.shape[0] // 2, 2) + self.parts.shape[1:])
        bit = lax.axis_index("dp") // self.step % 2
        sent = lax.dynamic_index_in_dim(pairs, 1 - bit, 1, keepdims=False).astype(low)
        self.kept = lax.dynamic_index_in_dim(pairs, bit, 1, keepdims=False).astype(wide)
        swap = [(i, i ^ self.step) for i in range(self.count)]
        self.got = lax.ppermute(sent, "dp", swap)

    def flying(self):
        return [(self, "got")] if self.step < self.count else []

    def hop(self):
        if self.step < self.count:
            self.parts = self.kept + self.got.astype(wide)
            self.step *= 2
            if self.step < self.count:
                self.send()


class RingGather:
    def __init__(self, shard, count):
        self.count, self.left = count, count // 2 - 1
        self.onward, self.backward = ring_perms(count)
        self.pieces = [shard]
        self.send(shard, shard)

    def send(self, ahead, behind):
        self.ahead = lax.ppermute(ahead, "dp", self.onward)
        self.behind = lax.ppermute(behind, "dp", self.backward)

    def flying(self):
        return [(self, "ahead"), (self, "behind")]

    def hop(self):
        ahead, behind = self.ahead, self.behind
        self.pieces += [ahead, behind]
        if self.left > 1:
            self.send(ahead, behind)
        elif self.left == 1:
            cut = ahead.shape[0] // 32 * 16
            self.send(ahead[:cut], behind[cut:])
        self.left -= 1

    def place(self, chain):
        while self.left >= 0:
            self.hop()
        return place_pieces(chain, ring_places(self.pieces[0].shape[0], self.count), self.pieces)


def share_hop(known, reach, count):
    return known + lax.ppermute(known, "dp", [(i, i ^ reach) for i in range(count)])


def in_group_order(pieces, place):
    stacked = jnp.stack(pieces, 0)
    return [
        lax.dynamic_index_in_dim(stacked, jnp.bitwise_xor(place, j), 0, keepdims=False)
        for j in range(4)
    ]


def key_windows(row_len, block):
    return [
        (at, max(0, at - REACH), min(row_len, at + block + REACH))
        for at in range(0, row_len, block)
    ]


def relative_at(place, j, block):
    return pl.multiple_of(jnp.bitwise_xor(place, j) * block, block)


def attend_forward_kernel(
    place_ref, qkv_ref, seg_col_ref, seg_row_ref, w_ref, out_ref, kept_ref, sent_ref, q_s, k_s, v_s, *, heads
):
    row_len = qkv_ref.shape[0]
    width = heads * HEAD_DIM
    block = row_len // 4
    place = place_ref[0]
    for j in range(4):
        at = relative_at(place, j, block)
        to = slice(j * block, (j + 1) * block)
        for h in range(heads):
            c = h * HEAD_DIM
            q_s[h, to, :] = qkv_ref[pl.ds(at, block), c : c + HEAD_DIM]
            k_s[h, to, :] = qkv_ref[pl.ds(at, block), width + c : width + c + HEAD_DIM]
            v_s[h, to, :] = qkv_ref[pl.ds(at, block), 2 * width + c : 2 * width + c + HEAD_DIM]
    for j, (at, start, stop) in enumerate(key_windows(row_len, block)):
        same = seg_col_ref[start:stop, :] == seg_row_ref[:, at : at + block]
        mixed = []
        for h in range(heads):
            scores = dot_as(k_s[h, start:stop, :], q_s[h, at : at + block, :], DOT_NT)
            scores = jnp.where(same, scores, neg_large)
            top = jnp.max(scores, axis=0, keepdims=True)
            weights = jnp.exp((scores - top) * score_scale)
            total = jnp.sum(weights, axis=0, keepdims=True)
            gathered = dot_as(v_s[h, start:stop, :], weights.astype(low), DOT_TN)
            mixed.append(gathered * (1.0 / total))
        out_ref[pl.ds(relative_at(place, j, block), block), :] = (
            jnp.concatenate(mixed, axis=0).T.astype(low)
        )
    w_out = w_ref[:, w_ref.shape[1] - width :]
    half = row_len // 2
    kept_ref[...] = dot_as(out_ref[:half, :], w_out, DOT_NT)
    sent_ref[...] = dot_as(out_ref[half:, :], w_out, DOT_NT).astype(low)


def attend_backward_kernel(
    place_ref, qkv_ref, g0_ref, g1_ref, g2_ref, g3_ref, seg_col_ref, seg_row_ref, w_ref,
    out_ref, kept_ref, sent_ref, sums_ref, q_s, k_s, v_s, g_s, dk_s, dv_s, *, heads
):
    row_len = qkv_ref.shape[0]
    width = heads * HEAD_DIM
    block = row_len // 4
    place = place_ref[0]
    dk_s[...] = jnp.zeros_like(dk_s)
    dv_s[...] = jnp.zeros_like(dv_s)
    w_out = w_ref[:, 3 * width :]
    for j, g_ref in enumerate((g0_ref, g1_ref, g2_ref, g3_ref)):
        grad = dot_as(g_ref[...], w_out, DOT_NN).astype(low)
        at = relative_at(place, j, block)
        for h in range(heads):
            g_s[h, pl.ds(at, block), :] = grad[:, h * HEAD_DIM : (h + 1) * HEAD_DIM]
    for j in range(4):
        at = relative_at(place, j, block)
        to = slice(j * block, (j + 1) * block)
        for h in range(heads):
            c = h * HEAD_DIM
            q_s[h, to, :] = qkv_ref[pl.ds(at, block), c : c + HEAD_DIM]
            k_s[h, to, :] = qkv_ref[pl.ds(at, block), width + c : width + c + HEAD_DIM]
            v_s[h, to, :] = qkv_ref[pl.ds(at, block), 2 * width + c : 2 * width + c + HEAD_DIM]
    for j, (at, start, stop) in enumerate(key_windows(row_len, block)):
        same = seg_col_ref[start:stop, :] == seg_row_ref[:, at : at + block]
        grads = []
        for h in range(heads):
            query = q_s[h, at : at + block, :]
            grad = g_s[h, at : at + block, :]
            keys = k_s[h, start:stop, :]
            scores = jnp.where(same, dot_as(keys, query, DOT_NT), neg_large)
            top = jnp.max(scores, axis=0, keepdims=True)
            weights = jnp.exp((scores - top) * score_scale)
            probs = weights * (1.0 / jnp.sum(weights, axis=0, keepdims=True))
            grad_probs = dot_as(v_s[h, start:stop, :], grad, DOT_NT)
            inner = jnp.sum(grad_probs * probs, axis=0, keepdims=True)
            grad_scores = (probs * (grad_probs - inner)).astype(low)
            dv_s[h, start:stop, :] += dot_as(probs.astype(low), grad, DOT_NN)
            dk_s[h, start:stop, :] += dot_as(grad_scores, query, DOT_NN)
            grads.append(dot_as(keys, grad_scores, DOT_TN) * score_scale)
        out_ref[pl.ds(relative_at(place, j, block), block), 0:width] = (
            jnp.concatenate(grads, axis=0).T.astype(low)
        )
    for j in range(4):
        at = slice(j * block, (j + 1) * block)
        to = relative_at(place, j, block)
        out_ref[pl.ds(to, block), width : 2 * width] = jnp.concatenate(
            [(dk_s[h, at, :] * score_scale).astype(low) for h in range(heads)], axis=1
        )
        out_ref[pl.ds(to, block), 2 * width : 3 * width] = jnp.concatenate(
            [dv_s[h, at, :].astype(low) for h in range(heads)], axis=1
        )
    half = row_len // 2
    w_qkv = w_ref[:, : 3 * width]
    kept_ref[...] = dot_as(out_ref[:half, :], w_qkv, DOT_NT)
    sent_ref[...] = dot_as(out_ref[half:, :], w_qkv, DOT_NT).astype(low)
    for u in range(row_len // UNIT):
        sums_ref[u : u + 1, :] = jnp.sum(
            out_ref[u * UNIT : (u + 1) * UNIT, :].astype(wide), axis=0, keepdims=True
        )


def shape_of(shape, kind):
    return jax.ShapeDtypeStruct(shape, kind)


def attend_forward(chain, qkv, seg_row, weights):
    row_len, width = qkv.shape[0], qkv.shape[1] // 3
    heads = width // HEAD_DIM
    full = weights.shape[0]
    args = (qkv, seg_row.reshape(row_len, 1), seg_row.reshape(1, row_len), weights)
    shapes = (
        shape_of((row_len, width), low),
        shape_of((row_len // 2, full), wide),
        shape_of((row_len // 2, full), low),
    )

    def body(*refs):
        attend_forward_kernel(*refs, heads=heads)

    return row_call(
        body,
        "attend_forward",
        chain,
        args,
        [fixed_spec(arg.shape) for arg in args[:3]]
        + [pl.BlockSpec((full, weights.shape[1] // 3), lambda i, p: (0, 2))],
        tuple(fixed_spec(shape.shape) for shape in shapes),
        shapes,
        scratch=[pltpu.VMEM((heads, row_len, HEAD_DIM), low)] * 3,
        flops=4 * row_len * 640 * width + 2 * row_len * width * full,
        exps=heads * row_len * 640,
    )


def attend_backward(chain, qkv, grads, seg_row, weights):
    row_len, width = qkv.shape[0], qkv.shape[1] // 3
    heads = width // HEAD_DIM
    full = weights.shape[0]
    args = (qkv, *grads, seg_row.reshape(row_len, 1), seg_row.reshape(1, row_len), weights)
    shapes = (
        shape_of((row_len, 3 * width), low),
        shape_of((row_len // 2, full), wide),
        shape_of((row_len // 2, full), low),
        shape_of((row_len // UNIT, 3 * width), wide),
    )

    def body(*refs):
        attend_backward_kernel(*refs, heads=heads)

    return row_call(
        body,
        "attend_backward",
        chain,
        args,
        [fixed_spec(arg.shape) for arg in args],
        tuple(fixed_spec(shape.shape) for shape in shapes),
        shapes,
        scratch=[pltpu.VMEM((heads, row_len, HEAD_DIM), low)] * 4
        + [pltpu.VMEM((heads, row_len, HEAD_DIM), wide)] * 2,
        flops=10 * row_len * 640 * width + 8 * row_len * width * full,
        exps=heads * row_len * 640,
    )


def norm_parts(values):
    centre = values - jnp.mean(values, axis=-1, keepdims=True)
    inverse = lax.rsqrt(jnp.mean(centre * centre, axis=-1, keepdims=True) + norm_eps)
    return centre * inverse, inverse


def norm_back(normed, inverse, grad):
    return inverse * (
        grad
        - jnp.mean(grad, axis=-1, keepdims=True)
        - normed * jnp.mean(grad * normed, axis=-1, keepdims=True)
    )


def unit_rows(ref):
    return [(u, slice(u * UNIT, (u + 1) * UNIT)) for u in range(ref.shape[0] // UNIT)]


def column(values, index, width):
    return values[:, index * width : (index + 1) * width]


def open_kernel(
    place_ref, x0_ref, x1_ref, tab0_ref, tab1_ref, add0_ref, add1_ref, w_ref, a_ref, qkv_ref
):
    width = x0_ref.shape[1]
    quarter = x0_ref.shape[0]
    for j, (x_ref, tab_ref) in enumerate(((x0_ref, tab0_ref), (x1_ref, tab1_ref))):
        for u, at in unit_rows(x_ref):
            normed, _ = norm_parts(x_ref[at, :].astype(wide))
            table = tab_ref[0, u : u + 1, :]
            out = normed * (1.0 + column(table, 1, width)) + column(table, 0, width)
            a_ref[j * quarter + u * UNIT : j * quarter + (u + 1) * UNIT, :] = out.astype(low)
    qkv = dot_as(a_ref[...], w_ref[:, : qkv_ref.shape[1]], DOT_NN)
    for j, add_ref in enumerate((add0_ref, add1_ref)):
        for u in range(quarter // UNIT):
            at = slice(j * quarter + u * UNIT, j * quarter + (u + 1) * UNIT)
            qkv_ref[at, :] = (qkv[at, :] + add_ref[0, u : u + 1, :]).astype(low)


def first_kernel(place_ref, x_ref, kept_ref, got_ref, passed_ref, bias_ref, tab_ref, att_ref, hid_ref, a_ref):
    width = x_ref.shape[1]
    for u, at in unit_rows(x_ref):
        table = tab_ref[0, u : u + 1, :]
        attended = kept_ref[at, :] + got_ref[at, :].astype(wide) + passed_ref[at, :].astype(wide)
        attended = attended + bias_ref[0:1, :]
        hidden = x_ref[at, :].astype(wide) + column(table, 0, width) * attended
        normed, _ = norm_parts(hidden)
        att_ref[at, :] = attended
        hid_ref[at, :] = hidden
        a_ref[at, :] = (normed * (1.0 + column(table, 2, width)) + column(table, 1, width)).astype(low)


def down_back_kernel(place_ref, cot0_ref, cot1_ref, tab0_ref, tab1_ref, w_ref, grad_ref, dm_ref):
    width = cot0_ref.shape[1]
    quarter = cot0_ref.shape[0]
    for j, (cot_ref, tab_ref) in enumerate(((cot0_ref, tab0_ref), (cot1_ref, tab1_ref))):
        for u, at in unit_rows(cot_ref):
            gate = column(tab_ref[0, u : u + 1, :], 3, width)
            out = (cot_ref[at, :].astype(wide) * gate).astype(low)
            grad_ref[j * quarter + u * UNIT : j * quarter + (u + 1) * UNIT, :] = out
    dm_ref[...] = dot_as(grad_ref[...], w_ref[...], DOT_NN).astype(low)


def gelu_both(values):
    scale = math.sqrt(2.0 / math.pi)
    square = values * values
    turned = jnp.tanh(scale * values * (1.0 + 0.044715 * square))
    upper = 0.5 * (1.0 + turned)
    slope = upper + 0.5 * values * (1.0 - turned * turned) * scale * (1.0 + 3 * 0.044715 * square)
    return values * upper, slope


def up_kernel(
    place_ref, a0_ref, a1_ref, a2_ref, a3_ref, dm_ref, bias_ref, w_ref, m_ref, dz_ref, kept_ref, sent_ref, sums_ref, a_s
):
    step = pl.program_id(0)
    quarter = a0_ref.shape[0]
    for j, piece in enumerate((a0_ref, a1_ref, a2_ref, a3_ref)):

        @pl.when(step == j // 2)
        def _(piece=piece, j=j):
            a_s[j % 2 * quarter : (j % 2 + 1) * quarter, :] = piece[...]

    sums = jnp.zeros(sums_ref.shape[1:], wide)
    for j in range(2):
        at = slice(j * quarter, (j + 1) * quarter)
        inner = dot_as(a_s[at, :], w_ref[...], DOT_NN) + bias_ref[...]
        active, slope = gelu_both(inner)
        m_ref[at, :] = active.astype(low)
        grad = (dm_ref[at, :].astype(wide) * slope).astype(low)
        dz_ref[at, :] = grad
        sums = sums + jnp.sum(grad.astype(wide).reshape(-1, 8, grad.shape[1]), axis=0)
    sums_ref[0] = sums
    back = dot_as(dz_ref[...], w_ref[...], DOT_NT)

    @pl.when(step == 0)
    def _():
        kept_ref[...] = back

    @pl.when(step == 1)
    def _():
        sent_ref[...] = back.astype(low)


def down_kernel(place_ref, m_ref, w_ref, kept_ref, sent_ref):
    step = pl.program_id(0)
    out = dot_as(m_ref[...], w_ref[...], DOT_NT)

    @pl.when(step == 0)
    def _():
        kept_ref[...] = out

    @pl.when(step == 1)
    def _():
        sent_ref[...] = out.astype(low)


def second_kernel(
    place_ref, cot_ref, kept_ref, got_ref, passed_ref, hid_ref, att_ref, tab_ref, gh_ref, ga_ref, sums_ref
):
    width = cot_ref.shape[1]
    bias = jnp.zeros((1, width), wide)
    sums_ref[...] = jnp.zeros_like(sums_ref)
    for u, at in unit_rows(cot_ref):
        table = tab_ref[0, u : u + 1, :]
        grad_two = kept_ref[at, :] + got_ref[at, :].astype(wide) + passed_ref[at, :].astype(wide)
        normed, inverse = norm_parts(hid_ref[at, :])
        grad = cot_ref[at, :].astype(wide) + norm_back(
            normed, inverse, grad_two * (1.0 + column(table, 2, width))
        )
        grad_att = grad * column(table, 0, width)
        gh_ref[at, :] = grad
        ga_ref[at, :] = grad_att.astype(low)
        bias = bias + jnp.sum(grad_att, axis=0, keepdims=True)
        sums_ref[u : u + 1, :] = jnp.sum(grad * att_ref[at, :], axis=0, keepdims=True)
        sums_ref[4 + u : 5 + u, :] = jnp.sum(grad_two, axis=0, keepdims=True)
        sums_ref[8 + u : 9 + u, :] = jnp.sum(grad_two * normed, axis=0, keepdims=True)
    sums_ref[12:13, :] = bias


def out_kernel(place_ref, bias_ref, *refs):
    rows = (len(refs) - 2) // 7
    out_ref, sums_ref = refs[-2:]
    quarter, width = refs[0].shape
    total = jnp.zeros((1, width), wide)
    other = jnp.zeros((1, width), wide)
    sums_ref[...] = jnp.zeros_like(sums_ref)
    for r in range(rows):
        cot_ref, kept_ref, got_ref, passed_ref, hid_ref, tab_ref, second_ref = refs[7 * r : 7 * r + 7]
        for u, at in unit_rows(cot_ref):
            gate = column(tab_ref[0, u : u + 1, :], 3, width)
            mlp = kept_ref[at, :] + got_ref[at, :].astype(wide) + passed_ref[at, :].astype(wide)
            mlp = mlp + bias_ref[1:2, :]
            out_ref[r * quarter + u * UNIT : r * quarter + (u + 1) * UNIT, :] = (
                hid_ref[at, :] + gate * mlp
            ).astype(low)
            cot = cot_ref[at, :].astype(wide)
            sums_ref[8 * r + u : 8 * r + u + 1, :] = jnp.sum(cot * mlp, axis=0, keepdims=True)
            total = total + jnp.sum(cot, axis=0, keepdims=True) * gate
        other = other + second_ref[12:13, :]
    tail = jnp.concatenate([other, total, jnp.zeros((14, width), wide)], axis=0)
    out_ref[rows * quarter :, :] = tail.astype(low)


def third_kernel(place_ref, *refs):
    rows = (len(refs) - 2) // 6
    out_ref, sums_ref = refs[-2:]
    quarter, width = refs[0].shape
    for r in range(rows):
        x_ref, kept_ref, got_ref, passed_ref, gh_ref, tab_ref = refs[6 * r : 6 * r + 6]
        for u, at in unit_rows(x_ref):
            grad_one = kept_ref[at, :] + got_ref[at, :].astype(wide) + passed_ref[at, :].astype(wide)
            normed, inverse = norm_parts(x_ref[at, :].astype(wide))
            table = tab_ref[0, u : u + 1, :]
            back = norm_back(normed, inverse, grad_one * (1.0 + column(table, 1, width)))
            out_ref[r * quarter + u * UNIT : r * quarter + (u + 1) * UNIT, :] = (
                gh_ref[at, :] + back
            ).astype(low)
            n = 8 * r + u
            sums_ref[n : n + 1, :] = jnp.sum(grad_one, axis=0, keepdims=True)
            sums_ref[n + 4 : n + 5, :] = jnp.sum(grad_one * normed, axis=0, keepdims=True)


def row_call(
    body, name, chain, args, in_specs, out_specs, out_shape, grid=1, scratch=(), flops=0, exps=0, aliases=None, prefetch=None
):
    moved = sum(math.prod(a.shape) * a.dtype.itemsize for a in args)
    shapes = out_shape if isinstance(out_shape, tuple) else (out_shape,)
    moved += sum(math.prod(o.shape) * o.dtype.itemsize for o in shapes)
    prefetch = chain.token if prefetch is None else chain.tie(prefetch)
    out = pl.pallas_call(
        body,
        grid_spec=pltpu.PrefetchScalarGridSpec(
            num_scalar_prefetch=1,
            grid=(grid,),
            in_specs=in_specs,
            out_specs=out_specs,
            scratch_shapes=scratch,
        ),
        out_shape=out_shape,
        input_output_aliases=aliases or {},
        compiler_params=pltpu.CompilerParams(vmem_limit_bytes=VMEM_GRANT),
        cost_estimate=pl.CostEstimate(
            flops=int(COST * flops) + 1, bytes_accessed=int(COST * moved) + 1, transcendentals=0
        ),
        name=name,
    )(prefetch, *args)
    return chain.close(*out) if isinstance(out_shape, tuple) else chain.close(out)


def fixed_spec(shape):
    return pl.BlockSpec(shape, lambda *_: (0,) * len(shape))


def unit_tables(chain, mp_arg, onehot, pieces, fields, group):
    units, slots = onehot.shape
    own = pieces[0].shape[1] // fields
    shape = (units // group, group, fields * 4 * own)

    def body(mp_ref, hot_ref, *refs):
        out_ref = refs[-1]
        mp_place = mp_ref[0]
        for i, piece in enumerate(refs[:-1]):
            spread = dot_as(hot_ref[...], piece[...], DOT_NN)
            for j in range(4):

                @pl.when(jnp.bitwise_xor(mp_place, i) == j)
                def _(spread=spread, j=j):
                    for f in range(fields):
                        at = f * 4 * own + j * own
                        values = column(spread, f, own)
                        for n in range(units // group):
                            out_ref[n, :, at : at + own] = values[n * group : (n + 1) * group, :]

    return row_call(
        body,
        "unit_tables",
        chain,
        (onehot, *pieces),
        [fixed_spec(onehot.shape)] + [fixed_spec(pieces[0].shape)] * 4,
        fixed_spec(shape),
        shape_of(shape, wide),
        flops=8 * units * slots * own * fields,
        prefetch=mp_arg,
    )


def weight_grad(chain, pairs, name):
    depth = pairs[0][0][0][0].shape[1]
    tile = depth // 3
    widths = [pair[0][1].shape[1] for pair in pairs]
    args, specs, plan = [], [], []
    flops = 0
    for pair in pairs:
        rows = []
        for left, right in pair:
            rows.append((len(args), len(left)))
            args += list(left) + [right]
            specs += [pl.BlockSpec((piece.shape[0], tile), lambda i, p: (0, i)) for piece in left]
            specs.append(fixed_spec(right.shape))
            flops += 2 * depth * math.prod(right.shape)
        plan.append(rows)

    def body(place_ref, *refs):
        out_ref = refs[-1]
        at = 0
        for rows, cols in zip(plan, widths):
            total = None
            for first, count in rows:
                left = [ref[...] for ref in refs[first : first + count]]
                left = left[0] if count == 1 else jnp.concatenate(left, axis=0)
                part = dot_as(left, refs[first + count][...], DOT_TN)
                total = part if total is None else total + part
            out_ref[:, at : at + cols] = total.astype(low)
            at += cols

    return row_call(
        body,
        name,
        chain,
        args,
        specs,
        pl.BlockSpec((tile, sum(widths)), lambda i, p: (i, 0)),
        shape_of((depth, sum(widths)), low),
        grid=3,
        flops=flops,
    )


def widen_rows(chain, pieces, rows):
    quarter, width = pieces[0].shape[0] // rows, pieces[0].shape[1]

    def body(place_ref, *refs):
        out_ref, wide_s, sems = refs[-3:]
        copies = []
        for r in range(rows):
            for j, piece in enumerate(refs[:4]):
                held = wide_s.at[r, j]
                held[...] = piece[r * quarter : (r + 1) * quarter, :].astype(wide)
                at = (r * 4 + jnp.bitwise_xor(place_ref[0], j)) * quarter
                to = out_ref.at[pl.ds(pl.multiple_of(at, quarter), quarter)]
                copies.append(pltpu.make_async_copy(held, to, sems.at[r, j]))
                copies[-1].start()
        for copy in copies:
            copy.wait()

    return row_call(
        body,
        "widen_rows",
        chain,
        tuple(pieces),
        [fixed_spec(pieces[0].shape)] * 4,
        pl.BlockSpec(memory_space=pl.ANY),
        shape_of((rows * 4 * quarter, width), wide),
        scratch=[pltpu.VMEM((rows, 4, quarter, width), wide), pltpu.SemaphoreType.DMA((rows, 4))],
    )


def adam_step(weight, gradient, first_old, second_old, ema_old, step_rate):
    first_new = beta_one * first_old + (1.0 - beta_one) * gradient
    second_new = beta_two * second_old + (1.0 - beta_two) * gradient * gradient
    first_hat = first_new * (1.0 / (1.0 - beta_one**STEP))
    second_hat = second_new * (1.0 / (1.0 - beta_two**STEP))
    weight_new = weight - step_rate * (
        first_hat / (jnp.sqrt(second_hat) + adam_eps) + decay_rate * weight
    )
    ema_new = ema_keep * ema_old + (1.0 - ema_keep) * weight_new
    return (first_new, second_new, weight_new, ema_new)


def adam_slabs(chain, plan, grads, make_grad, groups, before, name):
    slab = groups[0][0].shape[1:]
    count, held = len(plan), 4 * len(groups)

    def body(place_ref, *refs):
        grad_refs, state_refs = refs[: len(grads)], refs[len(grads) : len(grads) + held]
        out_refs = refs[-held - 4 : -4]
        old_s, new_s, arrive, leave = refs[-4:]
        reads, writes = [], []
        for n, (group, at) in enumerate(plan):
            for i in range(4):
                old = state_refs[4 * group + i].at[at]
                reads.append(pltpu.make_async_copy(old, old_s.at[n, i], arrive.at[n, i]))
                new = out_refs[4 * group + i].at[at]
                writes.append(pltpu.make_async_copy(new_s.at[n, i], new, leave.at[n, i]))
        for copy in reads:
            copy.start()
        for n in range(count):
            grad = make_grad(n, grad_refs)
            for copy in reads[4 * n : 4 * n + 4]:
                copy.wait()
            weight, *old = [old_s[n, i] for i in range(4)]
            for i, value in enumerate(adam_step(weight, grad, *old, rate_matrix)):
                new_s[n, i] = value
            for copy in writes[4 * n : 4 * n + 4]:
                copy.start()
        for copy in writes:
            copy.wait()

    flat = [x for group in groups for x in group]
    kept, aliases = [], {}
    for g, arrays in enumerate(before):
        for i, x in enumerate(arrays or ()):
            aliases[1 + len(grads) + held + len(kept)] = 4 * g + i
            kept.append(x)
    anywhere = pl.BlockSpec(memory_space=pl.ANY)
    return row_call(
        body,
        name,
        chain,
        (*grads, *flat, *kept),
        [fixed_spec(grad.shape) for grad in grads] + [anywhere] * (held + len(kept)),
        (anywhere,) * held,
        tuple(shape_of(x.shape, wide) for x in flat),
        scratch=[pltpu.VMEM((count, 4) + slab, wide)] * 2 + [pltpu.SemaphoreType.DMA((count, 4))] * 2,
        aliases=aliases,
    )


def per_device(
    tokens,
    seg_ids,
    time_steps,
    cotangent,
    weight_cols,
    weight_rows,
    bias_cols,
    bias_rows,
    first_cols,
    first_rows,
    first_bias_cols,
    first_bias_rows,
    second_cols,
    second_rows,
    second_bias_cols,
    second_bias_rows,
    ema_cols,
    ema_rows,
    ema_bias_cols,
    ema_bias_rows,
):
    own_width = weight_cols.shape[2]
    own_depth = weight_cols.shape[1]
    width = tokens.shape[1]
    rows = time_steps.shape[0]
    slots = time_steps.shape[1]
    token_count = tokens.shape[0]
    row_len = token_count // rows
    units = row_len // UNIT
    quarter = row_len // 4
    own_units = units // 4
    dp_count = width // own_depth
    dp_place = lax.axis_index("dp")
    slot_count = rows * slots
    mp_place = lax.axis_index("mp")
    core, chip = mp_place % 2, mp_place // 2
    place = (2 * core + chip).astype(jnp.int32)
    place_arg = place.reshape(1)

    chain = Chain(place_arg)

    ring = dp_count in (4, 8)
    known = jnp.zeros((dp_count,) + time_steps.shape, time_steps.dtype)
    known = lax.dynamic_update_slice_in_dim(known, time_steps[None], dp_place, 0)
    known, weight_cols, weight_rows = lax.optimization_barrier((known, weight_cols, weight_rows))
    cols_low = weight_cols.astype(low)
    own_rows = weight_rows.astype(low).transpose(2, 0, 1).reshape(own_depth, 5 * own_width)
    own_first = jnp.concatenate([cols_low[0], cols_low[1], cols_low[2], own_rows[:, :own_width]], 1)
    own_rest = jnp.concatenate([cols_low[5 + i] for i in range(4)] + [own_rows[:, own_width:]], 1)

    half_width = width // 2
    feature = dp_place * own_depth + jnp.arange(own_depth)
    is_cos = feature < half_width
    index = jnp.where(is_cos, feature, feature - half_width).astype(wide)
    frequency = jnp.exp(-math.log(10000.0) * index / half_width)

    def embed(steps):
        angles = steps.astype(wide)[:, None] * frequency[None, :]
        table = jnp.where(is_cos[None, :], jnp.cos(angles), jnp.sin(angles))
        return table.astype(low), jax.nn.silu(table).astype(low)

    near_maps = [jnp.concatenate([cols_low[i], cols_low[i + 1]], 1) for i in (9, 3)]
    far_maps = jnp.concatenate([cols_low[i] for i in (11, 12, 13, 14)], 1)

    def slot_products(pairs):
        out = jnp.concatenate([dot_as(left, maps, DOT_NN).astype(low) for left, maps in pairs], 1)
        return out.reshape(dp_count, rows * slots, -1)

    if ring:
        known = share_hop(known, 1, dp_count)
        known, own_first = lax.optimization_barrier((known, own_first))
        first_gather = RingGather(own_first, dp_count)

        def beside(value):
            value, first_gather.ahead, first_gather.behind = lax.optimization_barrier(
                (value, first_gather.ahead, first_gather.behind)
            )
            if first_gather.left > 0:
                first_gather.hop()
            return value

        known = beside(share_hop(known, 2, dp_count))
        if dp_count == 8:
            known = share_hop(known, 4, dp_count)
        time_low, ada_low = embed(known.reshape(-1))
        near = beside(slot_products([(ada_low, near_maps[0]), (time_low, near_maps[1])]))
        near = HalvingSum(near, dp_count)
        near.hop()
        if dp_count == 8:
            near.parts = beside(near.kept + near.got.astype(wide))
            near.step *= 2
            near.send()
        near.got, own_rest = beside((near.got, own_rest))
        rest_gather = RingGather(own_rest, dp_count)
        near.hop()
        near = near.parts[0]
    else:
        w_first = lax.all_gather(own_first, "dp", axis=0, tiled=True)
        w_rest = lax.all_gather(own_rest, "dp", axis=0, tiled=True)
        time_low, ada_low = embed(lax.all_gather(time_steps, "dp", axis=0, tiled=True).reshape(-1))
        near = slot_products([(ada_low, near_maps[0]), (time_low, near_maps[1])])
        near = lax.psum_scatter(near, "dp", scatter_dimension=0, tiled=True)[0].astype(wide)

    seg_grid = seg_ids.reshape(rows, row_len)
    unit_seg = seg_grid.reshape(rows, units, UNIT)[:, :, 0]
    onehot = unit_seg[:, :, None] == jnp.arange(slots, dtype=jnp.int32)
    blocks = onehot[:, :, None, :] & (jnp.arange(rows)[:, None] == jnp.arange(rows))[:, None, :, None]
    blocks = blocks.reshape(rows * units, rows * slots)
    seg_place = unit_seg.reshape(rows, 4, own_units)
    seg_place = jnp.stack(
        [
            lax.dynamic_index_in_dim(seg_place, jnp.bitwise_xor(place, j), 1, keepdims=False)
            for j in range(4)
        ],
        0,
    )
    row_slots = seg_place + slots * jnp.arange(rows)[None, :, None]

    def field_slots(field):
        return row_slots + slot_count * field

    def slot_matrix(to, height):
        to = jnp.concatenate(to, 1).reshape(1, -1)
        return (jnp.arange(height)[:, None] == to).astype(low)

    spare = 4 * slot_count
    far_to = []
    for r in range(rows):
        far_to += [field_slots(f)[:, r] for f in range(3)] + [jnp.full((4, own_units), -1)]
    for r in range(rows):
        far_to += [field_slots(3)[:, r], jnp.full((4, 4), -1)]
    near_to = [field_slots(f)[:, r] for r in range(rows) for f in range(2)]
    moved = row_slots.transpose(1, 0, 2).reshape(-1, 1) == jnp.arange(slot_count)[None, :]
    quarters = [(r * 4 + jnp.bitwise_xor(place, j)) * quarter for j in range(4) for r in range(rows)]
    hot, far_matrix, near_matrix, moved, at = chain.tie(
        blocks.astype(low),
        slot_matrix(far_to, spare + 16),
        slot_matrix(near_to, 2 * slot_count),
        moved.astype(wide),
        jnp.stack(quarters).astype(jnp.int32),
    )

    mp_arg = mp_place.astype(jnp.int32).reshape(1)

    def tables(spread, fields):
        spread.forward()
        pieces = [spread.own, spread.core, spread.chip, spread.both]
        return unit_tables(chain, mp_arg, hot, pieces, fields, own_units)

    far = slot_products([(lax.optimization_barrier((ada_low, near))[0], far_maps)])
    near_mod = (near[:, : 2 * own_width] + bias_cols[6:8].reshape(1, -1)).astype(low)
    near_tab = tables(GroupGather(near_mod), 2)
    if ring:
        far = HalvingSum(far, dp_count)
        w_first = first_gather.place(chain)
    time_add = jnp.concatenate(
        [
            near[:, 2 * own_width : 3 * own_width] + bias_cols[0],
            jnp.zeros((rows * slots, own_width), wide),
            near[:, 3 * own_width :] + bias_cols[1],
        ],
        1,
    )
    add_tab = jnp.dot(blocks.astype(wide), time_add, precision=highest)
    add_tab = add_tab.reshape(rows * 4, own_units, 3 * own_width)

    block, half_block = (quarter, width), (row_len // 2, width)
    qkv_width = 3 * own_width
    half = row_len // 2
    lows = lambda *shape: shape_of(shape, low)
    wides = lambda *shape: shape_of(shape, wide)

    def own_block(r):
        return pl.BlockSpec(block, lambda i, p: (r * 4 + p[0], 0))

    def moved_blocks(r):
        return [
            pl.BlockSpec(block, lambda i, p: (r * 4 + jnp.bitwise_xor(p[0], 2 * i), 0)),
            pl.BlockSpec(block, lambda i, p: (r * 4 + jnp.bitwise_xor(p[0], 2 * i + 1), 0)),
        ]

    def moved_tables(tab, r):
        shape = (1,) + tab.shape[1:]
        return [
            pl.BlockSpec(shape, lambda i, p: (r * 4 + jnp.bitwise_xor(p[0], 2 * i), 0, 0)),
            pl.BlockSpec(shape, lambda i, p: (r * 4 + jnp.bitwise_xor(p[0], 2 * i + 1), 0, 0)),
        ]

    def own_table(tab, r):
        return pl.BlockSpec((1,) + tab.shape[1:], lambda i, p: (r * 4 + p[0], 0, 0))

    here = fixed_spec(block)
    half_step = pl.BlockSpec(half_block, lambda i, p: (i, 0))
    half_fixed = fixed_spec(half_block)

    def open_row(r):
        return row_call(
            open_kernel,
            "open_row",
            chain,
            (tokens, tokens, near_tab, near_tab, add_tab, add_tab, w_first),
            moved_blocks(r) + moved_tables(near_tab, r) + moved_tables(add_tab, r) + [fixed_spec(w_first.shape)],
            (half_step, pl.BlockSpec((half, qkv_width), lambda i, p: (i, 0))),
            (lows(row_len, width), lows(row_len, qkv_width)),
            grid=2,
            flops=2 * row_len * width * qkv_width,
        )

    inputs_one, qkvs, mixed, parts = [], [], [], []

    def open_attend(r, between):
        a_one, qkv = open_row(r)
        inputs_one.append(a_one)
        qkvs.append(qkv)
        between()
        out, kept, sent = attend_forward(chain, qkv, seg_grid[r], w_first)
        mixed.append(out)
        parts.append(GroupSum(kept, sent))

    def both_hop():
        if ring:
            far.hop()
            rest_gather.hop()
            chain.land(*far.flying(), *rest_gather.flying())

    def far_spread():
        held = far.parts[0] if ring else lax.psum_scatter(far, "dp", scatter_dimension=0, tiled=True)[0]
        return GroupGather((held.astype(wide) + bias_cols[8:12].reshape(1, -1)).astype(low))

    def second_between():
        parts[0].cross()
        chain.land((parts[0], "last"))
        if ring:
            far.hop()
            chain.land(*rest_gather.flying())
        spreads.append(far_spread())
        chain.land(*spreads[0].flying())

    spreads = []
    if ring:
        chain.land(*far.flying(), *rest_gather.flying())
    open_attend(0, both_hop)
    if ring:
        far.hop()
        rest_gather.hop()
        chain.land(*far.flying())
    chain.land((parts[0], "got"))
    open_attend(1, second_between)
    if ring:
        rest_gather.hop()
    far_tab = tables(spreads[0], 4)

    attendeds, hiddens, inputs_two, down_grads = [], [], [], []

    def first_norm(r):
        attended, hidden, a_two = row_call(
            first_kernel,
            "first_norm",
            chain,
            (tokens, *parts[r].terms(), bias_rows, far_tab),
            [own_block(r), here, here, here, fixed_spec(bias_rows.shape), own_table(far_tab, r)],
            (here, here, here),
            (wides(*block), wides(*block), lows(*block)),
        )
        attendeds.append(attended)
        hiddens.append(hidden)
        inputs_two.append(GroupGather(a_two))

    def down_back(r):
        grads = row_call(
            down_back_kernel,
            "down_back",
            chain,
            (cotangent, cotangent, far_tab, far_tab, w_rest),
            moved_blocks(r) + moved_tables(far_tab, r) + [w_down_spec],
            (half_step, half_step),
            (lows(row_len, width), lows(row_len, width)),
            grid=2,
            flops=2 * row_len * width * width,
        )
        down_grads.append(grads)

    chain.land((parts[-1], "got"))
    first_norm(0)
    parts[-1].cross()
    if ring:
        w_rest = rest_gather.place(chain)
    w_down_spec = pl.BlockSpec((width, w_rest.shape[1] // 2), lambda i, p: (0, 1))
    w_up_spec = pl.BlockSpec((width, w_rest.shape[1] // 2), lambda i, p: (0, 0))
    chain.land(*inputs_two[0].flying())
    down_back(0)
    inputs_two[0].forward()
    chain.land((inputs_two[0], "both"), (parts[-1], "last"))
    down_back(1)
    first_norm(1)

    bias_up = bias_cols[2:6].reshape(1, -1)
    hidden_width = bias_up.shape[1]
    actives, inner_grads, up_parts, up_sums, down_parts = [], [], [], 0.0, []
    for r in range(rows):
        if r + 1 < rows:
            chain.land(*inputs_two[r + 1].flying())
        if r:
            chain.land((up_parts[r - 1], "last"), (down_parts[r - 1], "got"))
        active, inner_grad, kept, sent, sums = row_call(
            up_kernel,
            "up_and_back",
            chain,
            (*inputs_two[r].pieces(), down_grads[r][1], bias_up, w_rest),
            [here] * 4 + [half_step, fixed_spec(bias_up.shape), w_up_spec],
            (
                pl.BlockSpec((half, hidden_width), lambda i, p: (i, 0)),
                pl.BlockSpec((half, hidden_width), lambda i, p: (i, 0)),
                half_fixed,
                half_fixed,
                pl.BlockSpec((1, 8, hidden_width), lambda i, p: (i, 0, 0)),
            ),
            (
                lows(row_len, hidden_width),
                lows(row_len, hidden_width),
                wides(half, width),
                lows(half, width),
                wides(2, 8, hidden_width),
            ),
            grid=2,
            scratch=[pltpu.VMEM(half_block, low)],
            flops=4 * row_len * width * hidden_width,
        )
        actives.append(active)
        inner_grads.append(inner_grad)
        up_parts.append(GroupSum(kept, sent))
        up_sums = up_sums + jnp.sum(sums, axis=(0, 1))
        chain.land((up_parts[r], "got"))
        if r + 1 < rows:
            inputs_two[r + 1].forward()
            chain.land((inputs_two[r + 1], "both"))
        if r:
            down_parts[r - 1].cross()
            chain.land((down_parts[r - 1], "last"))
        kept, sent = row_call(
            down_kernel,
            "down",
            chain,
            (active, w_rest),
            [pl.BlockSpec((half, hidden_width), lambda i, p: (i, 0)), w_down_spec],
            (half_fixed, half_fixed),
            (wides(half, width), lows(half, width)),
            grid=2,
            flops=2 * row_len * width * hidden_width,
        )
        down_parts.append(GroupSum(kept, sent))
        up_parts[r].cross()

    grad_hiddens, grad_gathers, second_sums = [], [], []

    def second_norm(r):
        grad_hidden, grad_attended, sums = row_call(
            second_kernel,
            "second_norm",
            chain,
            (cotangent, *up_parts[r].terms(), hiddens[r], attendeds[r], far_tab),
            [own_block(r)] + [here] * 5 + [own_table(far_tab, r)],
            (here, here, fixed_spec((16, width))),
            (wides(*block), lows(*block), wides(16, width)),
        )
        grad_hiddens.append(grad_hidden)
        grad_gathers.append(GroupGather(grad_attended))
        second_sums.append(sums)

    chain.land((down_parts[-1], "got"))
    second_norm(0)
    down_parts[-1].cross()
    chain.land((up_parts[-1], "last"), *grad_gathers[0].flying())
    rest_grad = weight_grad(
        chain,
        [
            [(inputs_two[r].pieces(), inner_grads[r]) for r in range(rows)],
            [([down_grads[r][0]], actives[r]) for r in range(rows)],
        ],
        "grad_rest",
    )
    rest_ring = RingSum(rest_grad, dp_count)
    grad_gathers[0].forward()
    chain.land((grad_gathers[0], "both"))
    second_norm(1)

    def out_rows():
        args, specs = [bias_rows], [fixed_spec(bias_rows.shape)]
        for r in range(rows):
            args += [cotangent, *down_parts[r].terms(), hiddens[r], far_tab, second_sums[r]]
            specs += [own_block(r)] + [here] * 4 + [own_table(far_tab, r), fixed_spec((16, width))]
        own, sums = row_call(
            out_kernel,
            "out_tokens",
            chain,
            args,
            specs,
            (fixed_spec((rows * quarter + 16, width)), fixed_spec((8 * rows, width))),
            (lows(rows * quarter + 16, width), wides(8 * rows, width)),
        )
        return GroupGather(own), sums

    def part(held, which, columns):
        return lax.dynamic_slice_in_dim(held, which * columns, columns, 1)

    class Exchange:
        def __init__(self, values):
            values = values.astype(low)
            self.mine = part(values, chip, 2 * own_width)
            self.other = lax.ppermute(part(values, 1 - chip, 2 * own_width), "mp", CHIP_SWAP)

        def cross(self):
            values = self.whole()
            self.mine = part(values, core, own_width)
            self.other = lax.ppermute(part(values, 1 - core, own_width), "mp", CORE_SWAP)

        def whole(self):
            return jnp.concatenate([self.mine, self.other], 0)

    qkv_grads, one_parts, time_sums = [], [], []

    def backward(r):
        qkv_grad, kept, sent, sums = attend_backward(
            chain, qkvs[r], grad_gathers[r].pieces(), seg_grid[r], w_first
        )
        qkv_grads.append(qkv_grad)
        one_parts.append(GroupSum(kept, sent))
        time_sums.append(sums)

    chain.land(*rest_ring.flying(), *grad_gathers[1].flying(), (down_parts[-1], "last"))
    backward(0)
    rest_ring.hop()
    grad_gathers[1].forward()
    chain.land((one_parts[0], "got"), (grad_gathers[1], "both"))
    out_gather, out_sums = out_rows()
    one_parts[0].cross()
    far_swap = Exchange(jnp.concatenate(second_sums + [out_sums], 0))
    last_hop = slice(0, 1 if dp_count == 8 else 2)
    chain.land(*rest_ring.flying(), (one_parts[0], "last"), (out_gather, "core"))
    backward(1)
    rest_ring.hop()
    chain.land(*rest_ring.flying(), (one_parts[1], "got"), (out_gather, "chip"), (far_swap, "other"))
    first_grad = weight_grad(
        chain,
        [
            [([inputs_one[r]], qkv_grads[r]) for r in range(rows)],
            [(grad_gathers[r].pieces(), mixed[r]) for r in range(rows)],
        ],
        "grad_first",
    )
    first_ring = RingSum(first_grad, dp_count)
    one_parts[1].cross()
    rest_ring.hop()
    out_gather.forward()
    far_swap.cross()

    cols_state = (weight_cols, first_cols, second_cols, ema_cols)
    rows_state = [x.transpose(0, 2, 1) for x in (weight_rows, first_rows, second_rows, ema_rows)]
    cuts = [(r * quarter, quarter) for r in range(rows)]
    chain.land((out_gather, "both"), (far_swap, "other"))
    third_args, third_specs = [], []
    for r in range(rows):
        third_args += [tokens, *one_parts[r].terms(), grad_hiddens[r], near_tab]
        third_specs += [own_block(r)] + [here] * 4 + [own_table(near_tab, r)]
    out_tokens = place_pieces(chain, at, out_gather.pieces(), cuts)
    far_slots = dot_as(far_matrix, far_swap.whole(), DOT_NN)
    own, across, core_own, core_across = [
        x[rows * quarter : rows * quarter + 2].astype(wide) for x in out_gather.pieces()
    ]
    bias_part = (own + across) + (core_own + core_across)
    far_slots = lax.dynamic_update_slice(
        far_slots,
        jnp.concatenate([up_sums.reshape(4, own_width), bias_part.reshape(8, own_width)], 0),
        (spare, 0),
    ).astype(low)
    far_gather = DoublingGather(far_slots, dp_count)
    chain.land(*first_ring.flying(), *rest_ring.flying()[last_hop], *far_gather.flying())
    input_own, third_sums = row_call(
        third_kernel,
        "third_norm",
        chain,
        third_args,
        third_specs,
        (fixed_spec((rows * quarter, width)), fixed_spec((8 * rows, width))),
        (lows(rows * quarter, width), wides(8 * rows, width)),
    )
    first_ring.hop()
    far_gather.hop()
    input_gather = GroupGather(input_own)
    near_swap = Exchange(third_sums)

    def columns_of(ref, at):
        return column(ref[...], at, own_width).astype(wide)

    def map_grad(left, right, field):
        right = right[:, field * slot_count : (field + 1) * slot_count, :]
        return dot_as(left[...], right.reshape(-1, own_width), DOT_TN)

    rest_sum = rest_ring.total()
    chain.land(*first_ring.flying(), *far_gather.flying(), (near_swap, "other"))
    cols_new = adam_slabs(
        chain,
        [(0, i) for i in (5, 6, 7, 8)],
        (rest_sum,),
        lambda n, refs: columns_of(refs[0], n),
        [cols_state],
        [None],
        "adam_up",
    )
    first_ring.hop()
    near_swap.cross()
    far_gather.hop()
    chain.land(*first_ring.flying(), (near_swap, "other"), *far_gather.flying())
    rows_new = adam_slabs(
        chain,
        [(0, i) for i in (1, 2, 3, 4)],
        (rest_sum,),
        lambda n, refs: columns_of(refs[0], 4 + n),
        [rows_state],
        [None],
        "adam_down",
    )
    first_ring.hop()
    far_all = far_gather.whole()
    unit_sums = jnp.concatenate(time_sums, 0)
    time_slots = lax.dot_general(moved, unit_sums, DOT_TN, precision=highest)
    near_slots = jnp.concatenate(
        [
            dot_as(near_matrix, near_swap.whole(), DOT_NN),
            time_slots[:, :own_width],
            time_slots[:, 2 * own_width :],
        ],
        0,
    ).astype(low)
    near_gather = DoublingGather(near_slots, dp_count)
    chain.land(*near_gather.flying(), *first_ring.flying()[last_hop], (input_gather, "chip"))
    cols_new = adam_slabs(
        chain,
        [(0, i) for i in (11, 12, 13, 14)],
        (ada_low, far_all),
        lambda n, refs: map_grad(refs[0], refs[1], n),
        [cols_state],
        [cols_new],
        "adam_far",
    )
    near_gather.hop()
    input_gather.forward()
    first_sum = first_ring.total()
    chain.land(*near_gather.flying(), (input_gather, "core"), (input_gather, "both"))
    new = adam_slabs(
        chain,
        [(0, i) for i in (0, 1, 2)] + [(1, 0)],
        (first_sum,),
        lambda n, refs: columns_of(refs[0], n),
        [cols_state, rows_state],
        [cols_new, rows_new],
        "adam_first",
    )
    cols_new, rows_new = new[:4], [x.transpose(0, 2, 1) for x in new[4:]]
    near_gather.hop()
    chain.land(*near_gather.flying())
    input_grads = widen_rows(chain, input_gather.pieces(), rows)
    near_all = near_gather.whole()
    cols_new = adam_slabs(
        chain,
        [(0, i) for i in (9, 10, 3, 4)],
        (ada_low, time_low, near_all),
        lambda n, refs: map_grad(refs[n // 2], refs[2], n),
        [cols_state],
        [cols_new],
        "adam_near",
    )
    far_sum = jnp.sum(far_all.astype(wide), axis=0)
    far_biases = jnp.sum(far_sum[:spare].reshape(4, slot_count, own_width), axis=1)
    bias_up_sum = far_sum[spare : spare + 4]
    bias_rows_sum = far_sum[spare + 4 : spare + 12].reshape(2, width)
    near_sum = jnp.sum(near_all.astype(wide).reshape(dp_count, 4, slot_count, own_width), axis=(0, 2))
    bias_cols_sum = jnp.concatenate([near_sum[2:4], bias_up_sum, near_sum[:2], far_biases], 0)
    bias_cols_new = adam_step(
        bias_cols, bias_cols_sum, first_bias_cols, second_bias_cols, ema_bias_cols, rate_vector
    )
    bias_rows_new = adam_step(
        bias_rows, bias_rows_sum, first_bias_rows, second_bias_rows, ema_bias_rows, rate_vector
    )
    return (out_tokens, input_grads, *cols_new, *rows_new, *bias_cols_new, *bias_rows_new)


def solution(mesh):
    cols, rows, bias = P(None, "dp", "mp"), P(None, "mp", "dp"), P(None, "mp")
    state = (cols, rows, bias, P())
    placed = (P("dp", None), P("dp"), P("dp", None), P("dp", None)) + state * 4
    given = (P("dp", None), P("dp", None)) + (cols,) * 4 + (rows,) * 4 + (bias,) * 4 + (P(),) * 4
    return jax.shard_map(
        per_device, mesh=mesh, in_specs=placed, out_specs=given, check_vma=False
    )
```

```python
import math

import jax
import jax.numpy as jnp
from jax import lax
from jax.experimental import pallas as pl
from jax.experimental.pallas import tpu as pltpu
from jax.sharding import PartitionSpec as P

HEAD_DIM = 72
STEP = 10
UNIT = 64
REACH = 192


highest = lax.Precision.HIGHEST
beta_one = 0.9
beta_two = 0.999
adam_eps = 1e-08
decay_rate = 0.1
rate_matrix = 0.05
rate_vector = 0.5
ema_keep = 0.7
norm_eps = 1e-06
neg_large = -1e30
score_scale = HEAD_DIM**-0.5
two_scale = score_scale * math.log2(math.e)
low = jnp.bfloat16
wide = jnp.float32

DOT_NN = (((1,), (0,)), ((), ()))
DOT_NT = (((1,), (1,)), ((), ()))
DOT_TN = (((0,), (0,)), ((), ()))

COST = 0
VMEM_GRANT = 58 * 2**20
SMEM_SPEC = pl.BlockSpec(memory_space=pltpu.SMEM)

CORE_SWAP = [(i, i ^ 1) for i in range(4)]
CHIP_SWAP = [(i, i ^ 2) for i in range(4)]


def dot_as(left, right, dims):
    return lax.dot_general(left, right, dims, preferred_element_type=wide)


def ring_order(count):
    return list(range(0, count, 2)) + list(range(count - 1, 0, -2))


def ring_perms(count):
    order = ring_order(count)
    onward = [(order[i], order[(i + 1) % count]) for i in range(count)]
    return onward, [(b, a) for a, b in onward]


def ring_spot(count):
    me = lax.axis_index("dp")
    return jnp.where(me % 2 == 0, me // 2, count - 1 - me // 2)


def ring_at(spot, count):
    spot = spot % count
    return jnp.where(spot < count // 2, 2 * spot, 2 * (count - 1 - spot) + 1)


def ring_places(rows, count):
    spot = ring_spot(count)
    back = [0]
    for hop in range(1, count // 2):
        back += [-hop, hop]
    at = ring_at(spot + jnp.array(back + [count // 2] * 2), count) * rows
    return (at + jnp.array([0] * len(back) + [0, rows // 32 * 16])).astype(jnp.int32)


def place_pieces(chain, at, pieces, cuts=None):
    parts = [(n, *cut) for n, piece in enumerate(pieces) for cut in cuts or [(0, piece.shape[0])]]
    whole = (sum(count for _, _, count in parts),) + pieces[0].shape[1:]
    at = chain.tie(at)

    def body(at_ref, *refs):
        out_ref, held, sem_in, sem_out = refs[-4:]
        arrive, leave = [], []
        base = 0
        for i, (n, start, count) in enumerate(parts):
            spot = held.at[pl.ds(base, count)]
            piece = refs[n].at[pl.ds(start, count)]
            arrive.append(pltpu.make_async_copy(piece, spot, sem_in.at[i]))
            to = out_ref.at[pl.ds(pl.multiple_of(at_ref[i], 16), count)]
            leave.append(pltpu.make_async_copy(spot, to, sem_out.at[i]))
            base += count
        for copy in arrive:
            copy.start()
        for first, second in zip(arrive, leave):
            first.wait()
            second.start()
        for copy in leave:
            copy.wait()

    out = pl.pallas_call(
        body,
        out_shape=jax.ShapeDtypeStruct(whole, pieces[0].dtype),
        in_specs=[SMEM_SPEC] + [pl.BlockSpec(memory_space=pl.ANY)] * len(pieces),
        out_specs=pl.BlockSpec(memory_space=pl.ANY),
        scratch_shapes=[pltpu.VMEM(whole, pieces[0].dtype)]
        + [pltpu.SemaphoreType.DMA((len(parts),))] * 2,
        compiler_params=pltpu.CompilerParams(vmem_limit_bytes=VMEM_GRANT),
        cost_estimate=pl.CostEstimate(flops=1, bytes_accessed=1, transcendentals=0),
        name="place_pieces",
    )(at, *pieces)
    return chain.close(out)


class Chain:
    def __init__(self, token):
        self.token = token

        self.landing = []

    def tie(self, *arrays):
        self.token, *arrays = lax.optimization_barrier((self.token, *arrays))
        return arrays[0] if len(arrays) == 1 else tuple(arrays)

    def land(self, *transfers):
        self.landing += transfers

    def close(self, *arrays):
        landing, self.landing = self.landing, []
        values = self.tie(*arrays, *[getattr(held, name) for held, name in landing])
        values = values if isinstance(values, tuple) else (values,)
        for (held, name), value in zip(landing, values[len(arrays) :]):
            setattr(held, name, value)
        return values[0] if len(arrays) == 1 else values[: len(arrays)]


class RingSum:
    def __init__(self, parts, count):
        self.parts, self.count = parts, count
        self.left = count // 2 - 1 if count in (4, 8) else 0
        if self.left:
            self.rows = parts.shape[0] // count
            self.onward, self.backward = ring_perms(count)
            self.spot = ring_spot(count)
            self.send(self.chunk(count // 2), self.chunk(1 - count // 2))

    def chunk(self, ahead):
        at = ring_at(self.spot + ahead, self.count) * self.rows
        return lax.dynamic_slice_in_dim(self.parts, at, self.rows, 0).astype(wide)

    def send(self, ahead, behind):
        self.ahead = lax.ppermute(ahead.astype(low), "dp", self.onward)
        if behind is not None:
            self.behind = lax.ppermute(behind.astype(low), "dp", self.backward)

    def flying(self):
        return [(self, "ahead"), (self, "behind")] if self.count in (4, 8) else []

    def hop(self):
        if not self.left:
            return
        ahead = self.ahead.astype(wide) + self.chunk(self.left)
        behind = None
        if self.left > 1:
            behind = self.behind.astype(wide) + self.chunk(1 - self.left)
        self.send(ahead, behind)
        self.left -= 1

    def total(self):
        if self.count not in (4, 8):
            return lax.psum_scatter(self.parts, "dp", scatter_dimension=0, tiled=True).astype(wide)
        total = self.ahead.astype(wide) + self.behind.astype(wide) + self.chunk(0)
        return total.astype(low)


class GroupSum:
    def __init__(self, kept, sent):
        self.kept, self.got = kept, lax.ppermute(sent, "mp", CORE_SWAP)

    def cross(self):
        quarter = self.kept.shape[0] // 2
        passed = self.kept[quarter:].astype(wide) + self.got[quarter:].astype(wide)
        passed = passed.astype(low)
        self.last = lax.ppermute(passed, "mp", CHIP_SWAP)

    def terms(self):
        return self.kept, self.got, self.last


class GroupGather:
    def __init__(self, own):
        self.own = own
        self.chip = lax.ppermute(own, "mp", CHIP_SWAP)
        self.core = lax.ppermute(own, "mp", CORE_SWAP)

    def forward(self):
        self.both = lax.ppermute(self.chip, "mp", CORE_SWAP)

    def flying(self):
        return [(self, "chip"), (self, "core")]

    def pieces(self):
        return [self.own, self.chip, self.core, self.both]

    def in_order(self, mp_place):
        return in_group_order([self.own, self.core, self.chip, self.both], mp_place)


class DoublingGather:
    def __init__(self, shard, count):
        self.shard, self.count = shard, count
        self.known, self.step = shard[None], count // 2 if count in (4, 8) else 0
        self.send()

    def send(self):
        if self.step:
            swap = [(i, i ^ self.step) for i in range(self.count)]
            self.got = lax.ppermute(self.known, "dp", swap)

    def join(self, got):
        second = lax.axis_index("dp") // self.step % 2 == 1
        pair = [jnp.where(second, got, self.known), jnp.where(second, self.known, got)]
        self.known = jnp.stack(pair, 1).reshape((-1,) + self.shard.shape)
        self.step //= 2

    def flying(self):
        return [(self, "got")] if self.step else []

    def hop(self):
        if self.step > 1:
            self.join(self.got)
            self.send()

    def whole(self):
        if self.step:
            self.join(self.got)
        if self.count not in (4, 8):
            return lax.all_gather(self.shard, "dp", axis=0, tiled=False)
        return self.known


class HalvingSum:
    def __init__(self, parts, count):
        self.parts, self.count, self.step = parts, count, 1
        self.send()

    def send(self):
        pairs = self.parts.reshape((self.parts.shape[0] // 2, 2) + self.parts.shape[1:])
        bit = lax.axis_index("dp") // self.step % 2
        sent = lax.dynamic_index_in_dim(pairs, 1 - bit, 1, keepdims=False).astype(low)
        self.kept = lax.dynamic_index_in_dim(pairs, bit, 1, keepdims=False).astype(wide)
        swap = [(i, i ^ self.step) for i in range(self.count)]
        self.got = lax.ppermute(sent, "dp", swap)

    def flying(self):
        return [(self, "got")] if self.step < self.count else []

    def hop(self):
        if self.step < self.count:
            self.parts = self.kept + self.got.astype(wide)
            self.step *= 2
            if self.step < self.count:
                self.send()


class RingGather:
    def __init__(self, shard, count):
        self.count, self.left = count, count // 2 - 1
        self.onward, self.backward = ring_perms(count)
        self.pieces = [shard]
        self.send(shard, shard)

    def send(self, ahead, behind):
        self.ahead = lax.ppermute(ahead, "dp", self.onward)
        self.behind = lax.ppermute(behind, "dp", self.backward)

    def flying(self):
        return [(self, "ahead"), (self, "behind")]

    def hop(self):
        ahead, behind = self.ahead, self.behind
        self.pieces += [ahead, behind]
        if self.left > 1:
            self.send(ahead, behind)
        elif self.left == 1:
            cut = ahead.shape[0] // 32 * 16
            self.send(ahead[:cut], behind[cut:])
        self.left -= 1

    def place(self, chain):
        while self.left >= 0:
            self.hop()
        return place_pieces(chain, ring_places(self.pieces[0].shape[0], self.count), self.pieces)


def share_hop(known, reach, count):
    return known + lax.ppermute(known, "dp", [(i, i ^ reach) for i in range(count)])


def in_group_order(pieces, place):
    stacked = jnp.stack(pieces, 0)
    return [
        lax.dynamic_index_in_dim(stacked, jnp.bitwise_xor(place, j), 0, keepdims=False)
        for j in range(4)
    ]


def key_windows(row_len, block):
    return [
        (at, max(0, at - REACH), min(row_len, at + block + REACH))
        for at in range(0, row_len, block)
    ]


def relative_at(place, j, block):
    return pl.multiple_of(jnp.bitwise_xor(place, j) * block, block)


def attend_forward_kernel(
    place_ref, qkv_ref, seg_row_ref, w_ref, out_ref, kept_ref, sent_ref, q_s, k_s, v_s, *, heads
):
    row_len = qkv_ref.shape[0]
    width = heads * HEAD_DIM
    block = row_len // 4
    place = place_ref[0]
    for j in range(4):
        at = relative_at(place, j, block)
        to = slice(j * block, (j + 1) * block)
        for h in range(heads):
            c = h * HEAD_DIM
            q_s[h, to, :] = qkv_ref[pl.ds(at, block), c : c + HEAD_DIM]
            k_s[h, to, :] = qkv_ref[pl.ds(at, block), width + c : width + c + HEAD_DIM]
            v_s[h, to, :] = qkv_ref[pl.ds(at, block), 2 * width + c : 2 * width + c + HEAD_DIM]
    for j, (at, start, stop) in enumerate(key_windows(row_len, block)):
        keys_seg = jnp.broadcast_to(seg_row_ref[:, start:stop], (8, stop - start)).T[:, :1]
        same = keys_seg == seg_row_ref[:, at : at + block]
        mixed = []
        for h in range(heads):
            scores = dot_as(k_s[h, start:stop, :], q_s[h, at : at + block, :], DOT_NT)
            scores = jnp.where(same, scores, neg_large)
            top = jnp.max(scores, axis=0, keepdims=True)
            weights = jnp.exp2((scores - top) * two_scale)
            total = jnp.sum(weights, axis=0, keepdims=True)
            gathered = dot_as(v_s[h, start:stop, :], weights.astype(low), DOT_TN)
            mixed.append(gathered * (1.0 / total))
        out_ref[pl.ds(relative_at(place, j, block), block), :] = (
            jnp.concatenate(mixed, axis=0).T.astype(low)
        )
    w_out = w_ref[:, w_ref.shape[1] - width :]
    half = row_len // 2
    kept_ref[...] = dot_as(out_ref[:half, :], w_out, DOT_NT).astype(low)
    sent_ref[...] = dot_as(out_ref[half:, :], w_out, DOT_NT).astype(low)


def attend_backward_kernel(
    place_ref, qkv_ref, g0_ref, g1_ref, g2_ref, g3_ref, seg_row_ref, w_ref,
    out_ref, kept_ref, sent_ref, sums_ref, q_s, k_s, v_s, g_s, dk_s, dv_s, *, heads
):
    row_len = qkv_ref.shape[0]
    width = heads * HEAD_DIM
    block = row_len // 4
    place = place_ref[0]
    dk_s[...] = jnp.zeros_like(dk_s)
    dv_s[...] = jnp.zeros_like(dv_s)
    w_out = w_ref[:, 3 * width :]
    for j, g_ref in enumerate((g0_ref, g1_ref, g2_ref, g3_ref)):
        grad = dot_as(g_ref[...], w_out, DOT_NN).astype(low)
        at = relative_at(place, j, block)
        for h in range(heads):
            g_s[h, pl.ds(at, block), :] = grad[:, h * HEAD_DIM : (h + 1) * HEAD_DIM]
    for j in range(4):
        at = relative_at(place, j, block)
        to = slice(j * block, (j + 1) * block)
        for h in range(heads):
            c = h * HEAD_DIM
            q_s[h, to, :] = qkv_ref[pl.ds(at, block), c : c + HEAD_DIM]
            k_s[h, to, :] = qkv_ref[pl.ds(at, block), width + c : width + c + HEAD_DIM]
            v_s[h, to, :] = qkv_ref[pl.ds(at, block), 2 * width + c : 2 * width + c + HEAD_DIM]
    for j, (at, start, stop) in enumerate(key_windows(row_len, block)):
        keys_seg = jnp.broadcast_to(seg_row_ref[:, start:stop], (8, stop - start)).T[:, :1]
        same = keys_seg == seg_row_ref[:, at : at + block]
        grads = []
        for h in range(heads):
            query = q_s[h, at : at + block, :]
            grad = g_s[h, at : at + block, :]
            keys = k_s[h, start:stop, :]
            scores = jnp.where(same, dot_as(keys, query, DOT_NT), neg_large)
            top = jnp.max(scores, axis=0, keepdims=True)
            weights = jnp.exp2((scores - top) * two_scale)
            probs = weights * (1.0 / jnp.sum(weights, axis=0, keepdims=True))
            grad_probs = dot_as(v_s[h, start:stop, :], grad, DOT_NT)
            inner = jnp.sum(grad_probs * probs, axis=0, keepdims=True)
            grad_scores = (probs * (grad_probs - inner)).astype(low)
            dv_s[h, start:stop, :] += dot_as(probs.astype(low), grad, DOT_NN)
            dk_s[h, start:stop, :] += dot_as(grad_scores, query, DOT_NN)
            grads.append(dot_as(keys, grad_scores, DOT_TN) * score_scale)
        out_ref[pl.ds(relative_at(place, j, block), block), 0:width] = (
            jnp.concatenate(grads, axis=0).T.astype(low)
        )
    for j in range(4):
        at = slice(j * block, (j + 1) * block)
        to = relative_at(place, j, block)
        out_ref[pl.ds(to, block), width : 2 * width] = jnp.concatenate(
            [(dk_s[h, at, :] * score_scale).astype(low) for h in range(heads)], axis=1
        )
        out_ref[pl.ds(to, block), 2 * width : 3 * width] = jnp.concatenate(
            [dv_s[h, at, :].astype(low) for h in range(heads)], axis=1
        )
    half = row_len // 2
    w_qkv = w_ref[:, : 3 * width]
    kept_ref[...] = dot_as(out_ref[:half, :], w_qkv, DOT_NT).astype(low)
    sent_ref[...] = dot_as(out_ref[half:, :], w_qkv, DOT_NT).astype(low)
    for u in range(row_len // UNIT):
        sums_ref[u : u + 1, :] = jnp.sum(
            out_ref[u * UNIT : (u + 1) * UNIT, :].astype(wide), axis=0, keepdims=True
        )


def shape_of(shape, kind):
    return jax.ShapeDtypeStruct(shape, kind)


def attend_forward(chain, qkv, seg_row, weights):
    row_len, width = qkv.shape[0], qkv.shape[1] // 3
    heads = width // HEAD_DIM
    full = weights.shape[0]
    args = (qkv, seg_row, weights)
    shapes = (
        shape_of((row_len, width), low),
        shape_of((row_len // 2, full), low),
        shape_of((row_len // 2, full), low),
    )

    def body(*refs):
        attend_forward_kernel(*refs, heads=heads)

    return row_call(
        body,
        "attend_forward",
        chain,
        args,
        [fixed_spec(arg.shape) for arg in args[:2]]
        + [pl.BlockSpec((full, weights.shape[1] // 3), lambda i, p: (0, 2))],
        tuple(fixed_spec(shape.shape) for shape in shapes),
        shapes,
        scratch=[pltpu.VMEM((heads, row_len, HEAD_DIM), low)] * 3,
        flops=4 * row_len * 640 * width + 2 * row_len * width * full,
        exps=heads * row_len * 640,
    )


def attend_backward(chain, qkv, grads, seg_row, weights):
    row_len, width = qkv.shape[0], qkv.shape[1] // 3
    heads = width // HEAD_DIM
    full = weights.shape[0]
    args = (qkv, *grads, seg_row, weights)
    shapes = (
        shape_of((row_len, 3 * width), low),
        shape_of((row_len // 2, full), low),
        shape_of((row_len // 2, full), low),
        shape_of((row_len // UNIT, 3 * width), wide),
    )

    def body(*refs):
        attend_backward_kernel(*refs, heads=heads)

    return row_call(
        body,
        "attend_backward",
        chain,
        args,
        [fixed_spec(arg.shape) for arg in args],
        tuple(fixed_spec(shape.shape) for shape in shapes),
        shapes,
        scratch=[pltpu.VMEM((heads, row_len, HEAD_DIM), low)] * 4
        + [pltpu.VMEM((heads, row_len, HEAD_DIM), wide)] * 2,
        flops=10 * row_len * 640 * width + 8 * row_len * width * full,
        exps=heads * row_len * 640,
    )


def norm_parts(values):
    centre = values - jnp.mean(values, axis=-1, keepdims=True)
    inverse = lax.rsqrt(jnp.mean(centre * centre, axis=-1, keepdims=True) + norm_eps)
    return centre * inverse, inverse


def norm_back(normed, inverse, grad):
    return inverse * (
        grad
        - jnp.mean(grad, axis=-1, keepdims=True)
        - normed * jnp.mean(grad * normed, axis=-1, keepdims=True)
    )


def unit_rows(ref):
    return [(u, slice(u * UNIT, (u + 1) * UNIT)) for u in range(ref.shape[0] // UNIT)]


def column(values, index, width):
    return values[:, index * width : (index + 1) * width]


def open_kernel(
    place_ref, x0_ref, x1_ref, tab0_ref, tab1_ref, add0_ref, add1_ref, w_ref, a_ref, qkv_ref
):
    width = x0_ref.shape[1]
    quarter = x0_ref.shape[0]
    for j, (x_ref, tab_ref) in enumerate(((x0_ref, tab0_ref), (x1_ref, tab1_ref))):
        for u, at in unit_rows(x_ref):
            normed, _ = norm_parts(x_ref[at, :].astype(wide))
            table = tab_ref[0, u : u + 1, :]
            out = normed * (1.0 + column(table, 1, width)) + column(table, 0, width)
            a_ref[j * quarter + u * UNIT : j * quarter + (u + 1) * UNIT, :] = out.astype(low)
    qkv = dot_as(a_ref[...], w_ref[:, : qkv_ref.shape[1]], DOT_NN)
    for j, add_ref in enumerate((add0_ref, add1_ref)):
        for u in range(quarter // UNIT):
            at = slice(j * quarter + u * UNIT, j * quarter + (u + 1) * UNIT)
            qkv_ref[at, :] = (qkv[at, :] + add_ref[0, u : u + 1, :]).astype(low)


def first_kernel(place_ref, x_ref, kept_ref, got_ref, passed_ref, bias_ref, tab_ref, att_ref, hid_ref, a_ref):
    width = x_ref.shape[1]
    for u, at in unit_rows(x_ref):
        table = tab_ref[0, u : u + 1, :]
        attended = kept_ref[at, :].astype(wide) + got_ref[at, :].astype(wide) + passed_ref[at, :].astype(wide)
        attended = attended + bias_ref[0:1, :]
        hidden = x_ref[at, :].astype(wide) + column(table, 0, width) * attended
        normed, _ = norm_parts(hidden)
        att_ref[at, :] = attended
        hid_ref[at, :] = hidden
        a_ref[at, :] = (normed * (1.0 + column(table, 2, width)) + column(table, 1, width)).astype(low)


def down_back_kernel(place_ref, cot0_ref, cot1_ref, tab0_ref, tab1_ref, w_ref, grad_ref, dm_ref):
    width = cot0_ref.shape[1]
    quarter = cot0_ref.shape[0]
    for j, (cot_ref, tab_ref) in enumerate(((cot0_ref, tab0_ref), (cot1_ref, tab1_ref))):
        for u, at in unit_rows(cot_ref):
            gate = column(tab_ref[0, u : u + 1, :], 3, width)
            out = (cot_ref[at, :].astype(wide) * gate).astype(low)
            grad_ref[j * quarter + u * UNIT : j * quarter + (u + 1) * UNIT, :] = out
    dm_ref[...] = dot_as(grad_ref[...], w_ref[...], DOT_NN).astype(low)


def gelu_both(values):
    scale = math.sqrt(2.0 / math.pi)
    square = values * values
    turned = jnp.tanh(scale * values * (1.0 + 0.044715 * square))
    upper = 0.5 * (1.0 + turned)
    slope = upper + 0.5 * values * (1.0 - turned * turned) * scale * (1.0 + 3 * 0.044715 * square)
    return values * upper, slope


def up_kernel(
    place_ref, a0_ref, a1_ref, a2_ref, a3_ref, dm_ref, bias_ref, w_ref, m_ref, dz_ref, kept_ref, sent_ref, sums_ref, a_s
):
    step = pl.program_id(0)
    quarter = a0_ref.shape[0]
    for j, piece in enumerate((a0_ref, a1_ref, a2_ref, a3_ref)):

        @pl.when(step == j // 2)
        def _(piece=piece, j=j):
            a_s[j % 2 * quarter : (j % 2 + 1) * quarter, :] = piece[...]

    sums = jnp.zeros(sums_ref.shape[1:], wide)
    for j in range(2):
        at = slice(j * quarter, (j + 1) * quarter)
        inner = dot_as(a_s[at, :], w_ref[...], DOT_NN) + bias_ref[...]
        active, slope = gelu_both(inner)
        m_ref[at, :] = active.astype(low)
        grad = (dm_ref[at, :].astype(wide) * slope).astype(low)
        dz_ref[at, :] = grad
        sums = sums + jnp.sum(grad.astype(wide).reshape(-1, 8, grad.shape[1]), axis=0)
    sums_ref[0] = sums
    back = dot_as(dz_ref[...], w_ref[...], DOT_NT)

    @pl.when(step == 0)
    def _():
        kept_ref[...] = back.astype(low)

    @pl.when(step == 1)
    def _():
        sent_ref[...] = back.astype(low)


def down_kernel(place_ref, m_ref, w_ref, kept_ref, sent_ref):
    step = pl.program_id(0)
    out = dot_as(m_ref[...], w_ref[...], DOT_NT)

    @pl.when(step == 0)
    def _():
        kept_ref[...] = out.astype(low)

    @pl.when(step == 1)
    def _():
        sent_ref[...] = out.astype(low)


def second_kernel(
    place_ref, cot_ref, kept_ref, got_ref, passed_ref, hid_ref, att_ref, tab_ref, gh_ref, ga_ref, sums_ref
):
    width = cot_ref.shape[1]
    bias = jnp.zeros((1, width), wide)
    sums_ref[...] = jnp.zeros_like(sums_ref)
    for u, at in unit_rows(cot_ref):
        table = tab_ref[0, u : u + 1, :]
        grad_two = kept_ref[at, :].astype(wide) + got_ref[at, :].astype(wide) + passed_ref[at, :].astype(wide)
        normed, inverse = norm_parts(hid_ref[at, :])
        grad = cot_ref[at, :].astype(wide) + norm_back(
            normed, inverse, grad_two * (1.0 + column(table, 2, width))
        )
        grad_att = grad * column(table, 0, width)
        gh_ref[at, :] = grad
        ga_ref[at, :] = grad_att.astype(low)
        bias = bias + jnp.sum(grad_att, axis=0, keepdims=True)
        sums_ref[u : u + 1, :] = jnp.sum(grad * att_ref[at, :], axis=0, keepdims=True)
        sums_ref[4 + u : 5 + u, :] = jnp.sum(grad_two, axis=0, keepdims=True)
        sums_ref[8 + u : 9 + u, :] = jnp.sum(grad_two * normed, axis=0, keepdims=True)
    sums_ref[12:13, :] = bias


def out_kernel(place_ref, bias_ref, *refs):
    rows = (len(refs) - 2) // 7
    out_ref, sums_ref = refs[-2:]
    quarter, width = refs[0].shape
    total = jnp.zeros((1, width), wide)
    other = jnp.zeros((1, width), wide)
    sums_ref[...] = jnp.zeros_like(sums_ref)
    for r in range(rows):
        cot_ref, kept_ref, got_ref, passed_ref, hid_ref, tab_ref, second_ref = refs[7 * r : 7 * r + 7]
        for u, at in unit_rows(cot_ref):
            gate = column(tab_ref[0, u : u + 1, :], 3, width)
            mlp = kept_ref[at, :].astype(wide) + got_ref[at, :].astype(wide) + passed_ref[at, :].astype(wide)
            mlp = mlp + bias_ref[1:2, :]
            out_ref[r * quarter + u * UNIT : r * quarter + (u + 1) * UNIT, :] = (
                hid_ref[at, :] + gate * mlp
            ).astype(low)
            cot = cot_ref[at, :].astype(wide)
            sums_ref[8 * r + u : 8 * r + u + 1, :] = jnp.sum(cot * mlp, axis=0, keepdims=True)
            total = total + jnp.sum(cot, axis=0, keepdims=True) * gate
        other = other + second_ref[12:13, :]
    tail = jnp.concatenate([other, total, jnp.zeros((14, width), wide)], axis=0)
    out_ref[rows * quarter :, :] = tail.astype(low)


def third_kernel(place_ref, *refs):
    rows = (len(refs) - 2) // 6
    out_ref, sums_ref = refs[-2:]
    quarter, width = refs[0].shape
    for r in range(rows):
        x_ref, kept_ref, got_ref, passed_ref, gh_ref, tab_ref = refs[6 * r : 6 * r + 6]
        for u, at in unit_rows(x_ref):
            grad_one = kept_ref[at, :].astype(wide) + got_ref[at, :].astype(wide) + passed_ref[at, :].astype(wide)
            normed, inverse = norm_parts(x_ref[at, :].astype(wide))
            table = tab_ref[0, u : u + 1, :]
            back = norm_back(normed, inverse, grad_one * (1.0 + column(table, 1, width)))
            out_ref[r * quarter + u * UNIT : r * quarter + (u + 1) * UNIT, :] = (
                gh_ref[at, :] + back
            ).astype(low)
            n = 8 * r + u
            sums_ref[n : n + 1, :] = jnp.sum(grad_one, axis=0, keepdims=True)
            sums_ref[n + 4 : n + 5, :] = jnp.sum(grad_one * normed, axis=0, keepdims=True)


def row_call(
    body, name, chain, args, in_specs, out_specs, out_shape, grid=1, scratch=(), flops=0, exps=0, aliases=None, prefetch=None
):
    moved = sum(math.prod(a.shape) * a.dtype.itemsize for a in args)
    shapes = out_shape if isinstance(out_shape, tuple) else (out_shape,)
    moved += sum(math.prod(o.shape) * o.dtype.itemsize for o in shapes)
    prefetch = chain.token if prefetch is None else chain.tie(prefetch)
    out = pl.pallas_call(
        body,
        grid_spec=pltpu.PrefetchScalarGridSpec(
            num_scalar_prefetch=1,
            grid=(grid,),
            in_specs=in_specs,
            out_specs=out_specs,
            scratch_shapes=scratch,
        ),
        out_shape=out_shape,
        input_output_aliases=aliases or {},
        compiler_params=pltpu.CompilerParams(vmem_limit_bytes=VMEM_GRANT),
        cost_estimate=pl.CostEstimate(
            flops=int(COST * flops) + 1, bytes_accessed=int(COST * moved) + 1, transcendentals=0
        ),
        name=name,
    )(prefetch, *args)
    return chain.close(*out) if isinstance(out_shape, tuple) else chain.close(out)


def fixed_spec(shape):
    return pl.BlockSpec(shape, lambda *_: (0,) * len(shape))


def unit_tables(chain, mp_arg, onehot, pieces, fields, group):
    units, slots = onehot.shape
    own = pieces[0].shape[1] // fields
    shape = (units // group, group, fields * 4 * own)

    def body(mp_ref, hot_ref, *refs):
        out_ref = refs[-1]
        mp_place = mp_ref[0]
        for i, piece in enumerate(refs[:-1]):
            spread = dot_as(hot_ref[...], piece[...], DOT_NN)
            for j in range(4):

                @pl.when(jnp.bitwise_xor(mp_place, i) == j)
                def _(spread=spread, j=j):
                    for f in range(fields):
                        at = f * 4 * own + j * own
                        values = column(spread, f, own)
                        for n in range(units // group):
                            out_ref[n, :, at : at + own] = values[n * group : (n + 1) * group, :]

    return row_call(
        body,
        "unit_tables",
        chain,
        (onehot, *pieces),
        [fixed_spec(onehot.shape)] + [fixed_spec(pieces[0].shape)] * 4,
        fixed_spec(shape),
        shape_of(shape, wide),
        flops=8 * units * slots * own * fields,
        prefetch=mp_arg,
    )


def weight_grad(chain, pairs, name):
    depth = pairs[0][0][0][0].shape[1]
    tile = depth // 3
    widths = [pair[0][1].shape[1] for pair in pairs]
    args, specs, plan = [], [], []
    flops = 0
    for pair in pairs:
        rows = []
        for left, right in pair:
            rows.append((len(args), len(left)))
            args += list(left) + [right]
            specs += [pl.BlockSpec((piece.shape[0], tile), lambda i, p: (0, i)) for piece in left]
            specs.append(fixed_spec(right.shape))
            flops += 2 * depth * math.prod(right.shape)
        plan.append(rows)

    def body(place_ref, *refs):
        out_ref = refs[-1]
        at = 0
        for rows, cols in zip(plan, widths):
            total = None
            for first, count in rows:
                left = [ref[...] for ref in refs[first : first + count]]
                left = left[0] if count == 1 else jnp.concatenate(left, axis=0)
                part = dot_as(left, refs[first + count][...], DOT_TN)
                total = part if total is None else total + part
            out_ref[:, at : at + cols] = total.astype(low)
            at += cols

    return row_call(
        body,
        name,
        chain,
        args,
        specs,
        pl.BlockSpec((tile, sum(widths)), lambda i, p: (i, 0)),
        shape_of((depth, sum(widths)), low),
        grid=3,
        flops=flops,
    )


def widen_rows(chain, pieces, rows):
    quarter, width = pieces[0].shape[0] // rows, pieces[0].shape[1]

    def body(place_ref, *refs):
        out_ref, wide_s, sems = refs[-3:]
        copies = []
        for r in range(rows):
            for j, piece in enumerate(refs[:4]):
                held = wide_s.at[r, j]
                held[...] = piece[r * quarter : (r + 1) * quarter, :].astype(wide)
                at = (r * 4 + jnp.bitwise_xor(place_ref[0], j)) * quarter
                to = out_ref.at[pl.ds(pl.multiple_of(at, quarter), quarter)]
                copies.append(pltpu.make_async_copy(held, to, sems.at[r, j]))
                copies[-1].start()
        for copy in copies:
            copy.wait()

    return row_call(
        body,
        "widen_rows",
        chain,
        tuple(pieces),
        [fixed_spec(pieces[0].shape)] * 4,
        pl.BlockSpec(memory_space=pl.ANY),
        shape_of((rows * 4 * quarter, width), wide),
        scratch=[pltpu.VMEM((rows, 4, quarter, width), wide), pltpu.SemaphoreType.DMA((rows, 4))],
    )


def adam_step(weight, gradient, first_old, second_old, ema_old, step_rate):
    first_new = beta_one * first_old + (1.0 - beta_one) * gradient
    second_new = beta_two * second_old + (1.0 - beta_two) * gradient * gradient
    first_hat = first_new * (1.0 / (1.0 - beta_one**STEP))
    second_hat = second_new * (1.0 / (1.0 - beta_two**STEP))
    weight_new = weight - step_rate * (
        first_hat / (jnp.sqrt(second_hat) + adam_eps) + decay_rate * weight
    )
    ema_new = ema_keep * ema_old + (1.0 - ema_keep) * weight_new
    return (first_new, second_new, weight_new, ema_new)


def adam_slabs(chain, plan, grads, make_grad, groups, before, name):
    slab = groups[0][0].shape[1:]
    count, held = len(plan), 4 * len(groups)

    def body(place_ref, *refs):
        grad_refs, state_refs = refs[: len(grads)], refs[len(grads) : len(grads) + held]
        out_refs = refs[-held - 4 : -4]
        old_s, new_s, arrive, leave = refs[-4:]
        reads, writes = [], []
        for n, (group, at) in enumerate(plan):
            for i in range(4):
                old = state_refs[4 * group + i].at[at]
                reads.append(pltpu.make_async_copy(old, old_s.at[n, i], arrive.at[n, i]))
                new = out_refs[4 * group + i].at[at]
                writes.append(pltpu.make_async_copy(new_s.at[n, i], new, leave.at[n, i]))
        for copy in reads:
            copy.start()
        for n in range(count):
            grad = make_grad(n, grad_refs)
            for copy in reads[4 * n : 4 * n + 4]:
                copy.wait()
            weight, *old = [old_s[n, i] for i in range(4)]
            for i, value in enumerate(adam_step(weight, grad, *old, rate_matrix)):
                new_s[n, i] = value
            for copy in writes[4 * n : 4 * n + 4]:
                copy.start()
        for copy in writes:
            copy.wait()

    flat = [x for group in groups for x in group]
    kept, aliases = [], {}
    for g, arrays in enumerate(before):
        for i, x in enumerate(arrays or ()):
            aliases[1 + len(grads) + held + len(kept)] = 4 * g + i
            kept.append(x)
    anywhere = pl.BlockSpec(memory_space=pl.ANY)
    return row_call(
        body,
        name,
        chain,
        (*grads, *flat, *kept),
        [fixed_spec(grad.shape) for grad in grads] + [anywhere] * (held + len(kept)),
        (anywhere,) * held,
        tuple(shape_of(x.shape, wide) for x in flat),
        scratch=[pltpu.VMEM((count, 4) + slab, wide)] * 2 + [pltpu.SemaphoreType.DMA((count, 4))] * 2,
        aliases=aliases,
    )


def per_device(
    tokens,
    seg_ids,
    time_steps,
    cotangent,
    weight_cols,
    weight_rows,
    bias_cols,
    bias_rows,
    first_cols,
    first_rows,
    first_bias_cols,
    first_bias_rows,
    second_cols,
    second_rows,
    second_bias_cols,
    second_bias_rows,
    ema_cols,
    ema_rows,
    ema_bias_cols,
    ema_bias_rows,
):
    own_width = weight_cols.shape[2]
    own_depth = weight_cols.shape[1]
    width = tokens.shape[1]
    rows = time_steps.shape[0]
    slots = time_steps.shape[1]
    token_count = tokens.shape[0]
    row_len = token_count // rows
    units = row_len // UNIT
    quarter = row_len // 4
    own_units = units // 4
    dp_count = width // own_depth
    dp_place = lax.axis_index("dp")
    slot_count = rows * slots
    mp_place = lax.axis_index("mp")
    core, chip = mp_place % 2, mp_place // 2
    place = (2 * core + chip).astype(jnp.int32)
    place_arg = place.reshape(1)

    chain = Chain(place_arg)

    ring = dp_count in (4, 8)
    known = jnp.zeros((dp_count,) + time_steps.shape, time_steps.dtype)
    known = lax.dynamic_update_slice_in_dim(known, time_steps[None], dp_place, 0)
    known, weight_cols, weight_rows = lax.optimization_barrier((known, weight_cols, weight_rows))
    cols_low = weight_cols.astype(low)
    own_rows = weight_rows.astype(low).transpose(2, 0, 1).reshape(own_depth, 5 * own_width)
    own_first = jnp.concatenate([cols_low[0], cols_low[1], cols_low[2], own_rows[:, :own_width]], 1)
    own_rest = jnp.concatenate([cols_low[5 + i] for i in range(4)] + [own_rows[:, own_width:]], 1)

    half_width = width // 2
    feature = dp_place * own_depth + jnp.arange(own_depth)
    is_cos = feature < half_width
    index = jnp.where(is_cos, feature, feature - half_width).astype(wide)
    frequency = jnp.exp(-math.log(10000.0) * index / half_width)

    def embed(steps):
        angles = steps.astype(wide)[:, None] * frequency[None, :]
        table = jnp.where(is_cos[None, :], jnp.cos(angles), jnp.sin(angles))
        return table.astype(low), jax.nn.silu(table).astype(low)

    near_maps = [jnp.concatenate([cols_low[i], cols_low[i + 1]], 1) for i in (9, 3)]
    far_maps = jnp.concatenate([cols_low[i] for i in (11, 12, 13, 14)], 1)

    def slot_products(pairs):
        out = jnp.concatenate([dot_as(left, maps, DOT_NN).astype(low) for left, maps in pairs], 1)
        return out.reshape(dp_count, rows * slots, -1)

    if ring:
        known = share_hop(known, 1, dp_count)
        known, own_first = lax.optimization_barrier((known, own_first))
        first_gather = RingGather(own_first, dp_count)

        def beside(value):
            value, first_gather.ahead, first_gather.behind = lax.optimization_barrier(
                (value, first_gather.ahead, first_gather.behind)
            )
            if first_gather.left > 0:
                first_gather.hop()
            return value

        known = beside(share_hop(known, 2, dp_count))
        if dp_count == 8:
            known = share_hop(known, 4, dp_count)
        time_low, ada_low = embed(known.reshape(-1))
        near = beside(slot_products([(ada_low, near_maps[0]), (time_low, near_maps[1])]))
        near = HalvingSum(near, dp_count)
        near.hop()
        if dp_count == 8:
            near.parts = beside(near.kept + near.got.astype(wide))
            near.step *= 2
            near.send()
        near.got = beside(near.got)
        near.hop()
        near = near.parts[0]
    else:
        w_first = lax.all_gather(own_first, "dp", axis=0, tiled=True)
        w_rest = lax.all_gather(own_rest, "dp", axis=0, tiled=True)
        time_low, ada_low = embed(lax.all_gather(time_steps, "dp", axis=0, tiled=True).reshape(-1))
        near = slot_products([(ada_low, near_maps[0]), (time_low, near_maps[1])])
        near = lax.psum_scatter(near, "dp", scatter_dimension=0, tiled=True)[0].astype(wide)

    seg_grid = seg_ids.reshape(rows, row_len)
    unit_seg = seg_grid.reshape(rows, units, UNIT)[:, :, 0]
    onehot = unit_seg[:, :, None] == jnp.arange(slots, dtype=jnp.int32)
    blocks = onehot[:, :, None, :] & (jnp.arange(rows)[:, None] == jnp.arange(rows))[:, None, :, None]
    blocks = blocks.reshape(rows * units, rows * slots)
    seg_place = unit_seg.reshape(rows, 4, own_units)
    seg_place = jnp.stack(
        [
            lax.dynamic_index_in_dim(seg_place, jnp.bitwise_xor(place, j), 1, keepdims=False)
            for j in range(4)
        ],
        0,
    )
    row_slots = seg_place + slots * jnp.arange(rows)[None, :, None]

    def field_slots(field):
        return row_slots + slot_count * field

    def slot_matrix(to, height):
        to = jnp.concatenate(to, 1).reshape(1, -1)
        return (jnp.arange(height)[:, None] == to).astype(low)

    spare = 4 * slot_count
    far_to = []
    for r in range(rows):
        far_to += [field_slots(f)[:, r] for f in range(3)] + [jnp.full((4, own_units), -1)]
    for r in range(rows):
        far_to += [field_slots(3)[:, r], jnp.full((4, 4), -1)]
    near_to = [field_slots(f)[:, r] for r in range(rows) for f in range(2)]
    moved = row_slots.transpose(1, 0, 2).reshape(-1, 1) == jnp.arange(slot_count)[None, :]
    quarters = [(r * 4 + jnp.bitwise_xor(place, j)) * quarter for j in range(4) for r in range(rows)]
    seg_rows = [seg_grid[r].reshape(1, row_len) for r in range(rows)]
    hot, far_matrix, near_matrix, moved, at, *segs = chain.tie(
        blocks.astype(low),
        slot_matrix(far_to, spare + 16),
        slot_matrix(near_to, 2 * slot_count),
        moved.astype(wide),
        jnp.stack(quarters).astype(jnp.int32),
        *seg_rows,
    )
    seg_rows = segs

    mp_arg = mp_place.astype(jnp.int32).reshape(1)

    def tables(spread, fields):
        spread.forward()
        pieces = [spread.own, spread.core, spread.chip, spread.both]
        return unit_tables(chain, mp_arg, hot, pieces, fields, own_units)

    far = slot_products([(lax.optimization_barrier((ada_low, near))[0], far_maps)])
    near_mod = (near[:, : 2 * own_width] + bias_cols[6:8].reshape(1, -1)).astype(low)
    near_spread = GroupGather(near_mod)
    if ring:
        far = HalvingSum(far, dp_count)
        near_spread.chip, own_rest = lax.optimization_barrier((near_spread.chip, own_rest))
        rest_gather = RingGather(own_rest, dp_count)
    near_tab = tables(near_spread, 2)
    if ring:
        w_first = first_gather.place(chain)
    time_add = jnp.concatenate(
        [
            near[:, 2 * own_width : 3 * own_width] + bias_cols[0],
            jnp.zeros((rows * slots, own_width), wide),
            near[:, 3 * own_width :] + bias_cols[1],
        ],
        1,
    )
    add_tab = jnp.dot(blocks.astype(wide), time_add, precision=highest)
    add_tab = add_tab.reshape(rows * 4, own_units, 3 * own_width)

    block, half_block = (quarter, width), (row_len // 2, width)
    qkv_width = 3 * own_width
    half = row_len // 2
    lows = lambda *shape: shape_of(shape, low)
    wides = lambda *shape: shape_of(shape, wide)

    def own_block(r):
        return pl.BlockSpec(block, lambda i, p: (r * 4 + p[0], 0))

    def moved_blocks(r):
        return [
            pl.BlockSpec(block, lambda i, p: (r * 4 + jnp.bitwise_xor(p[0], 2 * i), 0)),
            pl.BlockSpec(block, lambda i, p: (r * 4 + jnp.bitwise_xor(p[0], 2 * i + 1), 0)),
        ]

    def moved_tables(tab, r):
        shape = (1,) + tab.shape[1:]
        return [
            pl.BlockSpec(shape, lambda i, p: (r * 4 + jnp.bitwise_xor(p[0], 2 * i), 0, 0)),
            pl.BlockSpec(shape, lambda i, p: (r * 4 + jnp.bitwise_xor(p[0], 2 * i + 1), 0, 0)),
        ]

    def own_table(tab, r):
        return pl.BlockSpec((1,) + tab.shape[1:], lambda i, p: (r * 4 + p[0], 0, 0))

    here = fixed_spec(block)
    half_step = pl.BlockSpec(half_block, lambda i, p: (i, 0))
    half_fixed = fixed_spec(half_block)

    def open_row(r):
        return row_call(
            open_kernel,
            "open_row",
            chain,
            (tokens, tokens, near_tab, near_tab, add_tab, add_tab, w_first),
            moved_blocks(r) + moved_tables(near_tab, r) + moved_tables(add_tab, r) + [fixed_spec(w_first.shape)],
            (half_step, pl.BlockSpec((half, qkv_width), lambda i, p: (i, 0))),
            (lows(row_len, width), lows(row_len, qkv_width)),
            grid=2,
            flops=2 * row_len * width * qkv_width,
        )

    inputs_one, qkvs, mixed, parts = [], [], [], []

    def open_attend(r, between):
        a_one, qkv = open_row(r)
        inputs_one.append(a_one)
        qkvs.append(qkv)
        between()
        out, kept, sent = attend_forward(chain, qkv, seg_rows[r], w_first)
        mixed.append(out)
        parts.append(GroupSum(kept, sent))

    def both_hop():
        if ring:
            far.hop()
            rest_gather.hop()
            chain.land(*far.flying(), *rest_gather.flying())

    def far_spread():
        held = far.parts[0] if ring else lax.psum_scatter(far, "dp", scatter_dimension=0, tiled=True)[0]
        return GroupGather((held.astype(wide) + bias_cols[8:12].reshape(1, -1)).astype(low))

    def second_between():
        parts[0].cross()
        chain.land((parts[0], "last"))
        if ring:
            far.hop()
            chain.land(*rest_gather.flying())
        spreads.append(far_spread())
        chain.land(*spreads[0].flying())

    spreads = []
    if ring:
        chain.land(*far.flying(), *rest_gather.flying())
    open_attend(0, both_hop)
    if ring:
        far.hop()
        rest_gather.hop()
        chain.land(*far.flying())
    chain.land((parts[0], "got"))
    open_attend(1, second_between)
    if ring:
        rest_gather.hop()
    far_tab = tables(spreads[0], 4)

    attendeds, hiddens, inputs_two, down_grads = [], [], [], []

    def first_norm(r):
        attended, hidden, a_two = row_call(
            first_kernel,
            "first_norm",
            chain,
            (tokens, *parts[r].terms(), bias_rows, far_tab),
            [own_block(r), here, here, here, fixed_spec(bias_rows.shape), own_table(far_tab, r)],
            (here, here, here),
            (wides(*block), wides(*block), lows(*block)),
        )
        attendeds.append(attended)
        hiddens.append(hidden)
        inputs_two.append(GroupGather(a_two))

    def down_back(r):
        grads = row_call(
            down_back_kernel,
            "down_back",
            chain,
            (cotangent, cotangent, far_tab, far_tab, w_rest),
            moved_blocks(r) + moved_tables(far_tab, r) + [w_down_spec],
            (half_step, half_step),
            (lows(row_len, width), lows(row_len, width)),
            grid=2,
            flops=2 * row_len * width * width,
        )
        down_grads.append(grads)

    chain.land((parts[-1], "got"))
    first_norm(0)
    parts[-1].cross()
    if ring:
        w_rest = rest_gather.place(chain)
    w_down_spec = pl.BlockSpec((width, w_rest.shape[1] // 2), lambda i, p: (0, 1))
    w_up_spec = pl.BlockSpec((width, w_rest.shape[1] // 2), lambda i, p: (0, 0))
    chain.land(*inputs_two[0].flying())
    down_back(0)
    inputs_two[0].forward()
    chain.land((inputs_two[0], "both"), (parts[-1], "last"))
    down_back(1)
    first_norm(1)

    bias_up = bias_cols[2:6].reshape(1, -1)
    hidden_width = bias_up.shape[1]
    actives, inner_grads, up_parts, up_sums, down_parts = [], [], [], 0.0, []
    for r in range(rows):
        if r + 1 < rows:
            chain.land(*inputs_two[r + 1].flying())
        if r:
            chain.land((up_parts[r - 1], "last"), (down_parts[r - 1], "got"))
        active, inner_grad, kept, sent, sums = row_call(
            up_kernel,
            "up_and_back",
            chain,
            (*inputs_two[r].pieces(), down_grads[r][1], bias_up, w_rest),
            [here] * 4 + [half_step, fixed_spec(bias_up.shape), w_up_spec],
            (
                pl.BlockSpec((half, hidden_width), lambda i, p: (i, 0)),
                pl.BlockSpec((half, hidden_width), lambda i, p: (i, 0)),
                half_fixed,
                half_fixed,
                pl.BlockSpec((1, 8, hidden_width), lambda i, p: (i, 0, 0)),
            ),
            (
                lows(row_len, hidden_width),
                lows(row_len, hidden_width),
                lows(half, width),
                lows(half, width),
                wides(2, 8, hidden_width),
            ),
            grid=2,
            scratch=[pltpu.VMEM(half_block, low)],
            flops=4 * row_len * width * hidden_width,
        )
        actives.append(active)
        inner_grads.append(inner_grad)
        up_parts.append(GroupSum(kept, sent))
        up_sums = up_sums + jnp.sum(sums, axis=(0, 1))
        chain.land((up_parts[r], "got"))
        if r + 1 < rows:
            inputs_two[r + 1].forward()
            chain.land((inputs_two[r + 1], "both"))
        if r:
            down_parts[r - 1].cross()
            chain.land((down_parts[r - 1], "last"))
        kept, sent = row_call(
            down_kernel,
            "down",
            chain,
            (active, w_rest),
            [pl.BlockSpec((half, hidden_width), lambda i, p: (i, 0)), w_down_spec],
            (half_fixed, half_fixed),
            (lows(half, width), lows(half, width)),
            grid=2,
            flops=2 * row_len * width * hidden_width,
        )
        down_parts.append(GroupSum(kept, sent))
        up_parts[r].cross()

    grad_hiddens, grad_gathers, second_sums = [], [], []

    def second_norm(r):
        grad_hidden, grad_attended, sums = row_call(
            second_kernel,
            "second_norm",
            chain,
            (cotangent, *up_parts[r].terms(), hiddens[r], attendeds[r], far_tab),
            [own_block(r)] + [here] * 5 + [own_table(far_tab, r)],
            (here, here, fixed_spec((16, width))),
            (wides(*block), lows(*block), wides(16, width)),
        )
        grad_hiddens.append(grad_hidden)
        grad_gathers.append(GroupGather(grad_attended))
        second_sums.append(sums)

    chain.land((down_parts[-1], "got"))
    second_norm(0)
    down_parts[-1].cross()
    chain.land((up_parts[-1], "last"), *grad_gathers[0].flying())
    rest_grad = weight_grad(
        chain,
        [
            [(inputs_two[r].pieces(), inner_grads[r]) for r in range(rows)],
            [([down_grads[r][0]], actives[r]) for r in range(rows)],
        ],
        "grad_rest",
    )
    rest_ring = RingSum(rest_grad, dp_count)
    grad_gathers[0].forward()
    chain.land((grad_gathers[0], "both"))
    second_norm(1)

    def out_rows():
        args, specs = [bias_rows], [fixed_spec(bias_rows.shape)]
        for r in range(rows):
            args += [cotangent, *down_parts[r].terms(), hiddens[r], far_tab, second_sums[r]]
            specs += [own_block(r)] + [here] * 4 + [own_table(far_tab, r), fixed_spec((16, width))]
        own, sums = row_call(
            out_kernel,
            "out_tokens",
            chain,
            args,
            specs,
            (fixed_spec((rows * quarter + 16, width)), fixed_spec((8 * rows, width))),
            (lows(rows * quarter + 16, width), wides(8 * rows, width)),
        )
        return GroupGather(own), sums

    def part(held, which, columns):
        return lax.dynamic_slice_in_dim(held, which * columns, columns, 1)

    class Exchange:
        def __init__(self, values):
            values = values.astype(low)
            self.mine = part(values, chip, 2 * own_width)
            self.other = lax.ppermute(part(values, 1 - chip, 2 * own_width), "mp", CHIP_SWAP)

        def cross(self):
            values = self.whole()
            self.mine = part(values, core, own_width)
            self.other = lax.ppermute(part(values, 1 - core, own_width), "mp", CORE_SWAP)

        def whole(self):
            return jnp.concatenate([self.mine, self.other], 0)

    qkv_grads, one_parts, time_sums = [], [], []

    def backward(r):
        qkv_grad, kept, sent, sums = attend_backward(
            chain, qkvs[r], grad_gathers[r].pieces(), seg_rows[r], w_first
        )
        qkv_grads.append(qkv_grad)
        one_parts.append(GroupSum(kept, sent))
        time_sums.append(sums)

    chain.land(*rest_ring.flying(), *grad_gathers[1].flying(), (down_parts[-1], "last"))
    backward(0)
    rest_ring.hop()
    grad_gathers[1].forward()
    chain.land((one_parts[0], "got"), (grad_gathers[1], "both"))
    out_gather, out_sums = out_rows()
    one_parts[0].cross()
    far_swap = Exchange(jnp.concatenate(second_sums + [out_sums], 0))
    last_hop = slice(0, 1 if dp_count == 8 else 2)
    chain.land(*rest_ring.flying(), (one_parts[0], "last"), (out_gather, "core"))
    backward(1)
    rest_ring.hop()
    chain.land(*rest_ring.flying(), (one_parts[1], "got"), (out_gather, "chip"), (far_swap, "other"))
    first_grad = weight_grad(
        chain,
        [
            [([inputs_one[r]], qkv_grads[r]) for r in range(rows)],
            [(grad_gathers[r].pieces(), mixed[r]) for r in range(rows)],
        ],
        "grad_first",
    )
    first_ring = RingSum(first_grad, dp_count)
    one_parts[1].cross()
    rest_ring.hop()
    out_gather.forward()
    far_swap.cross()

    cols_state = (weight_cols, first_cols, second_cols, ema_cols)
    rows_state = [x.transpose(0, 2, 1) for x in (weight_rows, first_rows, second_rows, ema_rows)]
    cuts = [(r * quarter, quarter) for r in range(rows)]
    chain.land((out_gather, "both"), (far_swap, "other"))
    third_args, third_specs = [], []
    for r in range(rows):
        third_args += [tokens, *one_parts[r].terms(), grad_hiddens[r], near_tab]
        third_specs += [own_block(r)] + [here] * 4 + [own_table(near_tab, r)]
    out_tokens = place_pieces(chain, at, out_gather.pieces(), cuts)
    far_slots = dot_as(far_matrix, far_swap.whole(), DOT_NN)
    own, across, core_own, core_across = [
        x[rows * quarter : rows * quarter + 2].astype(wide) for x in out_gather.pieces()
    ]
    bias_part = (own + across) + (core_own + core_across)
    far_slots = lax.dynamic_update_slice(
        far_slots,
        jnp.concatenate([up_sums.reshape(4, own_width), bias_part.reshape(8, own_width)], 0),
        (spare, 0),
    ).astype(low)
    far_gather = DoublingGather(far_slots, dp_count)
    chain.land(*first_ring.flying(), *rest_ring.flying()[last_hop], *far_gather.flying())
    input_own, third_sums = row_call(
        third_kernel,
        "third_norm",
        chain,
        third_args,
        third_specs,
        (fixed_spec((rows * quarter, width)), fixed_spec((8 * rows, width))),
        (lows(rows * quarter, width), wides(8 * rows, width)),
    )
    first_ring.hop()
    far_gather.hop()
    input_gather = GroupGather(input_own)
    near_swap = Exchange(third_sums)

    def columns_of(ref, at):
        return column(ref[...], at, own_width).astype(wide)

    def map_grad(left, right, field):
        right = right[:, field * slot_count : (field + 1) * slot_count, :]
        return dot_as(left[...], right.reshape(-1, own_width), DOT_TN)

    rest_sum = rest_ring.total()
    chain.land(*first_ring.flying(), *far_gather.flying(), (near_swap, "other"))
    cols_new = adam_slabs(
        chain,
        [(0, i) for i in (5, 6, 7, 8)],
        (rest_sum,),
        lambda n, refs: columns_of(refs[0], n),
        [cols_state],
        [None],
        "adam_up",
    )
    first_ring.hop()
    near_swap.cross()
    far_gather.hop()
    chain.land(*first_ring.flying(), (near_swap, "other"), *far_gather.flying())
    rows_new = adam_slabs(
        chain,
        [(0, i) for i in (1, 2, 3, 4)],
        (rest_sum,),
        lambda n, refs: columns_of(refs[0], 4 + n),
        [rows_state],
        [None],
        "adam_down",
    )
    first_ring.hop()
    far_all = far_gather.whole()
    unit_sums = jnp.concatenate(time_sums, 0)
    time_slots = lax.dot_general(moved, unit_sums, DOT_TN, precision=highest)
    near_slots = jnp.concatenate(
        [
            dot_as(near_matrix, near_swap.whole(), DOT_NN),
            time_slots[:, :own_width],
            time_slots[:, 2 * own_width :],
        ],
        0,
    ).astype(low)
    near_gather = DoublingGather(near_slots, dp_count)
    chain.land(*near_gather.flying(), *first_ring.flying()[last_hop], (input_gather, "chip"))
    cols_new = adam_slabs(
        chain,
        [(0, i) for i in (11, 12, 13, 14)],
        (ada_low, far_all),
        lambda n, refs: map_grad(refs[0], refs[1], n),
        [cols_state],
        [cols_new],
        "adam_far",
    )
    near_gather.hop()
    input_gather.forward()
    first_sum = first_ring.total()
    chain.land(*near_gather.flying(), (input_gather, "core"), (input_gather, "both"))
    new = adam_slabs(
        chain,
        [(0, i) for i in (0, 1, 2)] + [(1, 0)],
        (first_sum,),
        lambda n, refs: columns_of(refs[0], n),
        [cols_state, rows_state],
        [cols_new, rows_new],
        "adam_first",
    )
    cols_new, rows_new = new[:4], [x.transpose(0, 2, 1) for x in new[4:]]
    near_gather.hop()
    chain.land(*near_gather.flying())
    input_grads = widen_rows(chain, input_gather.pieces(), rows)
    near_all = near_gather.whole()
    cols_new = adam_slabs(
        chain,
        [(0, i) for i in (9, 10, 3, 4)],
        (ada_low, time_low, near_all),
        lambda n, refs: map_grad(refs[n // 2], refs[2], n),
        [cols_state],
        [cols_new],
        "adam_near",
    )
    far_sum = jnp.sum(far_all.astype(wide), axis=0)
    far_biases = jnp.sum(far_sum[:spare].reshape(4, slot_count, own_width), axis=1)
    bias_up_sum = far_sum[spare : spare + 4]
    bias_rows_sum = far_sum[spare + 4 : spare + 12].reshape(2, width)
    near_sum = jnp.sum(near_all.astype(wide).reshape(dp_count, 4, slot_count, own_width), axis=(0, 2))
    bias_cols_sum = jnp.concatenate([near_sum[2:4], bias_up_sum, near_sum[:2], far_biases], 0)
    bias_cols_new = adam_step(
        bias_cols, bias_cols_sum, first_bias_cols, second_bias_cols, ema_bias_cols, rate_vector
    )
    bias_rows_new = adam_step(
        bias_rows, bias_rows_sum, first_bias_rows, second_bias_rows, ema_bias_rows, rate_vector
    )
    return (out_tokens, input_grads, *cols_new, *rows_new, *bias_cols_new, *bias_rows_new)


def solution(mesh):
    cols, rows, bias = P(None, "dp", "mp"), P(None, "mp", "dp"), P(None, "mp")
    state = (cols, rows, bias, P())
    placed = (P("dp", None), P("dp"), P("dp", None), P("dp", None)) + state * 4
    given = (P("dp", None), P("dp", None)) + (cols,) * 4 + (rows,) * 4 + (bias,) * 4 + (P(),) * 4
    return jax.shard_map(
        per_device, mesh=mesh, in_specs=placed, out_specs=given, check_vma=False
    )
```

```python
import math

import jax
import jax.numpy as jnp
from jax import lax
from jax.experimental import pallas as pl
from jax.experimental.pallas import tpu as pltpu
from jax.sharding import PartitionSpec as P

HEAD_DIM = 72
STEP = 10
UNIT = 64
REACH = 192


highest = lax.Precision.HIGHEST
beta_one = 0.9
beta_two = 0.999
adam_eps = 1e-08
decay_rate = 0.1
rate_matrix = 0.05
rate_vector = 0.5
ema_keep = 0.7
norm_eps = 1e-06
neg_large = -1e30
score_scale = HEAD_DIM**-0.5
two_scale = score_scale * math.log2(math.e)
low = jnp.bfloat16
wide = jnp.float32

DOT_NN = (((1,), (0,)), ((), ()))
DOT_NT = (((1,), (1,)), ((), ()))
DOT_TN = (((0,), (0,)), ((), ()))

COST = 0
VMEM_GRANT = 58 * 2**20
SMEM_SPEC = pl.BlockSpec(memory_space=pltpu.SMEM)

CORE_SWAP = [(i, i ^ 1) for i in range(4)]
CHIP_SWAP = [(i, i ^ 2) for i in range(4)]


def dot_as(left, right, dims):
    return lax.dot_general(left, right, dims, preferred_element_type=wide)


def ring_order(count):
    return list(range(0, count, 2)) + list(range(count - 1, 0, -2))


def ring_perms(count):
    order = ring_order(count)
    onward = [(order[i], order[(i + 1) % count]) for i in range(count)]
    return onward, [(b, a) for a, b in onward]


def ring_spot(count):
    me = lax.axis_index("dp")
    return jnp.where(me % 2 == 0, me // 2, count - 1 - me // 2)


def ring_at(spot, count):
    spot = spot % count
    return jnp.where(spot < count // 2, 2 * spot, 2 * (count - 1 - spot) + 1)


def ring_places(rows, count):
    spot = ring_spot(count)
    back = [0]
    for hop in range(1, count // 2):
        back += [-hop, hop]
    at = ring_at(spot + jnp.array(back + [count // 2] * 2), count) * rows
    return (at + jnp.array([0] * len(back) + [0, rows // 32 * 16])).astype(jnp.int32)


def place_pieces(chain, at, pieces, cuts=None):
    parts = [(n, *cut) for n, piece in enumerate(pieces) for cut in cuts or [(0, piece.shape[0])]]
    whole = (sum(count for _, _, count in parts),) + pieces[0].shape[1:]
    at = chain.tie(at)

    def body(at_ref, *refs):
        out_ref, held, sem_in, sem_out = refs[-4:]
        arrive, leave = [], []
        base = 0
        for i, (n, start, count) in enumerate(parts):
            spot = held.at[pl.ds(base, count)]
            piece = refs[n].at[pl.ds(start, count)]
            arrive.append(pltpu.make_async_copy(piece, spot, sem_in.at[i]))
            to = out_ref.at[pl.ds(pl.multiple_of(at_ref[i], 16), count)]
            leave.append(pltpu.make_async_copy(spot, to, sem_out.at[i]))
            base += count
        for copy in arrive:
            copy.start()
        for first, second in zip(arrive, leave):
            first.wait()
            second.start()
        for copy in leave:
            copy.wait()

    out = pl.pallas_call(
        body,
        out_shape=jax.ShapeDtypeStruct(whole, pieces[0].dtype),
        in_specs=[SMEM_SPEC] + [pl.BlockSpec(memory_space=pl.ANY)] * len(pieces),
        out_specs=pl.BlockSpec(memory_space=pl.ANY),
        scratch_shapes=[pltpu.VMEM(whole, pieces[0].dtype)]
        + [pltpu.SemaphoreType.DMA((len(parts),))] * 2,
        compiler_params=pltpu.CompilerParams(vmem_limit_bytes=VMEM_GRANT),
        cost_estimate=pl.CostEstimate(flops=1, bytes_accessed=1, transcendentals=0),
        name="place_pieces",
    )(at, *pieces)
    return chain.close(out)


class Chain:
    def __init__(self, token):
        self.token = token

        self.landing = []

    def tie(self, *arrays):
        self.token, *arrays = lax.optimization_barrier((self.token, *arrays))
        return arrays[0] if len(arrays) == 1 else tuple(arrays)

    def land(self, *transfers):
        self.landing += transfers

    def close(self, *arrays):
        landing, self.landing = self.landing, []
        values = self.tie(*arrays, *[getattr(held, name) for held, name in landing])
        values = values if isinstance(values, tuple) else (values,)
        for (held, name), value in zip(landing, values[len(arrays) :]):
            setattr(held, name, value)
        return values[0] if len(arrays) == 1 else values[: len(arrays)]


class RingSum:
    def __init__(self, parts, count):
        self.parts, self.count = parts, count
        self.left = count // 2 - 1 if count in (4, 8) else 0
        if self.left:
            self.rows = parts.shape[0] // count
            self.onward, self.backward = ring_perms(count)
            self.spot = ring_spot(count)
            self.send(self.chunk(count // 2), self.chunk(1 - count // 2))

    def chunk(self, ahead):
        at = ring_at(self.spot + ahead, self.count) * self.rows
        return lax.dynamic_slice_in_dim(self.parts, at, self.rows, 0).astype(wide)

    def send(self, ahead, behind):
        self.ahead = lax.ppermute(ahead.astype(low), "dp", self.onward)
        if behind is not None:
            self.behind = lax.ppermute(behind.astype(low), "dp", self.backward)

    def flying(self):
        return [(self, "ahead"), (self, "behind")] if self.count in (4, 8) else []

    def hop(self):
        if not self.left:
            return
        ahead = self.ahead.astype(wide) + self.chunk(self.left)
        behind = None
        if self.left > 1:
            behind = self.behind.astype(wide) + self.chunk(1 - self.left)
        self.send(ahead, behind)
        self.left -= 1

    def total(self):
        if self.count not in (4, 8):
            return lax.psum_scatter(self.parts, "dp", scatter_dimension=0, tiled=True).astype(wide)
        total = self.ahead.astype(wide) + self.behind.astype(wide) + self.chunk(0)
        return total.astype(low)


class GroupSum:
    def __init__(self, kept, sent):
        self.kept, self.got = kept, lax.ppermute(sent, "mp", CORE_SWAP)

    def cross(self):
        quarter = self.kept.shape[0] // 2
        passed = self.kept[quarter:].astype(wide) + self.got[quarter:].astype(wide)
        passed = passed.astype(low)
        self.last = lax.ppermute(passed, "mp", CHIP_SWAP)

    def terms(self):
        return self.kept, self.got, self.last


class GroupGather:
    def __init__(self, own):
        self.own = own
        self.chip = lax.ppermute(own, "mp", CHIP_SWAP)
        self.core = lax.ppermute(own, "mp", CORE_SWAP)

    def forward(self):
        self.both = lax.ppermute(self.chip, "mp", CORE_SWAP)

    def flying(self):
        return [(self, "chip"), (self, "core")]

    def pieces(self):
        return [self.own, self.chip, self.core, self.both]

    def in_order(self, mp_place):
        return in_group_order([self.own, self.core, self.chip, self.both], mp_place)


class DoublingGather:
    def __init__(self, shard, count):
        self.shard, self.count = shard, count
        self.known, self.step = shard[None], count // 2 if count in (4, 8) else 0
        self.send()

    def send(self):
        if self.step:
            swap = [(i, i ^ self.step) for i in range(self.count)]
            self.got = lax.ppermute(self.known, "dp", swap)

    def join(self, got):
        second = lax.axis_index("dp") // self.step % 2 == 1
        pair = [jnp.where(second, got, self.known), jnp.where(second, self.known, got)]
        self.known = jnp.stack(pair, 1).reshape((-1,) + self.shard.shape)
        self.step //= 2

    def flying(self):
        return [(self, "got")] if self.step else []

    def hop(self):
        if self.step > 1:
            self.join(self.got)
            self.send()

    def whole(self):
        if self.step:
            self.join(self.got)
        if self.count not in (4, 8):
            return lax.all_gather(self.shard, "dp", axis=0, tiled=False)
        return self.known


class HalvingSum:
    def __init__(self, parts, count):
        self.parts, self.count, self.step = parts, count, 1
        self.send()

    def send(self):
        pairs = self.parts.reshape((self.parts.shape[0] // 2, 2) + self.parts.shape[1:])
        bit = lax.axis_index("dp") // self.step % 2
        sent = lax.dynamic_index_in_dim(pairs, 1 - bit, 1, keepdims=False).astype(low)
        self.kept = lax.dynamic_index_in_dim(pairs, bit, 1, keepdims=False).astype(wide)
        swap = [(i, i ^ self.step) for i in range(self.count)]
        self.got = lax.ppermute(sent, "dp", swap)

    def flying(self):
        return [(self, "got")] if self.step < self.count else []

    def hop(self):
        if self.step < self.count:
            self.parts = self.kept + self.got.astype(wide)
            self.step *= 2
            if self.step < self.count:
                self.send()


class RingGather:
    def __init__(self, shard, count):
        self.count, self.left = count, count // 2 - 1
        self.onward, self.backward = ring_perms(count)
        self.pieces = [shard]
        self.send(shard, shard)

    def send(self, ahead, behind):
        self.ahead = lax.ppermute(ahead, "dp", self.onward)
        self.behind = lax.ppermute(behind, "dp", self.backward)

    def flying(self):
        return [(self, "ahead"), (self, "behind")]

    def hop(self):
        ahead, behind = self.ahead, self.behind
        self.pieces += [ahead, behind]
        if self.left > 1:
            self.send(ahead, behind)
        elif self.left == 1:
            cut = ahead.shape[0] // 32 * 16
            self.send(ahead[:cut], behind[cut:])
        self.left -= 1

    def place(self, chain):
        while self.left >= 0:
            self.hop()
        return place_pieces(chain, ring_places(self.pieces[0].shape[0], self.count), self.pieces)


def share_hop(known, reach, count):
    return known + lax.ppermute(known, "dp", [(i, i ^ reach) for i in range(count)])


def in_group_order(pieces, place):
    stacked = jnp.stack(pieces, 0)
    return [
        lax.dynamic_index_in_dim(stacked, jnp.bitwise_xor(place, j), 0, keepdims=False)
        for j in range(4)
    ]


def key_windows(row_len, block):
    return [
        (at, max(0, at - REACH), min(row_len, at + block + REACH))
        for at in range(0, row_len, block)
    ]


def relative_at(place, j, block):
    return pl.multiple_of(jnp.bitwise_xor(place, j) * block, block)


def attend_forward_kernel(
    place_ref, qkv_ref, seg_row_ref, w_ref, out_ref, kept_ref, sent_ref, q_s, k_s, v_s, *, heads
):
    row_len = qkv_ref.shape[0]
    width = heads * HEAD_DIM
    block = row_len // 4
    place = place_ref[0]
    for j in range(4):
        at = relative_at(place, j, block)
        to = slice(j * block, (j + 1) * block)
        for h in range(heads):
            c = h * HEAD_DIM
            q_s[h, to, :] = qkv_ref[pl.ds(at, block), c : c + HEAD_DIM]
            k_s[h, to, :] = qkv_ref[pl.ds(at, block), width + c : width + c + HEAD_DIM]
            v_s[h, to, :] = qkv_ref[pl.ds(at, block), 2 * width + c : 2 * width + c + HEAD_DIM]
    for j, (at, start, stop) in enumerate(key_windows(row_len, block)):
        keys_seg = jnp.broadcast_to(seg_row_ref[:, start:stop], (8, stop - start)).T[:, :1]
        same = keys_seg == seg_row_ref[:, at : at + block]
        mixed = []
        for h in range(heads):
            scores = dot_as(k_s[h, start:stop, :], q_s[h, at : at + block, :], DOT_NT)
            scores = jnp.where(same, scores, neg_large)
            top = jnp.max(scores, axis=0, keepdims=True)
            weights = jnp.exp2((scores - top) * two_scale)
            total = jnp.sum(weights, axis=0, keepdims=True)
            gathered = dot_as(v_s[h, start:stop, :], weights.astype(low), DOT_TN)
            mixed.append(gathered * (1.0 / total))
        out_ref[pl.ds(relative_at(place, j, block), block), :] = (
            jnp.concatenate(mixed, axis=0).T.astype(low)
        )
    w_out = w_ref[:, w_ref.shape[1] - width :]
    half = row_len // 2
    kept_ref[...] = dot_as(out_ref[:half, :], w_out, DOT_NT).astype(low)
    sent_ref[...] = dot_as(out_ref[half:, :], w_out, DOT_NT).astype(low)


def attend_backward_kernel(
    place_ref, qkv_ref, g0_ref, g1_ref, g2_ref, g3_ref, seg_row_ref, w_ref,
    out_ref, kept_ref, sent_ref, sums_ref, q_s, k_s, v_s, g_s, dk_s, dv_s, *, heads
):
    row_len = qkv_ref.shape[0]
    width = heads * HEAD_DIM
    block = row_len // 4
    place = place_ref[0]
    dk_s[...] = jnp.zeros_like(dk_s)
    dv_s[...] = jnp.zeros_like(dv_s)
    w_out = w_ref[:, 3 * width :]
    for j, g_ref in enumerate((g0_ref, g1_ref, g2_ref, g3_ref)):
        grad = dot_as(g_ref[...], w_out, DOT_NN).astype(low)
        at = relative_at(place, j, block)
        for h in range(heads):
            g_s[h, pl.ds(at, block), :] = grad[:, h * HEAD_DIM : (h + 1) * HEAD_DIM]
    for j in range(4):
        at = relative_at(place, j, block)
        to = slice(j * block, (j + 1) * block)
        for h in range(heads):
            c = h * HEAD_DIM
            q_s[h, to, :] = qkv_ref[pl.ds(at, block), c : c + HEAD_DIM]
            k_s[h, to, :] = qkv_ref[pl.ds(at, block), width + c : width + c + HEAD_DIM]
            v_s[h, to, :] = qkv_ref[pl.ds(at, block), 2 * width + c : 2 * width + c + HEAD_DIM]
    for j, (at, start, stop) in enumerate(key_windows(row_len, block)):
        keys_seg = jnp.broadcast_to(seg_row_ref[:, start:stop], (8, stop - start)).T[:, :1]
        same = keys_seg == seg_row_ref[:, at : at + block]
        grads = []
        for h in range(heads):
            query = q_s[h, at : at + block, :]
            grad = g_s[h, at : at + block, :]
            keys = k_s[h, start:stop, :]
            scores = jnp.where(same, dot_as(keys, query, DOT_NT), neg_large)
            top = jnp.max(scores, axis=0, keepdims=True)
            weights = jnp.exp2((scores - top) * two_scale)
            probs = weights * (1.0 / jnp.sum(weights, axis=0, keepdims=True))
            grad_probs = dot_as(v_s[h, start:stop, :], grad, DOT_NT)
            inner = jnp.sum(grad_probs * probs, axis=0, keepdims=True)
            grad_scores = (probs * (grad_probs - inner)).astype(low)
            dv_s[h, start:stop, :] += dot_as(probs.astype(low), grad, DOT_NN)
            dk_s[h, start:stop, :] += dot_as(grad_scores, query, DOT_NN)
            grads.append(dot_as(keys, grad_scores, DOT_TN) * score_scale)
        out_ref[pl.ds(relative_at(place, j, block), block), 0:width] = (
            jnp.concatenate(grads, axis=0).T.astype(low)
        )
    for j in range(4):
        at = slice(j * block, (j + 1) * block)
        to = relative_at(place, j, block)
        out_ref[pl.ds(to, block), width : 2 * width] = jnp.concatenate(
            [(dk_s[h, at, :] * score_scale).astype(low) for h in range(heads)], axis=1
        )
        out_ref[pl.ds(to, block), 2 * width : 3 * width] = jnp.concatenate(
            [dv_s[h, at, :].astype(low) for h in range(heads)], axis=1
        )
    half = row_len // 2
    w_qkv = w_ref[:, : 3 * width]
    kept_ref[...] = dot_as(out_ref[:half, :], w_qkv, DOT_NT).astype(low)
    sent_ref[...] = dot_as(out_ref[half:, :], w_qkv, DOT_NT).astype(low)
    for u in range(row_len // UNIT):
        sums_ref[u : u + 1, :] = jnp.sum(
            out_ref[u * UNIT : (u + 1) * UNIT, :].astype(wide), axis=0, keepdims=True
        )


def shape_of(shape, kind):
    return jax.ShapeDtypeStruct(shape, kind)


def attend_forward(chain, qkv, seg_row, weights):
    row_len, width = qkv.shape[0], qkv.shape[1] // 3
    heads = width // HEAD_DIM
    full = weights.shape[0]
    args = (qkv, seg_row, weights)
    shapes = (
        shape_of((row_len, width), low),
        shape_of((row_len // 2, full), low),
        shape_of((row_len // 2, full), low),
    )

    def body(*refs):
        attend_forward_kernel(*refs, heads=heads)

    return row_call(
        body,
        "attend_forward",
        chain,
        args,
        [fixed_spec(arg.shape) for arg in args[:2]]
        + [pl.BlockSpec((full, weights.shape[1] // 3), lambda i, p: (0, 2))],
        tuple(fixed_spec(shape.shape) for shape in shapes),
        shapes,
        scratch=[pltpu.VMEM((heads, row_len, HEAD_DIM), low)] * 3,
        flops=4 * row_len * 640 * width + 2 * row_len * width * full,
        exps=heads * row_len * 640,
    )


def attend_backward(chain, qkv, grads, seg_row, weights):
    row_len, width = qkv.shape[0], qkv.shape[1] // 3
    heads = width // HEAD_DIM
    full = weights.shape[0]
    args = (qkv, *grads, seg_row, weights)
    shapes = (
        shape_of((row_len, 3 * width), low),
        shape_of((row_len // 2, full), low),
        shape_of((row_len // 2, full), low),
        shape_of((row_len // UNIT, 3 * width), wide),
    )

    def body(*refs):
        attend_backward_kernel(*refs, heads=heads)

    return row_call(
        body,
        "attend_backward",
        chain,
        args,
        [fixed_spec(arg.shape) for arg in args],
        tuple(fixed_spec(shape.shape) for shape in shapes),
        shapes,
        scratch=[pltpu.VMEM((heads, row_len, HEAD_DIM), low)] * 4
        + [pltpu.VMEM((heads, row_len, HEAD_DIM), wide)] * 2,
        flops=10 * row_len * 640 * width + 8 * row_len * width * full,
        exps=heads * row_len * 640,
    )


def norm_parts(values):
    centre = values - jnp.mean(values, axis=-1, keepdims=True)
    inverse = lax.rsqrt(jnp.mean(centre * centre, axis=-1, keepdims=True) + norm_eps)
    return centre * inverse, inverse


def norm_back(normed, inverse, grad):
    return inverse * (
        grad
        - jnp.mean(grad, axis=-1, keepdims=True)
        - normed * jnp.mean(grad * normed, axis=-1, keepdims=True)
    )


def unit_rows(ref):
    return [(u, slice(u * UNIT, (u + 1) * UNIT)) for u in range(ref.shape[0] // UNIT)]


def column(values, index, width):
    return values[:, index * width : (index + 1) * width]


def open_kernel(
    place_ref, x0_ref, x1_ref, tab0_ref, tab1_ref, add0_ref, add1_ref, w_ref, a_ref, qkv_ref
):
    width = x0_ref.shape[1]
    quarter = x0_ref.shape[0]
    for j, (x_ref, tab_ref) in enumerate(((x0_ref, tab0_ref), (x1_ref, tab1_ref))):
        for u, at in unit_rows(x_ref):
            normed, _ = norm_parts(x_ref[at, :].astype(wide))
            table = tab_ref[0, u : u + 1, :]
            out = normed * (1.0 + column(table, 1, width)) + column(table, 0, width)
            a_ref[j * quarter + u * UNIT : j * quarter + (u + 1) * UNIT, :] = out.astype(low)
    qkv = dot_as(a_ref[...], w_ref[:, : qkv_ref.shape[1]], DOT_NN)
    for j, add_ref in enumerate((add0_ref, add1_ref)):
        for u in range(quarter // UNIT):
            at = slice(j * quarter + u * UNIT, j * quarter + (u + 1) * UNIT)
            qkv_ref[at, :] = (qkv[at, :] + add_ref[0, u : u + 1, :]).astype(low)


def first_kernel(place_ref, x_ref, kept_ref, got_ref, passed_ref, bias_ref, tab_ref, att_ref, hid_ref, a_ref):
    width = x_ref.shape[1]
    for u, at in unit_rows(x_ref):
        table = tab_ref[0, u : u + 1, :]
        attended = kept_ref[at, :].astype(wide) + got_ref[at, :].astype(wide) + passed_ref[at, :].astype(wide)
        attended = attended + bias_ref[0:1, :]
        hidden = x_ref[at, :].astype(wide) + column(table, 0, width) * attended
        normed, _ = norm_parts(hidden)
        att_ref[at, :] = attended
        hid_ref[at, :] = hidden
        a_ref[at, :] = (normed * (1.0 + column(table, 2, width)) + column(table, 1, width)).astype(low)


def down_back_kernel(place_ref, cot0_ref, cot1_ref, tab0_ref, tab1_ref, w_ref, grad_ref, dm_ref):
    width = cot0_ref.shape[1]
    quarter = cot0_ref.shape[0]
    for j, (cot_ref, tab_ref) in enumerate(((cot0_ref, tab0_ref), (cot1_ref, tab1_ref))):
        for u, at in unit_rows(cot_ref):
            gate = column(tab_ref[0, u : u + 1, :], 3, width)
            out = (cot_ref[at, :].astype(wide) * gate).astype(low)
            grad_ref[j * quarter + u * UNIT : j * quarter + (u + 1) * UNIT, :] = out
    dm_ref[...] = dot_as(grad_ref[...], w_ref[...], DOT_NN).astype(low)


def gelu_both(values):
    scale = math.sqrt(2.0 / math.pi)
    square = values * values
    turned = jnp.tanh(scale * values * (1.0 + 0.044715 * square))
    upper = 0.5 * (1.0 + turned)
    slope = upper + 0.5 * values * (1.0 - turned * turned) * scale * (1.0 + 3 * 0.044715 * square)
    return values * upper, slope


def up_kernel(
    place_ref, a0_ref, a1_ref, a2_ref, a3_ref, dm_ref, bias_ref, w_ref, m_ref, dz_ref, kept_ref, sent_ref, sums_ref, a_s
):
    step = pl.program_id(0)
    quarter = a0_ref.shape[0]
    for j, piece in enumerate((a0_ref, a1_ref, a2_ref, a3_ref)):

        @pl.when(step == j // 2)
        def _(piece=piece, j=j):
            a_s[j % 2 * quarter : (j % 2 + 1) * quarter, :] = piece[...]

    sums = jnp.zeros(sums_ref.shape[1:], wide)
    for j in range(2):
        at = slice(j * quarter, (j + 1) * quarter)
        inner = dot_as(a_s[at, :], w_ref[...], DOT_NN) + bias_ref[...]
        active, slope = gelu_both(inner)
        m_ref[at, :] = active.astype(low)
        grad = (dm_ref[at, :].astype(wide) * slope).astype(low)
        dz_ref[at, :] = grad
        sums = sums + jnp.sum(grad.astype(wide).reshape(-1, 8, grad.shape[1]), axis=0)
    sums_ref[0] = sums
    back = dot_as(dz_ref[...], w_ref[...], DOT_NT)

    @pl.when(step == 0)
    def _():
        kept_ref[...] = back.astype(low)

    @pl.when(step == 1)
    def _():
        sent_ref[...] = back.astype(low)


def down_kernel(place_ref, m_ref, w_ref, kept_ref, sent_ref):
    step = pl.program_id(0)
    out = dot_as(m_ref[...], w_ref[...], DOT_NT)

    @pl.when(step == 0)
    def _():
        kept_ref[...] = out.astype(low)

    @pl.when(step == 1)
    def _():
        sent_ref[...] = out.astype(low)


def second_kernel(
    place_ref, cot_ref, kept_ref, got_ref, passed_ref, hid_ref, att_ref, tab_ref, gh_ref, ga_ref, sums_ref
):
    width = cot_ref.shape[1]
    bias = jnp.zeros((1, width), wide)
    sums_ref[...] = jnp.zeros_like(sums_ref)
    for u, at in unit_rows(cot_ref):
        table = tab_ref[0, u : u + 1, :]
        grad_two = kept_ref[at, :].astype(wide) + got_ref[at, :].astype(wide) + passed_ref[at, :].astype(wide)
        normed, inverse = norm_parts(hid_ref[at, :])
        grad = cot_ref[at, :].astype(wide) + norm_back(
            normed, inverse, grad_two * (1.0 + column(table, 2, width))
        )
        grad_att = grad * column(table, 0, width)
        gh_ref[at, :] = grad
        ga_ref[at, :] = grad_att.astype(low)
        bias = bias + jnp.sum(grad_att, axis=0, keepdims=True)
        sums_ref[u : u + 1, :] = jnp.sum(grad * att_ref[at, :], axis=0, keepdims=True)
        sums_ref[4 + u : 5 + u, :] = jnp.sum(grad_two, axis=0, keepdims=True)
        sums_ref[8 + u : 9 + u, :] = jnp.sum(grad_two * normed, axis=0, keepdims=True)
    sums_ref[12:13, :] = bias


def out_kernel(place_ref, bias_ref, *refs):
    rows = (len(refs) - 2) // 7
    out_ref, sums_ref = refs[-2:]
    quarter, width = refs[0].shape
    total = jnp.zeros((1, width), wide)
    other = jnp.zeros((1, width), wide)
    sums_ref[...] = jnp.zeros_like(sums_ref)
    for r in range(rows):
        cot_ref, kept_ref, got_ref, passed_ref, hid_ref, tab_ref, second_ref = refs[7 * r : 7 * r + 7]
        for u, at in unit_rows(cot_ref):
            gate = column(tab_ref[0, u : u + 1, :], 3, width)
            mlp = kept_ref[at, :].astype(wide) + got_ref[at, :].astype(wide) + passed_ref[at, :].astype(wide)
            mlp = mlp + bias_ref[1:2, :]
            out_ref[r * quarter + u * UNIT : r * quarter + (u + 1) * UNIT, :] = (
                hid_ref[at, :] + gate * mlp
            ).astype(low)
            cot = cot_ref[at, :].astype(wide)
            sums_ref[8 * r + u : 8 * r + u + 1, :] = jnp.sum(cot * mlp, axis=0, keepdims=True)
            total = total + jnp.sum(cot, axis=0, keepdims=True) * gate
        other = other + second_ref[12:13, :]
    tail = jnp.concatenate([other, total, jnp.zeros((14, width), wide)], axis=0)
    out_ref[rows * quarter :, :] = tail.astype(low)


def third_kernel(place_ref, *refs):
    rows = (len(refs) - 2) // 6
    out_ref, sums_ref = refs[-2:]
    quarter, width = refs[0].shape
    for r in range(rows):
        x_ref, kept_ref, got_ref, passed_ref, gh_ref, tab_ref = refs[6 * r : 6 * r + 6]
        for u, at in unit_rows(x_ref):
            grad_one = kept_ref[at, :].astype(wide) + got_ref[at, :].astype(wide) + passed_ref[at, :].astype(wide)
            normed, inverse = norm_parts(x_ref[at, :].astype(wide))
            table = tab_ref[0, u : u + 1, :]
            back = norm_back(normed, inverse, grad_one * (1.0 + column(table, 1, width)))
            out_ref[r * quarter + u * UNIT : r * quarter + (u + 1) * UNIT, :] = (
                gh_ref[at, :] + back
            ).astype(low)
            n = 8 * r + u
            sums_ref[n : n + 1, :] = jnp.sum(grad_one, axis=0, keepdims=True)
            sums_ref[n + 4 : n + 5, :] = jnp.sum(grad_one * normed, axis=0, keepdims=True)


def row_call(
    body, name, chain, args, in_specs, out_specs, out_shape, grid=1, scratch=(), flops=0, exps=0, aliases=None, prefetch=None
):
    moved = sum(math.prod(a.shape) * a.dtype.itemsize for a in args)
    shapes = out_shape if isinstance(out_shape, tuple) else (out_shape,)
    moved += sum(math.prod(o.shape) * o.dtype.itemsize for o in shapes)
    prefetch = chain.token if prefetch is None else chain.tie(prefetch)
    out = pl.pallas_call(
        body,
        grid_spec=pltpu.PrefetchScalarGridSpec(
            num_scalar_prefetch=1,
            grid=(grid,),
            in_specs=in_specs,
            out_specs=out_specs,
            scratch_shapes=scratch,
        ),
        out_shape=out_shape,
        input_output_aliases=aliases or {},
        compiler_params=pltpu.CompilerParams(vmem_limit_bytes=VMEM_GRANT),
        cost_estimate=pl.CostEstimate(
            flops=int(COST * flops) + 1, bytes_accessed=int(COST * moved) + 1, transcendentals=0
        ),
        name=name,
    )(prefetch, *args)
    return chain.close(*out) if isinstance(out_shape, tuple) else chain.close(out)


def fixed_spec(shape):
    return pl.BlockSpec(shape, lambda *_: (0,) * len(shape))


def unit_tables(chain, mp_arg, onehot, pieces, fields, group):
    units, slots = onehot.shape
    own = pieces[0].shape[1] // fields
    shape = (units // group, group, fields * 4 * own)

    def body(mp_ref, hot_ref, *refs):
        out_ref = refs[-1]
        mp_place = mp_ref[0]
        for i, piece in enumerate(refs[:-1]):
            spread = dot_as(hot_ref[...], piece[...], DOT_NN)
            for j in range(4):

                @pl.when(jnp.bitwise_xor(mp_place, i) == j)
                def _(spread=spread, j=j):
                    for f in range(fields):
                        at = f * 4 * own + j * own
                        values = column(spread, f, own)
                        for n in range(units // group):
                            out_ref[n, :, at : at + own] = values[n * group : (n + 1) * group, :]

    return row_call(
        body,
        "unit_tables",
        chain,
        (onehot, *pieces),
        [fixed_spec(onehot.shape)] + [fixed_spec(pieces[0].shape)] * 4,
        fixed_spec(shape),
        shape_of(shape, wide),
        flops=8 * units * slots * own * fields,
        prefetch=mp_arg,
    )


def weight_grad(chain, pairs, name):
    depth = pairs[0][0][0][0].shape[1]
    tile = depth // 3
    widths = [pair[0][1].shape[1] for pair in pairs]
    args, specs, plan = [], [], []
    flops = 0
    for pair in pairs:
        rows = []
        for left, right in pair:
            rows.append((len(args), len(left)))
            args += list(left) + [right]
            specs += [pl.BlockSpec((piece.shape[0], tile), lambda i, p: (0, i)) for piece in left]
            specs.append(fixed_spec(right.shape))
            flops += 2 * depth * math.prod(right.shape)
        plan.append(rows)

    def body(place_ref, *refs):
        out_ref = refs[-1]
        at = 0
        for rows, cols in zip(plan, widths):
            total = None
            for first, count in rows:
                left = [ref[...] for ref in refs[first : first + count]]
                left = left[0] if count == 1 else jnp.concatenate(left, axis=0)
                part = dot_as(left, refs[first + count][...], DOT_TN)
                total = part if total is None else total + part
            out_ref[:, at : at + cols] = total.astype(low)
            at += cols

    return row_call(
        body,
        name,
        chain,
        args,
        specs,
        pl.BlockSpec((tile, sum(widths)), lambda i, p: (i, 0)),
        shape_of((depth, sum(widths)), low),
        grid=3,
        flops=flops,
    )


def widen_rows(chain, pieces, rows):
    quarter, width = pieces[0].shape[0] // rows, pieces[0].shape[1]

    def body(place_ref, *refs):
        out_ref, wide_s, sems = refs[-3:]
        copies = []
        for r in range(rows):
            for j, piece in enumerate(refs[:4]):
                held = wide_s.at[r, j]
                held[...] = piece[r * quarter : (r + 1) * quarter, :].astype(wide)
                at = (r * 4 + jnp.bitwise_xor(place_ref[0], j)) * quarter
                to = out_ref.at[pl.ds(pl.multiple_of(at, quarter), quarter)]
                copies.append(pltpu.make_async_copy(held, to, sems.at[r, j]))
                copies[-1].start()
        for copy in copies:
            copy.wait()

    return row_call(
        body,
        "widen_rows",
        chain,
        tuple(pieces),
        [fixed_spec(pieces[0].shape)] * 4,
        pl.BlockSpec(memory_space=pl.ANY),
        shape_of((rows * 4 * quarter, width), wide),
        scratch=[pltpu.VMEM((rows, 4, quarter, width), wide), pltpu.SemaphoreType.DMA((rows, 4))],
    )


def adam_step(weight, gradient, first_old, second_old, ema_old, step_rate):
    first_new = beta_one * first_old + (1.0 - beta_one) * gradient
    second_new = beta_two * second_old + (1.0 - beta_two) * gradient * gradient
    first_hat = first_new * (1.0 / (1.0 - beta_one**STEP))
    second_hat = second_new * (1.0 / (1.0 - beta_two**STEP))
    weight_new = weight - step_rate * (
        first_hat / (jnp.sqrt(second_hat) + adam_eps) + decay_rate * weight
    )
    ema_new = ema_keep * ema_old + (1.0 - ema_keep) * weight_new
    return (first_new, second_new, weight_new, ema_new)


def adam_slabs(chain, plan, grads, make_grad, groups, before, name):
    slab = groups[0][0].shape[1:]
    count, held = len(plan), 4 * len(groups)

    def body(place_ref, *refs):
        grad_refs, state_refs = refs[: len(grads)], refs[len(grads) : len(grads) + held]
        out_refs = refs[-held - 4 : -4]
        old_s, new_s, arrive, leave = refs[-4:]
        reads, writes = [], []
        for n, (group, at) in enumerate(plan):
            for i in range(4):
                old = state_refs[4 * group + i].at[at]
                reads.append(pltpu.make_async_copy(old, old_s.at[n, i], arrive.at[n, i]))
                new = out_refs[4 * group + i].at[at]
                writes.append(pltpu.make_async_copy(new_s.at[n, i], new, leave.at[n, i]))
        for copy in reads:
            copy.start()
        for n in range(count):
            grad = make_grad(n, grad_refs)
            for copy in reads[4 * n : 4 * n + 4]:
                copy.wait()
            weight, *old = [old_s[n, i] for i in range(4)]
            for i, value in enumerate(adam_step(weight, grad, *old, rate_matrix)):
                new_s[n, i] = value
            for copy in writes[4 * n : 4 * n + 4]:
                copy.start()
        for copy in writes:
            copy.wait()

    flat = [x for group in groups for x in group]
    kept, aliases = [], {}
    for g, arrays in enumerate(before):
        for i, x in enumerate(arrays or ()):
            aliases[1 + len(grads) + held + len(kept)] = 4 * g + i
            kept.append(x)
    anywhere = pl.BlockSpec(memory_space=pl.ANY)
    return row_call(
        body,
        name,
        chain,
        (*grads, *flat, *kept),
        [fixed_spec(grad.shape) for grad in grads] + [anywhere] * (held + len(kept)),
        (anywhere,) * held,
        tuple(shape_of(x.shape, wide) for x in flat),
        scratch=[pltpu.VMEM((count, 4) + slab, wide)] * 2 + [pltpu.SemaphoreType.DMA((count, 4))] * 2,
        aliases=aliases,
    )


def per_device(
    tokens,
    seg_ids,
    time_steps,
    cotangent,
    weight_cols,
    weight_rows,
    bias_cols,
    bias_rows,
    first_cols,
    first_rows,
    first_bias_cols,
    first_bias_rows,
    second_cols,
    second_rows,
    second_bias_cols,
    second_bias_rows,
    ema_cols,
    ema_rows,
    ema_bias_cols,
    ema_bias_rows,
):
    own_width = weight_cols.shape[2]
    own_depth = weight_cols.shape[1]
    width = tokens.shape[1]
    rows = time_steps.shape[0]
    slots = time_steps.shape[1]
    token_count = tokens.shape[0]
    row_len = token_count // rows
    units = row_len // UNIT
    quarter = row_len // 4
    own_units = units // 4
    dp_count = width // own_depth
    dp_place = lax.axis_index("dp")
    slot_count = rows * slots
    mp_place = lax.axis_index("mp")
    core, chip = mp_place % 2, mp_place // 2
    place = (2 * core + chip).astype(jnp.int32)
    place_arg = place.reshape(1)

    chain = Chain(place_arg)

    ring = dp_count in (4, 8)
    known = jnp.zeros((dp_count,) + time_steps.shape, time_steps.dtype)
    known = lax.dynamic_update_slice_in_dim(known, time_steps[None], dp_place, 0)
    known, weight_cols, weight_rows = lax.optimization_barrier((known, weight_cols, weight_rows))
    cols_low = weight_cols.astype(low)
    own_rows = weight_rows.astype(low).transpose(2, 0, 1).reshape(own_depth, 5 * own_width)
    own_first = jnp.concatenate([cols_low[0], cols_low[1], cols_low[2], own_rows[:, :own_width]], 1)
    own_rest = jnp.concatenate([cols_low[5 + i] for i in range(4)] + [own_rows[:, own_width:]], 1)

    half_width = width // 2
    feature = dp_place * own_depth + jnp.arange(own_depth)
    is_cos = feature < half_width
    index = jnp.where(is_cos, feature, feature - half_width).astype(wide)
    frequency = jnp.exp(-math.log(10000.0) * index / half_width)

    def embed(steps):
        angles = steps.astype(wide)[:, None] * frequency[None, :]
        table = jnp.where(is_cos[None, :], jnp.cos(angles), jnp.sin(angles))
        return table.astype(low), jax.nn.silu(table).astype(low)

    near_maps = [jnp.concatenate([cols_low[i], cols_low[i + 1]], 1) for i in (9, 3)]
    far_maps = jnp.concatenate([cols_low[i] for i in (11, 12, 13, 14)], 1)

    def slot_products(pairs):
        out = jnp.concatenate([dot_as(left, maps, DOT_NN).astype(low) for left, maps in pairs], 1)
        return out.reshape(dp_count, rows * slots, -1)

    if ring:
        known = share_hop(known, 1, dp_count)
        known, own_first = lax.optimization_barrier((known, own_first))
        first_gather = RingGather(own_first, dp_count)

        def beside(value):
            value, first_gather.ahead, first_gather.behind = lax.optimization_barrier(
                (value, first_gather.ahead, first_gather.behind)
            )
            if first_gather.left > 0:
                first_gather.hop()
            return value

        known = beside(share_hop(known, 2, dp_count))
        if dp_count == 8:
            known = share_hop(known, 4, dp_count)
        time_low, ada_low = embed(known.reshape(-1))
        near = beside(slot_products([(ada_low, near_maps[0]), (time_low, near_maps[1])]))
        near = HalvingSum(near, dp_count)
        near.hop()
        if dp_count == 8:
            near.parts = beside(near.kept + near.got.astype(wide))
            near.step *= 2
            near.send()
        near.got = beside(near.got)
        near.hop()
        near = near.parts[0]
    else:
        w_first = lax.all_gather(own_first, "dp", axis=0, tiled=True)
        w_rest = lax.all_gather(own_rest, "dp", axis=0, tiled=True)
        time_low, ada_low = embed(lax.all_gather(time_steps, "dp", axis=0, tiled=True).reshape(-1))
        near = slot_products([(ada_low, near_maps[0]), (time_low, near_maps[1])])
        near = lax.psum_scatter(near, "dp", scatter_dimension=0, tiled=True)[0].astype(wide)

    seg_grid = seg_ids.reshape(rows, row_len)
    unit_seg = seg_grid.reshape(rows, units, UNIT)[:, :, 0]
    onehot = unit_seg[:, :, None] == jnp.arange(slots, dtype=jnp.int32)
    blocks = onehot[:, :, None, :] & (jnp.arange(rows)[:, None] == jnp.arange(rows))[:, None, :, None]
    blocks = blocks.reshape(rows * units, rows * slots)
    seg_place = unit_seg.reshape(rows, 4, own_units)
    seg_place = jnp.stack(
        [
            lax.dynamic_index_in_dim(seg_place, jnp.bitwise_xor(place, j), 1, keepdims=False)
            for j in range(4)
        ],
        0,
    )
    row_slots = seg_place + slots * jnp.arange(rows)[None, :, None]

    def field_slots(field):
        return row_slots + slot_count * field

    def slot_matrix(to, height):
        to = jnp.concatenate(to, 1).reshape(1, -1)
        return (jnp.arange(height)[:, None] == to).astype(low)

    spare = 4 * slot_count
    far_to = []
    for r in range(rows):
        far_to += [field_slots(f)[:, r] for f in range(3)] + [jnp.full((4, own_units), -1)]
    for r in range(rows):
        far_to += [field_slots(3)[:, r], jnp.full((4, 4), -1)]
    near_to = [field_slots(f)[:, r] for r in range(rows) for f in range(2)]
    moved = row_slots.transpose(1, 0, 2).reshape(-1, 1) == jnp.arange(slot_count)[None, :]
    quarters = [(r * 4 + jnp.bitwise_xor(place, j)) * quarter for j in range(4) for r in range(rows)]
    seg_rows = [seg_grid[r].reshape(1, row_len) for r in range(rows)]
    hot, far_matrix, near_matrix, moved, at, *segs = chain.tie(
        blocks.astype(low),
        slot_matrix(far_to, spare + 16),
        slot_matrix(near_to, 2 * slot_count),
        moved.astype(wide),
        jnp.stack(quarters).astype(jnp.int32),
        *seg_rows,
    )
    seg_rows = segs

    mp_arg = mp_place.astype(jnp.int32).reshape(1)

    def tables(spread, fields):
        spread.forward()
        pieces = [spread.own, spread.core, spread.chip, spread.both]
        return unit_tables(chain, mp_arg, hot, pieces, fields, own_units)

    far = slot_products([(lax.optimization_barrier((ada_low, near))[0], far_maps)])
    near_mod = (near[:, : 2 * own_width] + bias_cols[6:8].reshape(1, -1)).astype(low)
    near_spread = GroupGather(near_mod)
    if ring:
        far = HalvingSum(far, dp_count)
        near_spread.chip, own_rest = lax.optimization_barrier((near_spread.chip, own_rest))
        rest_gather = RingGather(own_rest, dp_count)
    near_tab = tables(near_spread, 2)
    if ring:
        w_first = first_gather.place(chain)
    time_add = jnp.concatenate(
        [
            near[:, 2 * own_width : 3 * own_width] + bias_cols[0],
            jnp.zeros((rows * slots, own_width), wide),
            near[:, 3 * own_width :] + bias_cols[1],
        ],
        1,
    )
    add_tab = jnp.dot(blocks.astype(wide), time_add, precision=highest)
    add_tab = add_tab.reshape(rows * 4, own_units, 3 * own_width)

    block, half_block = (quarter, width), (row_len // 2, width)
    qkv_width = 3 * own_width
    half = row_len // 2
    lows = lambda *shape: shape_of(shape, low)
    wides = lambda *shape: shape_of(shape, wide)

    def own_block(r):
        return pl.BlockSpec(block, lambda i, p: (r * 4 + p[0], 0))

    def moved_blocks(r):
        return [
            pl.BlockSpec(block, lambda i, p: (r * 4 + jnp.bitwise_xor(p[0], 2 * i), 0)),
            pl.BlockSpec(block, lambda i, p: (r * 4 + jnp.bitwise_xor(p[0], 2 * i + 1), 0)),
        ]

    def moved_tables(tab, r):
        shape = (1,) + tab.shape[1:]
        return [
            pl.BlockSpec(shape, lambda i, p: (r * 4 + jnp.bitwise_xor(p[0], 2 * i), 0, 0)),
            pl.BlockSpec(shape, lambda i, p: (r * 4 + jnp.bitwise_xor(p[0], 2 * i + 1), 0, 0)),
        ]

    def own_table(tab, r):
        return pl.BlockSpec((1,) + tab.shape[1:], lambda i, p: (r * 4 + p[0], 0, 0))

    here = fixed_spec(block)
    half_step = pl.BlockSpec(half_block, lambda i, p: (i, 0))
    half_fixed = fixed_spec(half_block)

    def open_row(r):
        return row_call(
            open_kernel,
            "open_row",
            chain,
            (tokens, tokens, near_tab, near_tab, add_tab, add_tab, w_first),
            moved_blocks(r) + moved_tables(near_tab, r) + moved_tables(add_tab, r) + [fixed_spec(w_first.shape)],
            (half_step, pl.BlockSpec((half, qkv_width), lambda i, p: (i, 0))),
            (lows(row_len, width), lows(row_len, qkv_width)),
            grid=2,
            flops=2 * row_len * width * qkv_width,
        )

    inputs_one, qkvs, mixed, parts = [], [], [], []

    def open_attend(r, between):
        a_one, qkv = open_row(r)
        inputs_one.append(a_one)
        qkvs.append(qkv)
        between()
        out, kept, sent = attend_forward(chain, qkv, seg_rows[r], w_first)
        mixed.append(out)
        parts.append(GroupSum(kept, sent))

    def both_hop():
        if ring:
            far.hop()
            rest_gather.hop()
            chain.land(*far.flying(), *rest_gather.flying())

    def far_spread():
        held = far.parts[0] if ring else lax.psum_scatter(far, "dp", scatter_dimension=0, tiled=True)[0]
        return GroupGather((held.astype(wide) + bias_cols[8:12].reshape(1, -1)).astype(low))

    def second_between():
        parts[0].cross()
        chain.land((parts[0], "last"))
        if ring:
            far.hop()
            chain.land(*rest_gather.flying())
        spreads.append(far_spread())
        chain.land(*spreads[0].flying())

    spreads = []
    if ring:
        chain.land(*far.flying(), *rest_gather.flying())
    open_attend(0, both_hop)
    if ring:
        far.hop()
        rest_gather.hop()
        chain.land(*far.flying())
    chain.land((parts[0], "got"))
    open_attend(1, second_between)
    if ring:
        rest_gather.hop()
    far_tab = tables(spreads[0], 4)

    attendeds, hiddens, inputs_two, down_grads = [], [], [], []

    def first_norm(r):
        attended, hidden, a_two = row_call(
            first_kernel,
            "first_norm",
            chain,
            (tokens, *parts[r].terms(), bias_rows, far_tab),
            [own_block(r), here, here, here, fixed_spec(bias_rows.shape), own_table(far_tab, r)],
            (here, here, here),
            (wides(*block), wides(*block), lows(*block)),
        )
        attendeds.append(attended)
        hiddens.append(hidden)
        inputs_two.append(GroupGather(a_two))

    def down_back(r):
        grads = row_call(
            down_back_kernel,
            "down_back",
            chain,
            (cotangent, cotangent, far_tab, far_tab, w_rest),
            moved_blocks(r) + moved_tables(far_tab, r) + [w_down_spec],
            (half_step, half_step),
            (lows(row_len, width), lows(row_len, width)),
            grid=2,
            flops=2 * row_len * width * width,
        )
        down_grads.append(grads)

    chain.land((parts[-1], "got"))
    first_norm(0)
    parts[-1].cross()
    if ring:
        w_rest = rest_gather.place(chain)
    w_down_spec = pl.BlockSpec((width, w_rest.shape[1] // 2), lambda i, p: (0, 1))
    w_up_spec = pl.BlockSpec((width, w_rest.shape[1] // 2), lambda i, p: (0, 0))
    chain.land(*inputs_two[0].flying())
    down_back(0)
    inputs_two[0].forward()
    chain.land((inputs_two[0], "both"), (parts[-1], "last"))
    down_back(1)
    first_norm(1)

    bias_up = bias_cols[2:6].reshape(1, -1)
    hidden_width = bias_up.shape[1]
    actives, inner_grads, up_parts, up_sums, down_parts = [], [], [], 0.0, []
    for r in range(rows):
        if r + 1 < rows:
            chain.land(*inputs_two[r + 1].flying())
        if r:
            chain.land((up_parts[r - 1], "last"), (down_parts[r - 1], "got"))
        active, inner_grad, kept, sent, sums = row_call(
            up_kernel,
            "up_and_back",
            chain,
            (*inputs_two[r].pieces(), down_grads[r][1], bias_up, w_rest),
            [here] * 4 + [half_step, fixed_spec(bias_up.shape), w_up_spec],
            (
                pl.BlockSpec((half, hidden_width), lambda i, p: (i, 0)),
                pl.BlockSpec((half, hidden_width), lambda i, p: (i, 0)),
                half_fixed,
                half_fixed,
                pl.BlockSpec((1, 8, hidden_width), lambda i, p: (i, 0, 0)),
            ),
            (
                lows(row_len, hidden_width),
                lows(row_len, hidden_width),
                lows(half, width),
                lows(half, width),
                wides(2, 8, hidden_width),
            ),
            grid=2,
            scratch=[pltpu.VMEM(half_block, low)],
            flops=4 * row_len * width * hidden_width,
        )
        actives.append(active)
        inner_grads.append(inner_grad)
        up_parts.append(GroupSum(kept, sent))
        up_sums = up_sums + jnp.sum(sums, axis=(0, 1))
        chain.land((up_parts[r], "got"))
        if r + 1 < rows:
            inputs_two[r + 1].forward()
            chain.land((inputs_two[r + 1], "both"))
        if r:
            down_parts[r - 1].cross()
        kept, sent = row_call(
            down_kernel,
            "down",
            chain,
            (active, w_rest),
            [pl.BlockSpec((half, hidden_width), lambda i, p: (i, 0)), w_down_spec],
            (half_fixed, half_fixed),
            (lows(half, width), lows(half, width)),
            grid=2,
            flops=2 * row_len * width * hidden_width,
        )
        down_parts.append(GroupSum(kept, sent))
        up_parts[r].cross()

    grad_hiddens, grad_gathers, second_sums = [], [], []

    def second_norm(r):
        grad_hidden, grad_attended, sums = row_call(
            second_kernel,
            "second_norm",
            chain,
            (cotangent, *up_parts[r].terms(), hiddens[r], attendeds[r], far_tab),
            [own_block(r)] + [here] * 5 + [own_table(far_tab, r)],
            (here, here, fixed_spec((16, width))),
            (wides(*block), lows(*block), wides(16, width)),
        )
        grad_hiddens.append(grad_hidden)
        grad_gathers.append(GroupGather(grad_attended))
        second_sums.append(sums)

    chain.land((down_parts[-1], "got"))
    second_norm(0)
    down_parts[-1].cross()
    chain.land((up_parts[-1], "last"), *grad_gathers[0].flying())
    rest_grad = weight_grad(
        chain,
        [
            [(inputs_two[r].pieces(), inner_grads[r]) for r in range(rows)],
            [([down_grads[r][0]], actives[r]) for r in range(rows)],
        ],
        "grad_rest",
    )
    rest_ring = RingSum(rest_grad, dp_count)
    grad_gathers[0].forward()
    chain.land((grad_gathers[0], "both"), (down_parts[0], "last"))
    second_norm(1)

    def out_rows():
        args, specs = [bias_rows], [fixed_spec(bias_rows.shape)]
        for r in range(rows):
            args += [cotangent, *down_parts[r].terms(), hiddens[r], far_tab, second_sums[r]]
            specs += [own_block(r)] + [here] * 4 + [own_table(far_tab, r), fixed_spec((16, width))]
        own, sums = row_call(
            out_kernel,
            "out_tokens",
            chain,
            args,
            specs,
            (fixed_spec((rows * quarter + 16, width)), fixed_spec((8 * rows, width))),
            (lows(rows * quarter + 16, width), wides(8 * rows, width)),
        )
        return GroupGather(own), sums

    def part(held, which, columns):
        return lax.dynamic_slice_in_dim(held, which * columns, columns, 1)

    class Exchange:
        def __init__(self, values):
            values = values.astype(low)
            self.mine = part(values, chip, 2 * own_width)
            self.other = lax.ppermute(part(values, 1 - chip, 2 * own_width), "mp", CHIP_SWAP)

        def cross(self):
            values = self.whole()
            self.mine = part(values, core, own_width)
            self.other = lax.ppermute(part(values, 1 - core, own_width), "mp", CORE_SWAP)

        def whole(self):
            return jnp.concatenate([self.mine, self.other], 0)

    qkv_grads, one_parts, time_sums = [], [], []

    def backward(r):
        qkv_grad, kept, sent, sums = attend_backward(
            chain, qkvs[r], grad_gathers[r].pieces(), seg_rows[r], w_first
        )
        qkv_grads.append(qkv_grad)
        one_parts.append(GroupSum(kept, sent))
        time_sums.append(sums)

    chain.land(*rest_ring.flying(), *grad_gathers[1].flying(), (down_parts[-1], "last"))
    backward(0)
    rest_ring.hop()
    grad_gathers[1].forward()
    chain.land((one_parts[0], "got"), (grad_gathers[1], "both"))
    out_gather, out_sums = out_rows()
    one_parts[0].cross()
    far_swap = Exchange(jnp.concatenate(second_sums + [out_sums], 0))
    last_hop = slice(0, 1 if dp_count == 8 else 2)
    chain.land(*rest_ring.flying(), (one_parts[0], "last"), (out_gather, "core"))
    backward(1)
    rest_ring.hop()
    chain.land(*rest_ring.flying(), (one_parts[1], "got"), (out_gather, "chip"), (far_swap, "other"))
    first_grad = weight_grad(
        chain,
        [
            [([inputs_one[r]], qkv_grads[r]) for r in range(rows)],
            [(grad_gathers[r].pieces(), mixed[r]) for r in range(rows)],
        ],
        "grad_first",
    )
    first_ring = RingSum(first_grad, dp_count)
    one_parts[1].cross()
    rest_ring.hop()
    out_gather.forward()
    far_swap.cross()

    cols_state = (weight_cols, first_cols, second_cols, ema_cols)
    rows_state = [x.transpose(0, 2, 1) for x in (weight_rows, first_rows, second_rows, ema_rows)]
    cuts = [(r * quarter, quarter) for r in range(rows)]
    chain.land((out_gather, "both"), (far_swap, "other"))
    third_args, third_specs = [], []
    for r in range(rows):
        third_args += [tokens, *one_parts[r].terms(), grad_hiddens[r], near_tab]
        third_specs += [own_block(r)] + [here] * 4 + [own_table(near_tab, r)]
    out_tokens = place_pieces(chain, at, out_gather.pieces(), cuts)
    far_slots = dot_as(far_matrix, far_swap.whole(), DOT_NN)
    own, across, core_own, core_across = [
        x[rows * quarter : rows * quarter + 2].astype(wide) for x in out_gather.pieces()
    ]
    bias_part = (own + across) + (core_own + core_across)
    far_slots = lax.dynamic_update_slice(
        far_slots,
        jnp.concatenate([up_sums.reshape(4, own_width), bias_part.reshape(8, own_width)], 0),
        (spare, 0),
    ).astype(low)
    far_gather = DoublingGather(far_slots, dp_count)
    chain.land(*first_ring.flying(), *rest_ring.flying()[last_hop], *far_gather.flying())
    input_own, third_sums = row_call(
        third_kernel,
        "third_norm",
        chain,
        third_args,
        third_specs,
        (fixed_spec((rows * quarter, width)), fixed_spec((8 * rows, width))),
        (lows(rows * quarter, width), wides(8 * rows, width)),
    )
    first_ring.hop()
    far_gather.hop()
    input_gather = GroupGather(input_own)
    near_swap = Exchange(third_sums)

    def columns_of(ref, at):
        return column(ref[...], at, own_width).astype(wide)

    def map_grad(left, right, field):
        right = right[:, field * slot_count : (field + 1) * slot_count, :]
        return dot_as(left[...], right.reshape(-1, own_width), DOT_TN)

    rest_sum = rest_ring.total()
    chain.land(*first_ring.flying(), *far_gather.flying(), (near_swap, "other"))
    cols_new = adam_slabs(
        chain,
        [(0, i) for i in (5, 6, 7, 8)],
        (rest_sum,),
        lambda n, refs: columns_of(refs[0], n),
        [cols_state],
        [None],
        "adam_up",
    )
    first_ring.hop()
    near_swap.cross()
    far_gather.hop()
    chain.land(*first_ring.flying(), (near_swap, "other"), *far_gather.flying())
    rows_new = adam_slabs(
        chain,
        [(0, i) for i in (1, 2, 3, 4)],
        (rest_sum,),
        lambda n, refs: columns_of(refs[0], 4 + n),
        [rows_state],
        [None],
        "adam_down",
    )
    first_ring.hop()
    far_all = far_gather.whole()
    unit_sums = jnp.concatenate(time_sums, 0)
    time_slots = lax.dot_general(moved, unit_sums, DOT_TN, precision=highest)
    near_slots = jnp.concatenate(
        [
            dot_as(near_matrix, near_swap.whole(), DOT_NN),
            time_slots[:, :own_width],
            time_slots[:, 2 * own_width :],
        ],
        0,
    ).astype(low)
    near_gather = DoublingGather(near_slots, dp_count)
    chain.land(*near_gather.flying(), *first_ring.flying()[last_hop], (input_gather, "chip"))
    cols_new = adam_slabs(
        chain,
        [(0, i) for i in (11, 12, 13, 14)],
        (ada_low, far_all),
        lambda n, refs: map_grad(refs[0], refs[1], n),
        [cols_state],
        [cols_new],
        "adam_far",
    )
    near_gather.hop()
    input_gather.forward()
    first_sum = first_ring.total()
    chain.land(*near_gather.flying(), (input_gather, "core"), (input_gather, "both"))
    new = adam_slabs(
        chain,
        [(0, i) for i in (0, 1, 2)] + [(1, 0)],
        (first_sum,),
        lambda n, refs: columns_of(refs[0], n),
        [cols_state, rows_state],
        [cols_new, rows_new],
        "adam_first",
    )
    cols_new, rows_new = new[:4], [x.transpose(0, 2, 1) for x in new[4:]]
    near_gather.hop()
    chain.land(*near_gather.flying())
    input_grads = widen_rows(chain, input_gather.pieces(), rows)
    near_all = near_gather.whole()
    cols_new = adam_slabs(
        chain,
        [(0, i) for i in (9, 10, 3, 4)],
        (ada_low, time_low, near_all),
        lambda n, refs: map_grad(refs[n // 2], refs[2], n),
        [cols_state],
        [cols_new],
        "adam_near",
    )
    far_sum = jnp.sum(far_all.astype(wide), axis=0)
    far_biases = jnp.sum(far_sum[:spare].reshape(4, slot_count, own_width), axis=1)
    bias_up_sum = far_sum[spare : spare + 4]
    bias_rows_sum = far_sum[spare + 4 : spare + 12].reshape(2, width)
    near_sum = jnp.sum(near_all.astype(wide).reshape(dp_count, 4, slot_count, own_width), axis=(0, 2))
    bias_cols_sum = jnp.concatenate([near_sum[2:4], bias_up_sum, near_sum[:2], far_biases], 0)
    bias_cols_new = adam_step(
        bias_cols, bias_cols_sum, first_bias_cols, second_bias_cols, ema_bias_cols, rate_vector
    )
    bias_rows_new = adam_step(
        bias_rows, bias_rows_sum, first_bias_rows, second_bias_rows, ema_bias_rows, rate_vector
    )
    return (out_tokens, input_grads, *cols_new, *rows_new, *bias_cols_new, *bias_rows_new)


def solution(mesh):
    cols, rows, bias = P(None, "dp", "mp"), P(None, "mp", "dp"), P(None, "mp")
    state = (cols, rows, bias, P())
    placed = (P("dp", None), P("dp"), P("dp", None), P("dp", None)) + state * 4
    given = (P("dp", None), P("dp", None)) + (cols,) * 4 + (rows,) * 4 + (bias,) * 4 + (P(),) * 4
    return jax.shard_map(
        per_device, mesh=mesh, in_specs=placed, out_specs=given, check_vma=False
    )
```
